32 devices in a mesh: row: 4 (over y, x), col: 8 (over z, core).
Axes of the slice: x: 2, y: 2, z: 4, core: 2. Of those that a mesh axis runs over, the one named last changes fastest.
Arguments:
- layer_input: bfloat16 [2, 4096, 1536], P(None, ('row', 'col')), may hold values from -6 to 6
- out_grad: bfloat16 [2, 4096, 1536], P(None, ('row', 'col')), may hold values from -6 to 6
- seq_lengths: int32 [2, 4], P(None, 'row'), may hold values from 256 to 1024, as said below
- routes: int32 [2, 4096, 6], P(None, 'row'), may hold values from 0 to 63, all different within a row; in each aligned block of 1024 rows (0 to 1023, 1024 to 2047, ..., all dimensions but the last counted through in order) at most 144 rows name the same one
- route_gates: float32 [2, 4096, 6], P(None, 'row'), may hold values from 0.2 to 0.6
- first_gain: float32 [1536], replicated, may hold values from 0.5 to 1.5
- gate_branch_proj: bfloat16 [1536, 3072], P('row', 'col'), may hold values from -0.15625 to 0.15625
- conv_in_proj: bfloat16 [1536, 3072], P('row', 'col'), may hold values from -0.15625 to 0.15625
- state_io_proj: bfloat16 [1536, 256], P('row', 'col'), may hold values from -0.15625 to 0.15625
- step_proj: bfloat16 [1536, 48], P('row', 'col'), may hold values from -0.15625 to 0.15625
- conv_kernel: float32 [4, 3072], P(None, 'col'), may hold values from -3 to 3
- conv_offset: float32 [3072], P('col'), may hold values from -1.5 to 1.5
- state_conv_kernel: float32 [4, 256], P(None, 'col'), may hold values from -3 to 3
- state_conv_offset: float32 [256], P('col'), may hold values from -1.5 to 1.5
- decay_log: float32 [48], P('col'), may hold values from 0 to 2.5
- step_offset: float32 [48], P('col'), may hold values from -9 to -3
- skip_scale: float32 [48], P('col'), may hold values from 0.5 to 1.5
- mixer_gain: float32 [3072], P('col'), may hold values from 0.5 to 1.5
- out_proj: bfloat16 [3072, 1536], P('col', 'row'), may hold values from -0.109375 to 0.109375
- second_gain: float32 [1536], replicated, may hold values from 0.5 to 1.5
- expert_gate: bfloat16 [64, 1536, 512], P('col', 'row'), may hold values from -0.15625 to 0.15625
- expert_up: bfloat16 [64, 1536, 512], P('col', 'row'), may hold values from -0.15625 to 0.15625
- expert_down: bfloat16 [64, 512, 1536], P('col', None, 'row'), may hold values from -0.25 to 0.25
- shared_gate: bfloat16 [1536, 1024], P('row', 'col'), may hold values from -0.15625 to 0.15625
- shared_up: bfloat16 [1536, 1024], P('row', 'col'), may hold values from -0.15625 to 0.15625
- shared_down: bfloat16 [1024, 1536], P('col', 'row'), may hold values from -0.1875 to 0.1875
Outputs:
- layer_output: bfloat16 [2, 4096, 1536], P(None, ('row', 'col'))
- input_grad: float32 [2, 4096, 1536], P(None, ('row', 'col'))
- first_gain_grad: float32 [1536], replicated
- gate_branch_proj_grad: float32 [1536, 3072], P('row', 'col')
- conv_in_proj_grad: float32 [1536, 3072], P('row', 'col')
- state_io_proj_grad: float32 [1536, 256], P('row', 'col')
- step_proj_grad: float32 [1536, 48], P('row', 'col')
- conv_kernel_grad: float32 [4, 3072], P(None, 'col')
- conv_offset_grad: float32 [3072], P('col')
- state_conv_kernel_grad: float32 [4, 256], P(None, 'col')
- state_conv_offset_grad: float32 [256], P('col')
- decay_log_grad: float32 [48], P('col')
- step_offset_grad: float32 [48], P('col')
- skip_scale_grad: float32 [48], P('col')
- mixer_gain_grad: float32 [3072], P('col')
- out_proj_grad: float32 [3072, 1536], P('col', 'row')
- second_gain_grad: float32 [1536], replicated
- expert_gate_grad: float32 [64, 1536, 512], P('col', 'row')
- expert_up_grad: float32 [64, 1536, 512], P('col', 'row')
- expert_down_grad: float32 [64, 512, 1536], P('col', None, 'row')
- shared_gate_grad: float32 [1536, 1024], P('row', 'col')
- shared_up_grad: float32 [1536, 1024], P('row', 'col')
- shared_down_grad: float32 [1024, 1536], P('col', 'row')
The draws below stay inside these ranges and needn't reach their ends.
Inputs may be any that keep to these rules, and one draw needn't show every extreme that they name: `seq_lengths`: in each micro-batch one sequence has length 1024. `routes`: each token names 6 different experts. Within the 1024 rows of one sequence slot no expert is named more than 144 times, a bound that some block reaches.
All inputs are finite; a program needn't handle non-finite values.
Results may differ from the reference program's by a relative error of at most 0.015.
Values may be sent and summed in bfloat16 or wider, within the bound.
A program may use at most 384 MiB of HBM per device.

```python
import math
import jax
import jax.numpy as jnp
import numpy as np
from jax import lax

D = 1536
NH = 48
P_SIZE = 64
NS = 128
CONV = 4
E = 64
TOPK = 6
H = 512
SH = 1024
SLOT = 1024
BLOCK = 256
MB = 2
DI = 3072
CAP = 144
SEQS = 4
TOKENS = 4096


def draw_seq_lengths(key, part):
    key = jax.random.fold_in(key, 7)
    first_key, second_key = jax.random.split(key)
    lengths = jax.random.randint(first_key, (MB, SEQS), SLOT // 4, SLOT + 1, dtype=jnp.int32)
    longest = jax.random.randint(second_key, (MB, 1), 0, SEQS, dtype=jnp.int32)
    places = jnp.arange(SEQS, dtype=jnp.int32)[None, :]
    return jnp.where(places == longest, SLOT, lengths).astype(jnp.int32)


def block_scale(key, shape, cuts, low, high):
    gain, own = 1.0, jax.random.fold_in(key, 6)
    for axis_at, shards_of in cuts:
        draws = jnp.exp(jax.random.uniform(jax.random.fold_in(own, axis_at), (shards_of,), jnp.float32, low / len(cuts), high / len(cuts)))
        gain = gain * jnp.repeat(draws, shape[axis_at] // shards_of).reshape([-1 if axis == axis_at else 1 for axis in range(len(shape))])
    return gain


def assign_block(key, own, number, rows, number_of, top, reach, slope):
    order = jax.random.permutation(key, number_of)
    heavy_load, common = shares(number_of, rows * top, reach, slope, True), shares(number_of, rows * top, reach, slope, False)
    places = jnp.arange(number_of)

    def named(sizes, offset_by):
        used = int((sizes > 0).sum())
        fixed = max(1, used // 4)
        moved = fixed + (places - fixed + offset_by * (used - fixed)) % max(1, number_of - fixed)
        return jnp.zeros((number_of,), jnp.int32).at[order[jnp.where(places < fixed, places, moved)]].set(jnp.asarray(sizes, jnp.int32))

    sizes = jnp.where(number % 4 == 0, named(heavy_load, number // 4), named(common, number - number // 4 - 1))
    mixed = jax.random.permutation(jax.random.fold_in(own, 3), number_of)
    giver, receiver = mixed[0:number_of // 2 * 2:2], mixed[1:number_of // 2 * 2:2]
    room = jnp.minimum(sizes[giver] - 1, reach - sizes[receiver]) // 2
    room = jnp.where((giver == order[0]) | (receiver == order[0]) | (sizes[receiver] == 0), 0, jnp.maximum(room, 0))
    moved = jax.random.randint(jax.random.fold_in(own, 4), (number_of // 2,), 0, 1 << 20) % (room + 1)
    sizes = sizes.at[giver].add(-moved).at[receiver].add(moved)
    members = jnp.searchsorted(jnp.cumsum(sizes), jnp.arange(rows * top), side="right").astype(jnp.int32)
    listing = members.reshape(top, rows).T
    listing = listing[jax.random.permutation(jax.random.fold_in(own, 1), rows)]
    offset_by = jax.random.randint(jax.random.fold_in(own, 2), (rows, 1), 0, top)
    return jnp.take_along_axis(listing, (jnp.arange(top)[None, :] + offset_by) % top, axis=1)


def shares(amount, total, bound, skew, full):
    weights = [(1 << 20) // math.isqrt(grade ** skew) + 1 for grade in range(1, amount + 1)]
    largest = bound if full else min(bound, max(-(-total // amount), total * weights[0] // sum(weights)))
    least = 1 if total - largest >= amount - 1 else 0
    holding, spare = [largest] + [least] * (amount - 1), total - largest - least * (amount - 1)
    while spare > 0:
        free = [i for i in range(1, amount) if holding[i] < largest] or [i for i in range(1, amount) if holding[i] < bound]
        mass, budget = sum([weights[i] for i in free]), spare
        for i in free:
            addition = min(bound - holding[i], max(1, budget * weights[i] // mass), spare)
            holding[i] = holding[i] + addition
            spare = spare - addition
    return np.array(holding)


def gaussian(rng, dims, deviation, most, pieces=(), held_as=jnp.bfloat16):
    loudness = block_scale(rng, dims, pieces, -0.22, 0.18) if pieces else 1.0
    drawn = jax.random.normal(rng, dims, jnp.float32) * deviation * loudness
    return jnp.minimum(jnp.maximum(drawn, -most), most).astype(held_as)


def setup_inputs(seed: int = 0) -> dict:
    key_list = jax.random.split(jax.random.key(seed), 27)
    layer_input = gaussian(key_list[0], (MB, TOKENS, D), 1.0, 6.0, ((1, 32),))
    out_grad = gaussian(key_list[1], (MB, TOKENS, D), 1.0, 6.0, ((1, 32),))
    seq_lengths = draw_seq_lengths(jax.random.fold_in(key_list[26], 71), 0)
    routes_keys = jax.random.split(jax.random.fold_in(key_list[3], 1), MB * TOKENS // SLOT)
    routes_turns = jax.random.permutation(jax.random.fold_in(key_list[3], 3), MB * TOKENS // SLOT)
    routes = jax.vmap(lambda own, number: assign_block(jax.random.fold_in(key_list[3], 2), own, number, SLOT, E, TOPK, CAP, 1))(routes_keys, routes_turns).reshape((MB, TOKENS, TOPK))
    route_gates = jnp.clip(0.2 + 0.400000021 * jax.random.uniform(key_list[4], (MB, TOKENS, TOPK), jnp.float32) ** block_scale(key_list[4], (MB, TOKENS, TOPK), ((1, 4),), -0.2, 0.2), 0.2, 0.6)
    first_gain = jnp.clip(1.0 + 0.1 * jax.random.normal(key_list[5], (D,), jnp.float32), 0.5, 1.5)
    gate_branch_proj = gaussian(key_list[6], (D, DI), D ** -0.5, 0.15625, ((0, 4), (1, 8)))
    conv_in_proj = gaussian(key_list[7], (D, DI), D ** -0.5, 0.15625, ((0, 4), (1, 8)))
    state_io_proj = gaussian(key_list[8], (D, 2 * NS), D ** -0.5, 0.15625, ((0, 4), (1, 8)))
    step_proj = gaussian(key_list[9], (D, NH), D ** -0.5, 0.15625, ((0, 4), (1, 8)))
    conv_kernel = gaussian(key_list[10], (CONV, DI), CONV ** -0.5, 3.0, ((1, 8),), jnp.float32)
    conv_offset = gaussian(key_list[11], (DI,), 0.3, 1.5, ((0, 8),), jnp.float32)
    state_conv_kernel = gaussian(key_list[12], (CONV, 2 * NS), CONV ** -0.5, 3.0, ((1, 8),), jnp.float32)
    state_conv_offset = gaussian(key_list[13], (2 * NS,), 0.3, 1.5, ((0, 8),), jnp.float32)
    decay_log = jnp.clip(2.5 * jax.random.uniform(key_list[14], (NH,), jnp.float32) ** block_scale(key_list[14], (NH,), ((0, 8),), -0.2, 0.2), 0.0, 2.5)
    step_offset = jnp.clip(-9.0 + 6.0 * jax.random.uniform(key_list[15], (NH,), jnp.float32) ** block_scale(key_list[15], (NH,), ((0, 8),), -0.2, 0.2), -9.0, -3.0)
    skip_scale = jnp.clip(0.5 + 1.0 * jax.random.uniform(key_list[16], (NH,), jnp.float32) ** block_scale(key_list[16], (NH,), ((0, 8),), -0.2, 0.2), 0.5, 1.5)
    mixer_gain = jnp.clip(1.0 + 0.1 * jax.random.normal(key_list[17], (DI,), jnp.float32), 0.5, 1.5)
    out_proj = gaussian(key_list[18], (DI, D), DI ** -0.5, 0.109375, ((0, 8), (1, 4)))
    second_gain = jnp.clip(1.0 + 0.1 * jax.random.normal(key_list[19], (D,), jnp.float32), 0.5, 1.5)
    expert_gate = gaussian(key_list[20], (E, D, H), D ** -0.5, 0.15625, ((0, 8), (1, 4)))
    expert_up = gaussian(key_list[21], (E, D, H), D ** -0.5, 0.15625, ((0, 8), (1, 4)))
    expert_down = gaussian(key_list[22], (E, H, D), H ** -0.5, 0.25, ((0, 8), (2, 4)))
    shared_gate = gaussian(key_list[23], (D, SH), D ** -0.5, 0.15625, ((0, 4), (1, 8)))
    shared_up = gaussian(key_list[24], (D, SH), D ** -0.5, 0.15625, ((0, 4), (1, 8)))
    shared_down = gaussian(key_list[25], (SH, D), SH ** -0.5, 0.1875, ((0, 8), (1, 4)))
    return {"layer_input": layer_input, "out_grad": out_grad, "seq_lengths": seq_lengths, "routes": routes, "route_gates": route_gates, "first_gain": first_gain, "gate_branch_proj": gate_branch_proj, "conv_in_proj": conv_in_proj, "state_io_proj": state_io_proj, "step_proj": step_proj, "conv_kernel": conv_kernel, "conv_offset": conv_offset, "state_conv_kernel": state_conv_kernel, "state_conv_offset": state_conv_offset, "decay_log": decay_log, "step_offset": step_offset, "skip_scale": skip_scale, "mixer_gain": mixer_gain, "out_proj": out_proj, "second_gain": second_gain, "expert_gate": expert_gate, "expert_up": expert_up, "expert_down": expert_down, "shared_gate": shared_gate, "shared_up": shared_up, "shared_down": shared_down}


EPS = 1e-05
PRECISE = lax.Precision.HIGHEST

@jax.custom_vjp
def low(v):
    return lax.optimization_barrier(v.astype(jnp.bfloat16)).astype(jnp.float32)

@jax.custom_vjp
def low_back(v):
    return v

def low_keep(v):
    return (low(v), None)

def low_pass(kept, grad):
    return (grad,)

def back_keep(v):
    return (v, None)

def back_low(kept, grad):
    return (low(grad),)
low.defvjp(low_keep, low_pass)
low_back.defvjp(back_keep, back_low)

def matmul(left_op, right_op):
    return jnp.dot(left_op, right_op, precision=PRECISE, preferred_element_type=jnp.float32)

def add_up(summed, term):
    return summed + term

def row_norm(values, scale_gain):
    return values * lax.rsqrt(lax.optimization_barrier(jnp.mean(values * values, axis=-1, keepdims=True)) + EPS) * scale_gain

def causal_conv(values, kernel, offset):
    length = values.shape[0]
    padded = jnp.pad(values, ((CONV - 1, 0), (0, 0)))
    summed = jnp.zeros_like(values) + offset
    for shift_back in range(CONV):
        summed = summed + kernel[shift_back] * padded[shift_back:shift_back + length]
    return summed

def block_scan(x_heads, step_size, rates, write_rows, read_rows):
    length, head_count, head_width = x_heads.shape
    blocks = length // BLOCK
    states_n = write_rows.shape[1]
    log_decay = -(step_size * rates)
    cumulative = jnp.cumsum(log_decay.reshape(blocks, BLOCK, head_count), axis=1)
    cum_heads = jnp.transpose(cumulative, (0, 2, 1))
    weighted = (x_heads * step_size[:, :, None]).reshape(blocks, BLOCK, head_count, head_width)
    write_block = write_rows.reshape(blocks, BLOCK, states_n)
    read_block = read_rows.reshape(blocks, BLOCK, states_n)
    places = jnp.arange(BLOCK)
    causal = places[:, None] >= places[None, :]
    spread = cum_heads[:, :, :, None] - cum_heads[:, :, None, :]
    decays = jnp.exp(jnp.where(causal[None, None], spread, -jnp.inf))
    scores = jnp.einsum('cin,cjn->cij', read_block, write_block, precision=PRECISE)
    mixing = scores[:, None] * decays
    within = jnp.einsum('chij,cjhp->cihp', mixing, weighted, precision=PRECISE)
    to_end = jnp.exp(cum_heads[:, :, -1:] - cum_heads)
    block_states = jnp.einsum('cjn,chj,cjhp->chpn', write_block, to_end, weighted, precision=PRECISE)
    through = jnp.exp(cum_heads[:, :, -1])

    def advance(carried, element):
        fresh_state, factor = element
        return (carried * factor[:, None, None] + fresh_state, carried)
    initial = jnp.zeros((head_count, head_width, states_n), jnp.float32)
    unused, starts = lax.scan(advance, initial, (block_states, through))
    carried_out = jnp.einsum('cin,chpn,chi->cihp', read_block, starts, jnp.exp(cum_heads), precision=PRECISE)
    return (within + carried_out).reshape(length, head_count, head_width)

def expert_slots(route_rows, gate_rows, first_expert, expert_count):
    token_count, pick_count = route_rows.shape
    flat_routes = (route_rows.reshape(-1) - first_expert).astype(jnp.int32)
    owner = (flat_routes[:, None] == jnp.arange(expert_count, dtype=jnp.int32)[None, :]).astype(jnp.int32)
    ranks = lax.optimization_barrier(jnp.sum((jnp.cumsum(owner, axis=0) - 1) * owner, axis=1)).astype(jnp.int32)
    inside = lax.optimization_barrier(jnp.sum(owner, axis=1)) > 0
    dump_slot = expert_count * CAP
    target = jnp.where(inside, flat_routes * CAP + ranks, dump_slot).astype(jnp.int32)
    row_ids = (jnp.arange(token_count * pick_count, dtype=jnp.int32) // pick_count).astype(jnp.int32)
    slot_token = jnp.zeros((dump_slot + 1,), jnp.int32).at[target].set(row_ids)[:dump_slot]
    slot_gate = jnp.zeros((dump_slot + 1,), jnp.float32).at[target].set(gate_rows.reshape(-1))[:dump_slot]
    return (slot_token, slot_gate)

def layer(inputs, params, route_rows, gate_rows):
    first_gain, gate_branch_proj, conv_in_proj, state_io_proj, step_proj, conv_kernel, conv_offset, state_conv_kernel, state_conv_offset, decay_log, step_offset, skip_scale, mixer_gain, out_proj, second_gain, expert_gate, expert_up, expert_down, shared_gate, shared_up, shared_down = params
    length = inputs.shape[0]
    first_normed = low(row_norm(inputs, first_gain))
    branch_pre = low_back(matmul(first_normed, gate_branch_proj))
    conv_pre = low_back(matmul(first_normed, conv_in_proj))
    io_pre = low_back(matmul(first_normed, state_io_proj))
    step_pre = low_back(matmul(first_normed, step_proj))
    conv_out = jax.nn.silu(causal_conv(conv_pre, conv_kernel, conv_offset))
    state_io = low(jax.nn.silu(causal_conv(io_pre, state_conv_kernel, state_conv_offset)))
    step_size = jax.nn.softplus(step_pre + step_offset)
    x_heads = conv_out.reshape(length, NH, P_SIZE)
    scanned = block_scan(x_heads, step_size, jnp.exp(decay_log), state_io[:, :NS], state_io[:, NS:])
    scanned = scanned + skip_scale[:, None] * x_heads
    gated_out = scanned.reshape(length, NH * P_SIZE) * jax.nn.silu(branch_pre)
    mixed_out = low(row_norm(gated_out, mixer_gain))
    residual = inputs + low_back(matmul(mixed_out, out_proj))
    second_normed = low(row_norm(residual, second_gain))
    slot_token, slot_gate = expert_slots(route_rows, gate_rows, 0, E)
    picked = second_normed[slot_token].reshape(E, CAP, -1)
    gate_pre = low_back(jnp.einsum('ecd,edh->ech', picked, expert_gate, precision=PRECISE))
    up_pre = low_back(jnp.einsum('ecd,edh->ech', picked, expert_up, precision=PRECISE))
    hidden = low(jax.nn.silu(gate_pre) * up_pre)
    expert_out = low_back(jnp.einsum('ech,ehd->ecd', hidden, expert_down, precision=PRECISE))
    weighted = (slot_gate.reshape(E, CAP, 1) * expert_out).reshape(E * CAP, -1)
    routed = jnp.zeros_like(residual).at[slot_token].add(weighted)
    shared_gate_pre = low_back(matmul(second_normed, shared_gate))
    shared_up_pre = low_back(matmul(second_normed, shared_up))
    shared_hidden = low(jax.nn.silu(shared_gate_pre) * shared_up_pre)
    shared_out = low_back(matmul(shared_hidden, shared_down))
    return residual + routed + shared_out

def reference(layer_input, out_grad, seq_lengths, routes, route_gates, first_gain, gate_branch_proj, conv_in_proj, state_io_proj, step_proj, conv_kernel, conv_offset, state_conv_kernel, state_conv_offset, decay_log, step_offset, skip_scale, mixer_gain, out_proj, second_gain, expert_gate, expert_up, expert_down, shared_gate, shared_up, shared_down):
    params = tuple((weight.astype(jnp.float32) for weight in (first_gain, gate_branch_proj, conv_in_proj, state_io_proj, step_proj, conv_kernel, conv_offset, state_conv_kernel, state_conv_offset, decay_log, step_offset, skip_scale, mixer_gain, out_proj, second_gain, expert_gate, expert_up, expert_down, shared_gate, shared_up, shared_down)))
    seq_count = seq_lengths.shape[0] * seq_lengths.shape[1]
    inputs_seq = layer_input.reshape(seq_count, SLOT, D)
    grads_seq = out_grad.reshape(seq_count, SLOT, D)
    routes_seq = routes.reshape(seq_count, SLOT, TOPK)
    gates_seq = route_gates.reshape(seq_count, SLOT, TOPK)
    lengths_seq = seq_lengths.reshape(seq_count)

    def one_sequence(totals, element):
        seq_in, seq_grad, seq_routes, seq_gates, seq_length = element
        valid_rows = (jnp.arange(SLOT) < seq_length).astype(jnp.float32)

        def forward(inputs, weights):
            return layer(inputs, weights, seq_routes, seq_gates)
        output, backward = jax.vjp(forward, seq_in.astype(jnp.float32), params)
        input_grad, param_grads = backward(seq_grad.astype(jnp.float32) * valid_rows[:, None])
        return (jax.tree.map(add_up, totals, param_grads), (output.astype(jnp.bfloat16), input_grad))
    initial_sums = jax.tree.map(jnp.zeros_like, params)
    totals, (outputs, input_grads) = lax.scan(one_sequence, initial_sums, (inputs_seq, grads_seq, routes_seq, gates_seq, lengths_seq))
    shape_out = layer_input.shape
    return (outputs.reshape(shape_out), input_grads.reshape(shape_out), totals[0], totals[1], totals[2], totals[3], totals[4], totals[5], totals[6], totals[7], totals[8], totals[9], totals[10], totals[11], totals[12], totals[13], totals[14], totals[15], totals[16], totals[17], totals[18], totals[19], totals[20])
```

```python
import functools

import jax
import jax.numpy as jnp
from jax import lax
from jax.experimental import pallas as pl
from jax.experimental.pallas import tpu as pltpu
from jax.sharding import PartitionSpec as P

NS = 128
BLOCK = 256
CAP = 144
EPS = 1e-05
HEAD_ROWS = 16
LANES = 128
F32 = jnp.float32
BF16 = jnp.bfloat16
VMEM = pl.BlockSpec(memory_space=pltpu.VMEM)
VMEM_LIMIT = 56 * 1024 * 1024


def contract(left_op, right_op, left_dim, right_dim, precision=None):
    return lax.dot_general(
        left_op,
        right_op,
        (((left_dim,), (right_dim,)), ((), ())),
        preferred_element_type=F32,
        precision=precision,
    )


def dot_plain(left_op, right_op):
    return contract(left_op, right_op, 1, 0)


def dot_first(left_op, right_op):
    return contract(left_op, right_op, 0, 0)


def dot_last(left_op, right_op):
    return contract(left_op, right_op, 1, 1)


def silu_slope(values):
    logistic = jax.nn.sigmoid(values)
    return logistic * (1.0 + values * (1.0 - logistic))


def softplus(values):
    return jnp.maximum(values, 0.0) + jnp.log1p(jnp.exp(-jnp.abs(values)))


def shifts_back(current, before):
    joined = jnp.concatenate([before, current], axis=1)
    return [pltpu.roll(joined, step, 1)[:, LANES:] for step in (1, 2, 3)]


def load_block(ref, rows, block):
    cols = pl.ds(pl.multiple_of(block * BLOCK, BLOCK), BLOCK)
    current = ref[rows, cols]
    ahead = pl.multiple_of(jnp.maximum(block * BLOCK - LANES, 0), LANES)
    before = jnp.where(block > 0, ref[rows, pl.ds(ahead, LANES)], 0.0)
    return current, shifts_back(current, before)


def convolved(current, back, taps):
    return (
        taps[:, 4:5]
        + taps[:, 3:4] * current
        + taps[:, 2:3] * back[0]
        + taps[:, 1:2] * back[1]
        + taps[:, 0:1] * back[2]
    )


def conv_adjoint(adjoint, after, taps):
    joined = jnp.concatenate([adjoint, after], axis=1)
    width = joined.shape[1]
    total = taps[:, 3:4] * adjoint
    for step in (1, 2, 3):
        ahead = pltpu.roll(joined, width - step, 1)[:, :BLOCK]
        total = total + taps[:, 3 - step : 4 - step] * ahead
    return total


def lane_tile(columns):
    rows = columns[0].shape[0]
    lane = lax.broadcasted_iota(jnp.int32, (rows, LANES), 1)
    tile = jnp.zeros((rows, LANES), F32)
    for place, column in enumerate(columns):
        tile = jnp.where(lane == place, column, tile)
    return tile


def row_sum(values):
    return jnp.sum(values, axis=1, keepdims=True)


def decay_block(cum_row, cum_cols, head):
    lane = lax.broadcasted_iota(jnp.int32, cum_cols.shape, 1)
    cum_col = row_sum(jnp.where(lane == head, cum_cols, 0.0))
    place_j = lax.broadcasted_iota(jnp.int32, (BLOCK, BLOCK), 0)
    place_i = lax.broadcasted_iota(jnp.int32, (BLOCK, BLOCK), 1)
    return jnp.exp(jnp.where(place_j <= place_i, cum_row - cum_col, -1e30))


def step_rows(step_pre, head_params, step_s, cum_s, cum_t_s, blocks):
    step = softplus(step_pre + head_params[:, 0:1])
    step_s[...] = step
    log_decay = -(step * head_params[:, 1:2])
    place_j = lax.broadcasted_iota(jnp.int32, (BLOCK, BLOCK), 0)
    place_i = lax.broadcasted_iota(jnp.int32, (BLOCK, BLOCK), 1)
    upper = jnp.where(place_j <= place_i, 1.0, 0.0)
    for block in range(blocks):
        cols = slice(block * BLOCK, (block + 1) * BLOCK)
        cum = contract(log_decay[:, cols], upper, 1, 0, lax.Precision.HIGHEST)
        cum_s[:, cols] = cum
        cum_t_s[cols, :] = jnp.transpose(cum)


def score_blocks(io, scores_s, blocks):
    for block in range(blocks):
        cols = slice(block * BLOCK, (block + 1) * BLOCK)
        scores_s[block] = dot_first(io[:NS, cols], io[NS:, cols])


def block_cols(block):
    return pl.ds(pl.multiple_of(block * BLOCK, BLOCK), BLOCK)


def mixer_forward_kernel(
    heads,
    xn,
    wb,
    wc,
    wio,
    ws,
    wo,
    chan,
    io_taps,
    head_params,
    y,
    squares,
    branch,
    conv,
    io_pre,
    io,
    step_pre,
    starts,
    step_s,
    cum_s,
    cum_t_s,
    scores_s,
    z_s,
):
    length = xn.shape[0]
    blocks = length // BLOCK
    size = wb.shape[0] // heads
    step_pre[...] = dot_last(ws[...], xn[...])
    step_rows(step_pre[...], head_params[...], step_s, cum_s, cum_t_s, blocks)

    def project(block, carry):
        cols = block_cols(block)
        rows = xn[cols, :]
        io_pre[:, cols] = dot_last(wio[...], rows)
        branch[:, cols] = dot_last(wb[...], rows)
        conv[:, cols] = dot_last(wc[...], rows)
        return carry

    lax.fori_loop(0, blocks, project, 0)

    def io_step(at, carry):
        rows = pl.ds(pl.multiple_of((at // blocks) * 64, 64), 64)
        block = at % blocks
        current, back = load_block(io_pre, rows, block)
        io[rows, block_cols(block)] = jax.nn.silu(
            convolved(current, back, io_taps[rows, :])
        ).astype(BF16)
        return carry

    lax.fori_loop(0, blocks * (2 * NS // 64), io_step, 0)
    score_blocks(io, scores_s, blocks)
    squares[...] = jnp.zeros_like(squares)

    def head_step(head, carry):
        rows = pl.ds(pl.multiple_of(head * size, size), size)
        params = chan[rows, :]

        def block_step(block, state):
            cols = block_cols(block)
            current, back = load_block(conv, rows, block)
            x = jax.nn.silu(convolved(current, back, params))
            step_row = step_s[pl.ds(head, 1), cols]
            cum_row = cum_s[pl.ds(head, 1), cols]
            last = cum_row[:, BLOCK - 1 : BLOCK]
            mixing = (scores_s[block] * decay_block(cum_row, cum_t_s[cols, :], head)).astype(BF16)
            weighted = x * step_row
            starts[pl.ds(pl.multiple_of((head * blocks + block) * size, size), size), :] = state
            scanned = dot_plain(weighted.astype(BF16), mixing)
            scanned = scanned + dot_plain(state.astype(BF16), io[NS:, cols]) * jnp.exp(cum_row)
            scanned = scanned + params[:, 6:7] * x
            gated = scanned * jax.nn.silu(branch[rows, cols])
            squares[:, cols] += jnp.sum((gated * gated).reshape(size // 8, 8, BLOCK), axis=0)
            z_s[rows, cols] = (gated * params[:, 5:6]).astype(BF16)
            to_end = (weighted * jnp.exp(last - cum_row)).astype(BF16)
            return state * jnp.exp(last) + dot_last(to_end, io[:NS, cols])

        lax.fori_loop(0, blocks, block_step, jnp.zeros((size, NS), F32))
        return carry

    lax.fori_loop(0, heads, head_step, 0)

    def out_step(block, carry):
        cols = block_cols(block)
        y[cols, :] = dot_first(z_s[:, cols], wo[...]).astype(BF16)
        return carry

    lax.fori_loop(0, blocks, out_step, 0)


def mixer_forward(xn, wb, wc, wio, ws, wo, chan, io_taps, head_params, heads):
    length, width = xn.shape
    share = wb.shape[0]
    blocks = length // BLOCK
    size = share // heads
    shape = jax.ShapeDtypeStruct
    flops = 2 * length * width * (3 * share + 2 * NS + HEAD_ROWS) + 10**8
    return pl.pallas_call(
        functools.partial(mixer_forward_kernel, heads),
        out_shape=(
            shape((length, width), BF16),
            shape((8, length), F32),
            shape((share, length), F32),
            shape((share, length), F32),
            shape((2 * NS, length), F32),
            shape((2 * NS, length), BF16),
            shape((HEAD_ROWS, length), F32),
            shape((heads * blocks * size, NS), F32),
        ),
        in_specs=[VMEM] * 9,
        out_specs=[VMEM] * 8,
        scratch_shapes=[
            pltpu.VMEM((HEAD_ROWS, length), F32),
            pltpu.VMEM((HEAD_ROWS, length), F32),
            pltpu.VMEM((length, HEAD_ROWS), F32),
            pltpu.VMEM((blocks, BLOCK, BLOCK), F32),
            pltpu.VMEM((share, length), BF16),
        ],
        compiler_params=pltpu.CompilerParams(vmem_limit_bytes=VMEM_LIMIT),
        cost_estimate=pl.CostEstimate(
            flops=4 * flops, bytes_accessed=4 * 2 * length * width, transcendentals=10**7
        ),
    )(xn, wb, wc, wio, ws, wo, chan, io_taps, head_params)


def mixer_backward_kernel(
    heads,
    d_res,
    scale_rows,
    xn,
    wb,
    wc,
    wio,
    ws,
    wo,
    chan,
    io_taps,
    head_params,
    branch,
    conv,
    io_pre,
    io,
    step_pre,
    starts,
    first_part,
    gain_part,
    mixed,
    d_branch,
    d_conv,
    d_io,
    d_step,
    chan_grad,
    io_grad,
    head_grad,
    step_s,
    cum_s,
    cum_t_s,
    scores_s,
    d_scores_s,
    d_mixed_s,
    d_io_s,
    d_cum_s,
    d_size_s,
    adjoint_s,
):
    length = xn.shape[0]
    blocks = length // BLOCK
    size = wb.shape[0] // heads
    step_rows(step_pre[...], head_params[...], step_s, cum_s, cum_t_s, blocks)
    score_blocks(io, scores_s, blocks)
    d_scores_s[...] = jnp.zeros_like(d_scores_s)
    d_io_s[...] = jnp.zeros_like(d_io_s)
    d_cum_s[...] = jnp.zeros_like(d_cum_s)
    d_size_s[...] = jnp.zeros_like(d_size_s)
    chan_grad[...] = jnp.zeros_like(chan_grad)
    io_grad[...] = jnp.zeros_like(io_grad)
    adjoint_s[:, length:] = jnp.zeros((adjoint_s.shape[0], LANES), F32)

    def project(block, carry):
        cols = block_cols(block)
        d_mixed_s[:, cols] = dot_last(wo[...], d_res[cols, :])
        return carry

    lax.fori_loop(0, blocks, project, 0)

    def head_step(head, carry):
        rows = pl.ds(pl.multiple_of(head * size, size), size)
        params = chan[rows, :]

        def block_step(reverse, d_state):
            block = blocks - 1 - reverse
            cols = block_cols(block)
            state = starts[pl.ds(pl.multiple_of((head * blocks + block) * size, size), size), :]
            state_low = state.astype(BF16)
            d_state_low = d_state.astype(BF16)
            write_rows = io[:NS, cols]
            read_rows = io[NS:, cols]
            step_row = step_s[pl.ds(head, 1), cols]
            cum_row = cum_s[pl.ds(head, 1), cols]
            last = cum_row[:, BLOCK - 1 : BLOCK]
            decays = decay_block(cum_row, cum_t_s[cols, :], head)
            mixing = (scores_s[block] * decays).astype(BF16)
            current, back = load_block(conv, rows, block)
            conv_act = convolved(current, back, params)
            logistic = jax.nn.sigmoid(conv_act)
            x = conv_act * logistic
            slope = logistic * (1.0 + conv_act * (1.0 - logistic))
            weighted = x * step_row
            weighted_low = weighted.astype(BF16)
            grown = jnp.exp(cum_row)
            within = dot_plain(weighted_low, mixing)
            carried = dot_plain(state_low, read_rows) * grown
            scanned = within + carried + params[:, 6:7] * x

            inverse_rms = scale_rows[0:1, cols]
            gate_in = branch[rows, cols]
            gate_logistic = jax.nn.sigmoid(gate_in)
            gate_out = gate_in * gate_logistic
            gated = scanned * gate_out
            d_mixed = d_mixed_s[rows, cols]
            gain = params[:, 5:6]
            mixed[rows, cols] = (gated * inverse_rms * gain).astype(BF16)
            d_gated = inverse_rms * (d_mixed * gain) - gated * scale_rows[1:2, cols]
            d_gain = row_sum(d_mixed * gated * inverse_rms)
            d_scanned = d_gated * gate_out
            d_branch[rows, cols] = (
                d_gated * scanned * (gate_logistic * (1.0 + gate_in * (1.0 - gate_logistic)))
            ).astype(BF16)
            d_low = d_scanned.astype(BF16)
            d_skip = row_sum(d_scanned * x)

            d_within = dot_last(d_low, mixing)
            shrunk = jnp.exp(last - cum_row)
            d_fed = dot_plain(d_state_low, write_rows) * shrunk
            d_weighted = d_within + d_fed
            d_scores_s[block] += dot_first(weighted_low, d_low) * decays
            d_grown = (d_scanned * grown).astype(BF16)
            fed = (weighted * shrunk).astype(BF16)
            d_io_s[NS:, cols] += dot_first(state_low, d_grown)
            d_io_s[:NS, cols] += dot_first(d_state_low, fed)
            d_before = d_state * jnp.exp(last) + dot_last(d_grown, read_rows)

            fed_terms = weighted * d_fed
            d_cum = jnp.sum(
                d_low.astype(F32) * within
                - weighted_low.astype(F32) * d_within
                + d_scanned * carried
                - fed_terms,
                axis=0,
                keepdims=True,
            )
            at_end = jnp.sum(row_sum(fed_terms), axis=0, keepdims=True) + jnp.exp(last) * jnp.sum(
                row_sum(d_state * state), axis=0, keepdims=True
            )
            lane = lax.broadcasted_iota(jnp.int32, (1, BLOCK), 1)
            d_cum_s[pl.ds(head, 1), cols] = d_cum + jnp.where(lane == BLOCK - 1, at_end, 0.0)
            d_size_s[pl.ds(head, 1), cols] = jnp.sum(d_weighted * x, axis=0, keepdims=True)

            d_act = (d_weighted * step_row + params[:, 6:7] * d_scanned) * slope
            adjoint_s[:, cols] = d_act
            after = adjoint_s[:, pl.ds(pl.multiple_of((block + 1) * BLOCK, BLOCK), LANES)]
            d_conv[rows, cols] = conv_adjoint(d_act, after, params).astype(BF16)
            chan_grad[rows, :] += lane_tile(
                [
                    row_sum(d_act * back[2]),
                    row_sum(d_act * back[1]),
                    row_sum(d_act * back[0]),
                    row_sum(d_act * current),
                    row_sum(d_act),
                    d_gain,
                    d_skip,
                ]
            )
            return d_before

        lax.fori_loop(0, blocks, block_step, jnp.zeros((size, NS), F32))
        return carry

    lax.fori_loop(0, heads, head_step, 0)

    def scores_step(block, carry):
        cols = block_cols(block)
        d_scores = d_scores_s[block].astype(BF16)
        d_io_s[NS:, cols] += dot_plain(io[:NS, cols], d_scores)
        d_io_s[:NS, cols] += dot_last(io[NS:, cols], d_scores)
        return carry

    lax.fori_loop(0, blocks, scores_step, 0)

    def io_step(at, carry):
        rows = pl.ds(pl.multiple_of((at // blocks) * 64, 64), 64)
        block = blocks - 1 - at % blocks
        cols = block_cols(block)
        taps = io_taps[rows, :]
        current, back = load_block(io_pre, rows, block)
        d_act = d_io_s[rows, cols] * silu_slope(convolved(current, back, taps))
        adjoint_s[:64, cols] = d_act
        after = adjoint_s[:64, pl.ds(pl.multiple_of((block + 1) * BLOCK, BLOCK), LANES)]
        d_io[rows, cols] = conv_adjoint(d_act, after, taps).astype(BF16)
        io_grad[rows, :] += lane_tile(
            [
                row_sum(d_act * back[2]),
                row_sum(d_act * back[1]),
                row_sum(d_act * back[0]),
                row_sum(d_act * current),
                row_sum(d_act),
            ]
        )
        return carry

    lax.fori_loop(0, blocks * (2 * NS // 64), io_step, 0)

    place_j = lax.broadcasted_iota(jnp.int32, (BLOCK, BLOCK), 0)
    place_i = lax.broadcasted_iota(jnp.int32, (BLOCK, BLOCK), 1)
    lower = jnp.where(place_j >= place_i, 1.0, 0.0)
    rate = head_params[:, 1:2]
    decay_grad = jnp.zeros((HEAD_ROWS, 1), F32)
    offset_grad = jnp.zeros((HEAD_ROWS, 1), F32)
    for block in range(blocks):
        cols = slice(block * BLOCK, (block + 1) * BLOCK)
        d_log = contract(d_cum_s[:, cols], lower, 1, 0, lax.Precision.HIGHEST)
        decay_grad = decay_grad - row_sum(step_s[:, cols] * rate * d_log)
        d_size = d_size_s[:, cols] - rate * d_log
        d_pre = d_size * jax.nn.sigmoid(step_pre[:, cols] + head_params[:, 0:1])
        offset_grad = offset_grad + row_sum(d_pre)
        d_step[:, cols] = d_pre.astype(BF16)
    head_grad[...] = lane_tile([decay_grad, offset_grad])
    gain_part[...] = jnp.zeros_like(gain_part)

    def first_step(block, carry):
        cols = block_cols(block)
        part = (
            dot_first(d_branch[:, cols], wb[...])
            + dot_first(d_conv[:, cols], wc[...])
            + dot_first(d_io[:, cols], wio[...])
            + dot_first(d_step[:, cols], ws[...])
        )
        first_part[cols, :] = part.astype(BF16)
        product = part * xn[cols, :].astype(F32)
        gain_part[...] += jnp.sum(product.reshape(BLOCK // 8, 8, -1), axis=0)
        return carry

    lax.fori_loop(0, blocks, first_step, 0)


def mixer_backward(d_res, scale_rows, xn, weights, saved, heads):
    length, width = xn.shape
    share = weights[0].shape[0]
    blocks = length // BLOCK
    size = share // heads
    shape = jax.ShapeDtypeStruct
    flops = 2 * length * width * (3 * share + 2 * NS + HEAD_ROWS) + 10**8
    return pl.pallas_call(
        functools.partial(mixer_backward_kernel, heads),
        out_shape=(
            shape((length, width), BF16),
            shape((8, width), F32),
            shape((share, length), BF16),
            shape((share, length), BF16),
            shape((share, length), BF16),
            shape((2 * NS, length), BF16),
            shape((HEAD_ROWS, length), BF16),
            shape((share, LANES), F32),
            shape((2 * NS, LANES), F32),
            shape((HEAD_ROWS, LANES), F32),
        ),
        in_specs=[VMEM] * 17,
        out_specs=[VMEM] * 10,
        scratch_shapes=[
            pltpu.VMEM((HEAD_ROWS, length), F32),
            pltpu.VMEM((HEAD_ROWS, length), F32),
            pltpu.VMEM((length, HEAD_ROWS), F32),
            pltpu.VMEM((blocks, BLOCK, BLOCK), F32),
            pltpu.VMEM((blocks, BLOCK, BLOCK), F32),
            pltpu.VMEM((share, length), F32),
            pltpu.VMEM((2 * NS, length), F32),
            pltpu.VMEM((HEAD_ROWS, length), F32),
            pltpu.VMEM((HEAD_ROWS, length), F32),
            pltpu.VMEM((size, length + LANES), F32),
        ],
        compiler_params=pltpu.CompilerParams(vmem_limit_bytes=VMEM_LIMIT),
        cost_estimate=pl.CostEstimate(
            flops=8 * flops, bytes_accessed=8 * 2 * length * width, transcendentals=10**7
        ),
    )(d_res, scale_rows, xn, *weights, *saved)


def row_norm(values, scale_gain):
    return values * lax.rsqrt(jnp.mean(values * values, axis=1, keepdims=True) + EPS) * scale_gain


def norm_adjoint(values, scale_gain, cotangent):
    inverse = lax.rsqrt(jnp.mean(values * values, axis=1, keepdims=True) + EPS)
    unit = values * inverse
    scaled = cotangent * scale_gain
    back = inverse * (scaled - unit * jnp.mean(scaled * unit, axis=1, keepdims=True))
    return back, jnp.sum(cotangent * unit, axis=0)


def local(
    layer_input,
    out_grad,
    seq_lengths,
    routes,
    route_gates,
    first_gain,
    gate_branch_proj,
    conv_in_proj,
    state_io_proj,
    step_proj,
    conv_kernel,
    conv_offset,
    state_conv_kernel,
    state_conv_offset,
    decay_log,
    step_offset,
    skip_scale,
    mixer_gain,
    out_proj,
    second_gain,
    expert_gate,
    expert_up,
    expert_down,
    shared_gate,
    shared_up,
    shared_down,
):
    rows_n = lax.axis_size("row")
    cols_n = lax.axis_size("col")
    row_index = lax.axis_index("row")
    col_index = lax.axis_index("col")
    micro_count, own_count, width = layer_input.shape
    length = own_count * cols_n
    local_experts, depth, hidden_width = expert_gate.shape
    share = conv_kernel.shape[1]
    heads = decay_log.shape[0]
    size = share // heads
    inner = share * cols_n
    io_width = state_conv_kernel.shape[1]
    shared_width = shared_gate.shape[1]
    per_device = max(1, local_experts // rows_n)
    split = max(1, rows_n // local_experts)
    part_width = hidden_width // split
    slots = per_device * CAP

    def swap(values, k):
        if k == 0:
            return values
        return lax.ppermute(values, "row", [(i, i ^ k) for i in range(rows_n)])

    def peer(k):
        return row_index ^ k

    def unit_of(member):
        return (member * per_device) // split, (member % split) * part_width

    def gather_width(pack):
        full = jnp.zeros((pack.shape[0], width), pack.dtype)
        for k in range(rows_n):
            full = lax.dynamic_update_slice(full, swap(pack, k), (0, peer(k) * depth))
        return full

    def add_shares(full):
        total = None
        for k in range(rows_n):
            part = lax.dynamic_slice(full, (0, peer(k) * depth), (full.shape[0], depth))
            part = swap(part, k).astype(F32)
            total = part if total is None else total + part
        return total

    micro = range(micro_count)
    own_rows = [layer_input[m].astype(F32) for m in micro]
    normed = [
        lax.all_gather(row_norm(own_rows[m], first_gain).astype(BF16), "col", axis=0, tiled=True)
        for m in micro
    ]

    io_gathered = lax.all_gather(
        jnp.concatenate(
            [state_io_proj.astype(F32), state_conv_kernel, state_conv_offset[None, :]], axis=0
        ),
        "col",
        axis=1,
        tiled=True,
    )
    step_rows_t = jnp.pad(step_proj.T, ((0, HEAD_ROWS - heads), (0, 0)))
    in_full = gather_width(
        jnp.concatenate(
            [gate_branch_proj.T, conv_in_proj.T, io_gathered[:depth].astype(BF16).T, step_rows_t],
            axis=0,
        )
    )
    out_full = gather_width(
        jnp.concatenate([out_proj, shared_gate.T, shared_up.T, shared_down], axis=0)
    )
    wb, wc = in_full[:share], in_full[share : 2 * share]
    wio = in_full[2 * share : 2 * share + 2 * NS]
    ws = in_full[2 * share + 2 * NS :]
    wo = out_full[:share]
    shared_in = out_full[share : share + 2 * shared_width]
    shared_out = out_full[share + 2 * shared_width :]
    chan = jnp.concatenate(
        [
            conv_kernel.T,
            conv_offset[:, None],
            mixer_gain[:, None],
            jnp.repeat(skip_scale, size)[:, None],
            jnp.zeros((share, 1), F32),
        ],
        axis=1,
    )
    io_taps = jnp.pad(io_gathered[depth:].T, ((0, 0), (0, 3)))
    head_params = jnp.pad(
        jnp.stack([step_offset, jnp.exp(decay_log)], axis=1), ((0, HEAD_ROWS - heads), (0, 6))
    )
    weights = (wb, wc, wio, ws, wo, chan, io_taps, head_params)

    gate_up = jnp.zeros((per_device, width, 2 * part_width), BF16)
    down = jnp.zeros((per_device, part_width, width), BF16)
    for k in range(rows_n):
        first, hidden_at = unit_of(peer(k))
        cut = (first, 0, hidden_at)
        sizes = (per_device, depth, part_width)
        up_part = jnp.concatenate(
            [
                lax.dynamic_slice(expert_gate, cut, sizes),
                lax.dynamic_slice(expert_up, cut, sizes),
            ],
            axis=2,
        )
        down_part = lax.dynamic_slice(
            expert_down, (first, hidden_at, 0), (per_device, part_width, depth)
        )
        at = peer(k) * depth
        gate_up = lax.dynamic_update_slice(gate_up, swap(up_part, k), (0, at, 0))
        down = lax.dynamic_update_slice(down, swap(down_part, k), (0, 0, at))

    place_j = lax.broadcasted_iota(jnp.int32, (length, length), 0)
    place_i = lax.broadcasted_iota(jnp.int32, (length, length), 1)
    upper = (place_j <= place_i).astype(BF16)
    expert_ids = col_index * local_experts + jnp.arange(local_experts, dtype=jnp.int32)

    def dispatch(m):
        hit = routes[m].T[None] == expert_ids[:, None, None]
        mask = jnp.any(hit, axis=1)
        gates = jnp.sum(jnp.where(hit, route_gates[m].T[None], 0.0), axis=1)
        rank = dot_plain(mask.astype(BF16), upper).astype(jnp.int32) - 1
        slot = jnp.where(mask, rank, -1)
        picks, slot_gates = [], []
        for k in range(rows_n):
            first, _ = unit_of(peer(k))
            slot_k = lax.dynamic_slice(slot, (first, 0), (per_device, length))
            gates_k = lax.dynamic_slice(gates, (first, 0), (per_device, length))
            chosen = slot_k[:, None, :] == jnp.arange(CAP, dtype=jnp.int32)[None, :, None]
            slot_gates.append(
                jnp.sum(jnp.where(chosen, gates_k[:, None, :], 0.0), axis=2).reshape(slots, 1)
            )
            picks.append(chosen.astype(BF16).reshape(slots, length))
        return picks, slot_gates

    def stack_rows(parts):
        return jnp.stack(
            [part.reshape(per_device, CAP, width) for part in parts], axis=1
        ).reshape(per_device, rows_n * CAP, width)

    def send_back(rows):
        rows = rows.astype(BF16).reshape(per_device, rows_n, CAP, width)
        return [swap(rows[:, k].reshape(slots, width), k) for k in range(rows_n)]

    outputs, input_grads = [], []
    dense_grads, gate_up_grads, down_grads = [], [], []
    all_sums, row_sums = [], []
    for m in micro:
        positions = col_index * own_count + jnp.arange(own_count)
        valid = (positions < seq_lengths[m, 0])[:, None]
        own_cot = jnp.where(valid, out_grad[m], jnp.zeros_like(out_grad[m]))
        cot = lax.all_gather(own_cot, "col", axis=0, tiled=True)
        xn = normed[m]
        y, squares, *saved = mixer_forward(xn, *weights, heads)
        mean_square = lax.psum(jnp.sum(squares, axis=0), "col") / inner
        inverse_rms = lax.rsqrt(mean_square + EPS)
        y_own = lax.psum_scatter(y, "col", scatter_dimension=0, tiled=True).astype(F32)
        own_rms = lax.dynamic_slice(inverse_rms, (col_index * own_count,), (own_count,))
        residual = own_rows[m] + own_rms[:, None] * y_own
        second = lax.all_gather(
            row_norm(residual, second_gain).astype(BF16), "col", axis=0, tiled=True
        )

        picks, slot_gates = dispatch(m)
        cot_rows = stack_rows(
            [
                swap((dot_plain(picks[k], cot) * slot_gates[k]).astype(BF16), k)
                for k in range(rows_n)
            ]
        )
        token_rows = stack_rows(
            [swap(dot_plain(picks[k], second).astype(BF16), k) for k in range(rows_n)]
        )
        pre = jnp.einsum("ecd,edh->ech", token_rows, gate_up, preferred_element_type=F32)
        gate_pre, up_pre = pre[..., :part_width], pre[..., part_width:]
        hidden = (jax.nn.silu(gate_pre) * up_pre).astype(BF16)
        d_hidden = jnp.einsum("ecd,ehd->ech", cot_rows, down, preferred_element_type=F32)
        d_pre = jnp.concatenate(
            [
                (d_hidden * up_pre * silu_slope(gate_pre)).astype(BF16),
                (d_hidden * jax.nn.silu(gate_pre)).astype(BF16),
            ],
            axis=2,
        )
        d_rows = jnp.einsum("ech,edh->ecd", d_pre, gate_up, preferred_element_type=F32)
        out_rows = jnp.einsum("ech,ehd->ecd", hidden, down, preferred_element_type=F32)
        gate_up_grads.append(
            jnp.einsum("ecd,ech->edh", token_rows, d_pre, preferred_element_type=F32)
        )
        down_grads.append(
            jnp.einsum("ech,ecd->ehd", hidden, cot_rows, preferred_element_type=F32)
        )

        shared_pre = dot_last(second, shared_in)
        shared_gate_pre = shared_pre[:, :shared_width]
        shared_up_pre = shared_pre[:, shared_width:]
        shared_hidden = (jax.nn.silu(shared_gate_pre) * shared_up_pre).astype(BF16)
        d_shared = dot_last(cot, shared_out)
        d_shared_pre = jnp.concatenate(
            [
                (d_shared * shared_up_pre * silu_slope(shared_gate_pre)).astype(BF16),
                (d_shared * jax.nn.silu(shared_gate_pre)).astype(BF16),
            ],
            axis=1,
        )

        pick_all = jnp.concatenate(picks, axis=0)
        back_rows = jnp.concatenate(send_back(d_rows), axis=0)
        second_part = dot_first(pick_all, back_rows) + dot_plain(d_shared_pre, shared_in)
        second_share = lax.psum_scatter(
            second_part.astype(BF16), "col", scatter_dimension=0, tiled=True
        ).astype(F32)
        residual_back, second_gain_grad = norm_adjoint(residual, second_gain, second_share)
        residual_grad = own_cot.astype(F32) + residual_back
        residual_low = residual_grad.astype(BF16)
        d_res = lax.all_gather(residual_low, "col", axis=0, tiled=True)
        cross = lax.all_gather(
            jnp.sum(residual_low.astype(F32) * y_own, axis=1), "col", axis=0, tiled=True
        )
        cube = inverse_rms * inverse_rms * inverse_rms * cross / inner
        scale_rows = jnp.pad(jnp.stack([inverse_rms, cube]), ((0, 6), (0, 0)))
        (
            first_part,
            gain_part,
            mixed,
            d_branch,
            d_conv,
            d_io,
            d_step,
            chan_grad,
            io_grad,
            head_grad,
        ) = mixer_backward(d_res, scale_rows, xn, weights, saved, heads)
        first_share = lax.psum_scatter(
            first_part, "col", scatter_dimension=0, tiled=True
        ).astype(F32)
        rows_back, _ = norm_adjoint(own_rows[m], first_gain, first_share)
        input_grads.append(residual_grad + rows_back)

        out_back = jnp.concatenate(
            [
                (gate * rows.astype(F32)).astype(BF16)
                for gate, rows in zip(slot_gates, send_back(out_rows))
            ],
            axis=0,
        )
        branch_part = dot_first(pick_all, out_back) + dot_plain(shared_hidden, shared_out)
        branch_share = lax.psum_scatter(
            branch_part.astype(BF16), "col", scatter_dimension=0, tiled=True
        ).astype(F32)
        outputs.append((residual + branch_share).astype(BF16))

        dense_grads.append(
            (
                dot_plain(d_branch, xn),
                dot_plain(d_conv, xn),
                dot_plain(d_io, xn),
                dot_plain(d_step, xn),
                dot_plain(mixed, d_res),
                dot_first(d_shared_pre, second),
                dot_first(shared_hidden, cot),
            )
        )
        all_sums.append(
            (jnp.sum(gain_part, axis=0) / first_gain, second_gain_grad, io_grad[:, :5].reshape(-1))
        )
        row_sums.append(
            (
                chan_grad[:, :6].reshape(-1),
                jnp.sum(chan_grad[:, 6].reshape(heads, size), axis=1),
                head_grad[:heads, 0],
                head_grad[:heads, 1],
            )
        )

    def total_of(parts):
        return jax.tree.map(lambda *terms: functools.reduce(jnp.add, terms), *parts)

    gate_up_total = total_of(gate_up_grads).astype(BF16)
    down_total = total_of(down_grads).astype(BF16)
    expert_gate_grad = jnp.zeros(expert_gate.shape, F32)
    expert_up_grad = jnp.zeros(expert_up.shape, F32)
    expert_down_grad = jnp.zeros(expert_down.shape, F32)
    for k in range(rows_n):
        at = peer(k) * depth
        first, hidden_at = unit_of(peer(k))
        part = swap(
            lax.dynamic_slice(gate_up_total, (0, at, 0), (per_device, depth, 2 * part_width)), k
        ).astype(F32)
        place = (first, 0, hidden_at)
        expert_gate_grad = lax.dynamic_update_slice(expert_gate_grad, part[..., :part_width], place)
        expert_up_grad = lax.dynamic_update_slice(expert_up_grad, part[..., part_width:], place)
        part = swap(
            lax.dynamic_slice(down_total, (0, 0, at), (per_device, part_width, depth)), k
        ).astype(F32)
        expert_down_grad = lax.dynamic_update_slice(expert_down_grad, part, (first, hidden_at, 0))

    dense = add_shares(jnp.concatenate(total_of(dense_grads), axis=0).astype(BF16))
    ends = []
    at = 0
    for rows in (share, share, 2 * NS, HEAD_ROWS, share, 2 * shared_width, shared_width):
        ends.append(dense[at : at + rows])
        at += rows
    branch_grad, conv_grad, io_proj_part, step_grad, out_grad_sum, shared_in_grad, down_grad = ends
    io_proj_grad = lax.psum_scatter(io_proj_part, "col", scatter_dimension=0, tiled=True)

    all_total = total_of(all_sums)
    row_total = total_of(row_sums)
    sums = lax.psum(jnp.concatenate(all_total + row_total), "row")
    all_count = sum(part.shape[0] for part in all_total)
    all_values = lax.psum(sums[:all_count], "col")
    first_gain_grad = all_values[:width]
    second_gain_grad = all_values[width : 2 * width]
    io_values = lax.dynamic_slice(
        all_values[2 * width :].reshape(2 * NS, 5), (col_index * io_width, 0), (io_width, 5)
    )
    chan_values = sums[all_count : all_count + 6 * share].reshape(share, 6)
    head_values = sums[all_count + 6 * share :]
    return (
        jnp.stack(outputs),
        jnp.stack(input_grads),
        first_gain_grad,
        branch_grad.T,
        conv_grad.T,
        io_proj_grad.T,
        step_grad[:heads].T,
        chan_values[:, :4].T,
        chan_values[:, 4],
        io_values[:, :4].T,
        io_values[:, 4],
        head_values[heads : 2 * heads],
        head_values[2 * heads :],
        head_values[:heads],
        chan_values[:, 5],
        out_grad_sum,
        second_gain_grad,
        expert_gate_grad,
        expert_up_grad,
        expert_down_grad,
        shared_in_grad[:shared_width].T,
        shared_in_grad[shared_width:].T,
        down_grad,
    )


def solution(mesh):
    both = P(None, ("row", "col"), None)
    placed = (
        both,
        both,
        P(None, "row"),
        P(None, "row", None),
        P(None, "row", None),
        P(),
        P("row", "col"),
        P("row", "col"),
        P("row", "col"),
        P("row", "col"),
        P(None, "col"),
        P("col"),
        P(None, "col"),
        P("col"),
        P("col"),
        P("col"),
        P("col"),
        P("col"),
        P("col", "row"),
        P(),
        P("col", "row", None),
        P("col", "row", None),
        P("col", None, "row"),
        P("row", "col"),
        P("row", "col"),
        P("col", "row"),
    )
    return jax.shard_map(
        local,
        mesh=mesh,
        in_specs=placed,
        out_specs=(both, both, P()) + placed[6:19] + (P(),) + placed[20:],
        check_vma=False,
    )
```

```python
import functools

import jax
import jax.numpy as jnp
from jax import lax
from jax.experimental import pallas as pl
from jax.experimental.pallas import tpu as pltpu
from jax.sharding import PartitionSpec as P

NS = 128
BLOCK = 256
CAP = 144
EPS = 1e-05
HEAD_ROWS = 16
LANES = 128
F32 = jnp.float32
BF16 = jnp.bfloat16
VMEM = pl.BlockSpec(memory_space=pltpu.VMEM)
VMEM_LIMIT = 56 * 1024 * 1024
KERNEL_COST = pl.CostEstimate(flops=3 * 10**10, bytes_accessed=2**20, transcendentals=0)
ANY = pl.BlockSpec(memory_space=pl.ANY)
MESH = pl.DeviceIdType.MESH


def contract(left_op, right_op, left_dim, right_dim, precision=None):
    return lax.dot_general(
        left_op,
        right_op,
        (((left_dim,), (right_dim,)), ((), ())),
        preferred_element_type=F32,
        precision=precision,
    )


def dot_plain(left_op, right_op):
    return contract(left_op, right_op, 1, 0)


def dot_first(left_op, right_op):
    return contract(left_op, right_op, 0, 0)


def dot_last(left_op, right_op):
    return contract(left_op, right_op, 1, 1)


def silu_slope(values):
    logistic = jax.nn.sigmoid(values)
    return logistic * (1.0 + values * (1.0 - logistic))


def softplus(values):
    return jnp.maximum(values, 0.0) + jnp.log1p(jnp.exp(-jnp.abs(values)))


def shifts_back(current, before):
    joined = jnp.concatenate([before, current], axis=1)
    return [pltpu.roll(joined, step, 1)[:, LANES:] for step in (1, 2, 3)]


def load_block(ref, rows, block):
    cols = pl.ds(pl.multiple_of(block * BLOCK, BLOCK), BLOCK)
    current = ref[rows, cols]
    ahead = pl.multiple_of(jnp.maximum(block * BLOCK - LANES, 0), LANES)
    before = jnp.where(block > 0, ref[rows, pl.ds(ahead, LANES)], 0.0)
    return current, shifts_back(current, before)


def convolved(current, back, taps):
    return (
        taps[:, 4:5]
        + taps[:, 3:4] * current
        + taps[:, 2:3] * back[0]
        + taps[:, 1:2] * back[1]
        + taps[:, 0:1] * back[2]
    )


def conv_adjoint(adjoint, after, taps):
    joined = jnp.concatenate([adjoint, after], axis=1)
    width = joined.shape[1]
    total = taps[:, 3:4] * adjoint
    for step in (1, 2, 3):
        ahead = pltpu.roll(joined, width - step, 1)[:, :BLOCK]
        total = total + taps[:, 3 - step : 4 - step] * ahead
    return total


def lane_tile(columns):
    rows = columns[0].shape[0]
    lane = lax.broadcasted_iota(jnp.int32, (rows, LANES), 1)
    tile = jnp.zeros((rows, LANES), F32)
    for place, column in enumerate(columns):
        tile = jnp.where(lane == place, column, tile)
    return tile


def row_sum(values):
    return jnp.sum(values, axis=1, keepdims=True)


def decay_block(cum_row, cum_cols, head):
    lane = lax.broadcasted_iota(jnp.int32, cum_cols.shape, 1)
    cum_col = row_sum(jnp.where(lane == head, cum_cols, 0.0))
    place_j = lax.broadcasted_iota(jnp.int32, (BLOCK, BLOCK), 0)
    place_i = lax.broadcasted_iota(jnp.int32, (BLOCK, BLOCK), 1)
    return jnp.exp(jnp.where(place_j <= place_i, cum_row - cum_col, -1e30))


def step_rows(step_pre, head_params, step_s, cum_s, cum_t_s, blocks):
    step = softplus(step_pre + head_params[:, 0:1])
    step_s[...] = step
    log_decay = -(step * head_params[:, 1:2])
    place_j = lax.broadcasted_iota(jnp.int32, (BLOCK, BLOCK), 0)
    place_i = lax.broadcasted_iota(jnp.int32, (BLOCK, BLOCK), 1)
    upper = jnp.where(place_j <= place_i, 1.0, 0.0)
    for block in range(blocks):
        cols = slice(block * BLOCK, (block + 1) * BLOCK)
        cum = contract(log_decay[:, cols], upper, 1, 0, lax.Precision.HIGHEST)
        cum_s[:, cols] = cum
        cum_t_s[cols, :] = jnp.transpose(cum)


def score_blocks(io, scores_s, blocks):
    for block in range(blocks):
        cols = slice(block * BLOCK, (block + 1) * BLOCK)
        scores_s[block] = dot_first(io[:NS, cols], io[NS:, cols])


def block_cols(block):
    return pl.ds(pl.multiple_of(block * BLOCK, BLOCK), BLOCK)


def greet(peers):
    barrier = pltpu.get_barrier_semaphore()
    for other in peers:
        pl.semaphore_signal(barrier, inc=1, device_id=other, device_id_type=MESH)
    pl.semaphore_wait(barrier, len(peers))


def row_partners(members):
    me = lax.axis_index("row")
    return [{"row": me ^ k} for k in range(1, members)]


def send(source, target, send_sem, recv_sem, other):
    copy = pltpu.make_async_remote_copy(
        src_ref=source,
        dst_ref=target,
        send_sem=send_sem,
        recv_sem=recv_sem,
        device_id=other,
        device_id_type=MESH,
    )
    copy.start()
    return copy


def send_parts(parts, received, sems):
    partners = row_partners(len(parts) + 1)
    greet(partners)
    return [
        send(parts[k], received[k], sems.at[0, k], sems.at[1, k], other)
        for k, other in enumerate(partners)
    ]


def mixer_forward_kernel(
    heads,
    xn,
    wb,
    wc,
    wio,
    ws,
    wo,
    chan,
    io_taps,
    head_params,
    *refs,
):
    refs = list(refs)
    count = (len(refs) - 14) // 2
    parts, refs = refs[:count], refs[count:]
    y, squares, branch, conv, io_pre, io, step_pre, starts = refs[:8]
    received = refs[8 : 8 + count]
    step_s, cum_s, cum_t_s, scores_s, z_s, sems = refs[8 + count :]
    copies = send_parts(parts, received, sems)
    length = xn.shape[0]
    blocks = length // BLOCK
    size = wb.shape[0] // heads
    step_pre[...] = dot_last(ws[...], xn[...])
    step_rows(step_pre[...], head_params[...], step_s, cum_s, cum_t_s, blocks)

    def project(block, carry):
        cols = block_cols(block)
        rows = xn[cols, :]
        io_pre[:, cols] = dot_last(wio[...], rows)
        branch[:, cols] = dot_last(wb[...], rows)
        conv[:, cols] = dot_last(wc[...], rows)
        return carry

    lax.fori_loop(0, blocks, project, 0)

    def io_step(at, carry):
        rows = pl.ds(pl.multiple_of((at // blocks) * 64, 64), 64)
        block = at % blocks
        current, back = load_block(io_pre, rows, block)
        io[rows, block_cols(block)] = jax.nn.silu(
            convolved(current, back, io_taps[rows, :])
        ).astype(BF16)
        return carry

    lax.fori_loop(0, blocks * (2 * NS // 64), io_step, 0)
    score_blocks(io, scores_s, blocks)
    squares[...] = jnp.zeros_like(squares)

    def head_step(head, carry):
        rows = pl.ds(pl.multiple_of(head * size, size), size)
        params = chan[rows, :]

        def block_step(block, state):
            cols = block_cols(block)
            current, back = load_block(conv, rows, block)
            x = jax.nn.silu(convolved(current, back, params))
            step_row = step_s[pl.ds(head, 1), cols]
            cum_row = cum_s[pl.ds(head, 1), cols]
            last = cum_row[:, BLOCK - 1 : BLOCK]
            mixing = (scores_s[block] * decay_block(cum_row, cum_t_s[cols, :], head)).astype(BF16)
            weighted = x * step_row
            starts[pl.ds(pl.multiple_of((head * blocks + block) * size, size), size), :] = state
            scanned = dot_plain(weighted.astype(BF16), mixing)
            scanned = scanned + dot_plain(state.astype(BF16), io[NS:, cols]) * jnp.exp(cum_row)
            scanned = scanned + params[:, 6:7] * x
            gated = scanned * jax.nn.silu(branch[rows, cols])
            squares[:, cols] += jnp.sum((gated * gated).reshape(size // 8, 8, BLOCK), axis=0)
            z_s[rows, cols] = (gated * params[:, 5:6]).astype(BF16)
            to_end = (weighted * jnp.exp(last - cum_row)).astype(BF16)
            return state * jnp.exp(last) + dot_last(to_end, io[:NS, cols])

        lax.fori_loop(0, blocks, block_step, jnp.zeros((size, NS), F32))
        return carry

    lax.fori_loop(0, heads, head_step, 0)

    def out_step(block, carry):
        cols = block_cols(block)
        y[cols, :] = dot_first(z_s[:, cols], wo[...]).astype(BF16)
        return carry

    lax.fori_loop(0, blocks, out_step, 0)
    for copy in copies:
        copy.wait()


def mixer_forward(parts, xn, wb, wc, wio, ws, wo, chan, io_taps, head_params, heads):
    length, width = xn.shape
    share = wb.shape[0]
    blocks = length // BLOCK
    size = share // heads
    shape = jax.ShapeDtypeStruct
    out = pl.pallas_call(
        functools.partial(mixer_forward_kernel, heads),
        out_shape=(
            shape((length, width), BF16),
            shape((8, length), F32),
            shape((share, length), F32),
            shape((share, length), F32),
            shape((2 * NS, length), F32),
            shape((2 * NS, length), BF16),
            shape((HEAD_ROWS, length), F32),
            shape((heads * blocks * size, NS), F32),
        )
        + tuple(shape(part.shape, part.dtype) for part in parts),
        in_specs=[VMEM] * 9 + [ANY] * len(parts),
        out_specs=(VMEM,) * 8 + (ANY,) * len(parts),
        scratch_shapes=[
            pltpu.VMEM((HEAD_ROWS, length), F32),
            pltpu.VMEM((HEAD_ROWS, length), F32),
            pltpu.VMEM((length, HEAD_ROWS), F32),
            pltpu.VMEM((blocks, BLOCK, BLOCK), F32),
            pltpu.VMEM((share, length), BF16),
            pltpu.SemaphoreType.DMA((2, len(parts))),
        ],
        compiler_params=pltpu.CompilerParams(
            vmem_limit_bytes=VMEM_LIMIT, collective_id=2, has_side_effects=True
        ),
        cost_estimate=KERNEL_COST,
    )(xn, wb, wc, wio, ws, wo, chan, io_taps, head_params, *parts)
    return out[:8], out[8:]


def mixer_backward_kernel(
    heads,
    d_res,
    scale_rows,
    xn,
    wb,
    wc,
    wio,
    ws,
    wo,
    chan,
    io_taps,
    head_params,
    branch,
    conv,
    io_pre,
    io,
    step_pre,
    starts,
    *refs,
):
    refs = list(refs)
    count = (len(refs) - 22) // 2
    parts, refs = refs[:count], refs[count:]
    first_part, gain_part, mixed, d_branch, d_conv, d_io, d_step = refs[:7]
    chan_grad, io_grad, head_grad = refs[7:10]
    received, refs = refs[10 : 10 + count], refs[10 + count :]
    step_s, cum_s, cum_t_s, scores_s, d_scores_s, d_mixed_s, d_io_s = refs[:7]
    d_cum_s, d_size_s, adjoint_s, cube_s, sems = refs[7:]
    copies = send_parts(parts, received, sems)
    length, width = xn.shape
    blocks = length // BLOCK
    size = wb.shape[0] // heads
    step_rows(step_pre[...], head_params[...], step_s, cum_s, cum_t_s, blocks)
    score_blocks(io, scores_s, blocks)
    d_scores_s[...] = jnp.zeros_like(d_scores_s)
    d_io_s[...] = jnp.zeros_like(d_io_s)
    d_cum_s[...] = jnp.zeros_like(d_cum_s)
    d_size_s[...] = jnp.zeros_like(d_size_s)
    chan_grad[...] = jnp.zeros_like(chan_grad)
    io_grad[...] = jnp.zeros_like(io_grad)
    adjoint_s[:, length:] = jnp.zeros((adjoint_s.shape[0], LANES), F32)

    def project(block, carry):
        cols = block_cols(block)
        d_mixed_s[:, cols] = dot_last(wo[...], d_res[cols, :width])
        cross = jnp.transpose(d_res[cols, width:].astype(F32))
        cross = cross[0:1] + cross[1:2] + cross[2:3]
        rms = scale_rows[0:1, cols]
        cube_s[:, cols] = rms * rms * rms * cross * scale_rows[1:2, cols]
        return carry

    lax.fori_loop(0, blocks, project, 0)

    def head_step(head, carry):
        rows = pl.ds(pl.multiple_of(head * size, size), size)
        params = chan[rows, :]

        def block_step(reverse, d_state):
            block = blocks - 1 - reverse
            cols = block_cols(block)
            state = starts[pl.ds(pl.multiple_of((head * blocks + block) * size, size), size), :]
            state_low = state.astype(BF16)
            d_state_low = d_state.astype(BF16)
            write_rows = io[:NS, cols]
            read_rows = io[NS:, cols]
            step_row = step_s[pl.ds(head, 1), cols]
            cum_row = cum_s[pl.ds(head, 1), cols]
            last = cum_row[:, BLOCK - 1 : BLOCK]
            decays = decay_block(cum_row, cum_t_s[cols, :], head)
            mixing = (scores_s[block] * decays).astype(BF16)
            current, back = load_block(conv, rows, block)
            conv_act = convolved(current, back, params)
            logistic = jax.nn.sigmoid(conv_act)
            x = conv_act * logistic
            slope = logistic * (1.0 + conv_act * (1.0 - logistic))
            weighted = x * step_row
            weighted_low = weighted.astype(BF16)
            grown = jnp.exp(cum_row)
            within = dot_plain(weighted_low, mixing)
            carried = dot_plain(state_low, read_rows) * grown
            scanned = within + carried + params[:, 6:7] * x

            inverse_rms = scale_rows[0:1, cols]
            gate_in = branch[rows, cols]
            gate_logistic = jax.nn.sigmoid(gate_in)
            gate_out = gate_in * gate_logistic
            gated = scanned * gate_out
            d_mixed = d_mixed_s[rows, cols]
            gain = params[:, 5:6]
            mixed[rows, cols] = (gated * inverse_rms * gain).astype(BF16)
            d_gated = inverse_rms * (d_mixed * gain) - gated * cube_s[:, cols]
            d_gain = row_sum(d_mixed * gated * inverse_rms)
            d_scanned = d_gated * gate_out
            d_branch[rows, cols] = (
                d_gated * scanned * (gate_logistic * (1.0 + gate_in * (1.0 - gate_logistic)))
            ).astype(BF16)
            d_low = d_scanned.astype(BF16)
            d_skip = row_sum(d_scanned * x)

            d_within = dot_last(d_low, mixing)
            shrunk = jnp.exp(last - cum_row)
            d_fed = dot_plain(d_state_low, write_rows) * shrunk
            d_weighted = d_within + d_fed
            d_scores_s[block] += dot_first(weighted_low, d_low) * decays
            d_grown = (d_scanned * grown).astype(BF16)
            fed = (weighted * shrunk).astype(BF16)
            d_io_s[NS:, cols] += dot_first(state_low, d_grown)
            d_io_s[:NS, cols] += dot_first(d_state_low, fed)
            d_before = d_state * jnp.exp(last) + dot_last(d_grown, read_rows)

            fed_terms = weighted * d_fed
            d_cum = jnp.sum(
                d_low.astype(F32) * within
                - weighted_low.astype(F32) * d_within
                + d_scanned * carried
                - fed_terms,
                axis=0,
                keepdims=True,
            )
            at_end = jnp.sum(row_sum(fed_terms), axis=0, keepdims=True) + jnp.exp(last) * jnp.sum(
                row_sum(d_state * state), axis=0, keepdims=True
            )
            lane = lax.broadcasted_iota(jnp.int32, (1, BLOCK), 1)
            d_cum_s[pl.ds(head, 1), cols] = d_cum + jnp.where(lane == BLOCK - 1, at_end, 0.0)
            d_size_s[pl.ds(head, 1), cols] = jnp.sum(d_weighted * x, axis=0, keepdims=True)

            d_act = (d_weighted * step_row + params[:, 6:7] * d_scanned) * slope
            adjoint_s[:, cols] = d_act
            after = adjoint_s[:, pl.ds(pl.multiple_of((block + 1) * BLOCK, BLOCK), LANES)]
            d_conv[rows, cols] = conv_adjoint(d_act, after, params).astype(BF16)
            chan_grad[rows, :] += lane_tile(
                [
                    row_sum(d_act * back[2]),
                    row_sum(d_act * back[1]),
                    row_sum(d_act * back[0]),
                    row_sum(d_act * current),
                    row_sum(d_act),
                    d_gain,
                    d_skip,
                ]
            )
            return d_before

        lax.fori_loop(0, blocks, block_step, jnp.zeros((size, NS), F32))
        return carry

    lax.fori_loop(0, heads, head_step, 0)

    def scores_step(block, carry):
        cols = block_cols(block)
        d_scores = d_scores_s[block].astype(BF16)
        d_io_s[NS:, cols] += dot_plain(io[:NS, cols], d_scores)
        d_io_s[:NS, cols] += dot_last(io[NS:, cols], d_scores)
        return carry

    lax.fori_loop(0, blocks, scores_step, 0)

    def io_step(at, carry):
        rows = pl.ds(pl.multiple_of((at // blocks) * 64, 64), 64)
        block = blocks - 1 - at % blocks
        cols = block_cols(block)
        taps = io_taps[rows, :]
        current, back = load_block(io_pre, rows, block)
        d_act = d_io_s[rows, cols] * silu_slope(convolved(current, back, taps))
        adjoint_s[:64, cols] = d_act
        after = adjoint_s[:64, pl.ds(pl.multiple_of((block + 1) * BLOCK, BLOCK), LANES)]
        d_io[rows, cols] = conv_adjoint(d_act, after, taps).astype(BF16)
        io_grad[rows, :] += lane_tile(
            [
                row_sum(d_act * back[2]),
                row_sum(d_act * back[1]),
                row_sum(d_act * back[0]),
                row_sum(d_act * current),
                row_sum(d_act),
            ]
        )
        return carry

    lax.fori_loop(0, blocks * (2 * NS // 64), io_step, 0)

    place_j = lax.broadcasted_iota(jnp.int32, (BLOCK, BLOCK), 0)
    place_i = lax.broadcasted_iota(jnp.int32, (BLOCK, BLOCK), 1)
    lower = jnp.where(place_j >= place_i, 1.0, 0.0)
    rate = head_params[:, 1:2]
    decay_grad = jnp.zeros((HEAD_ROWS, 1), F32)
    offset_grad = jnp.zeros((HEAD_ROWS, 1), F32)
    for block in range(blocks):
        cols = slice(block * BLOCK, (block + 1) * BLOCK)
        d_log = contract(d_cum_s[:, cols], lower, 1, 0, lax.Precision.HIGHEST)
        decay_grad = decay_grad - row_sum(step_s[:, cols] * rate * d_log)
        d_size = d_size_s[:, cols] - rate * d_log
        d_pre = d_size * jax.nn.sigmoid(step_pre[:, cols] + head_params[:, 0:1])
        offset_grad = offset_grad + row_sum(d_pre)
        d_step[:, cols] = d_pre.astype(BF16)
    head_grad[...] = lane_tile([decay_grad, offset_grad])
    gain_part[...] = jnp.zeros_like(gain_part)

    def first_step(block, carry):
        cols = block_cols(block)
        part = (
            dot_first(d_branch[:, cols], wb[...])
            + dot_first(d_conv[:, cols], wc[...])
            + dot_first(d_io[:, cols], wio[...])
            + dot_first(d_step[:, cols], ws[...])
        )
        first_part[cols, :] = part.astype(BF16)
        product = part * xn[cols, :].astype(F32)
        gain_part[...] += jnp.sum(product.reshape(BLOCK // 8, 8, -1), axis=0)
        return carry

    lax.fori_loop(0, blocks, first_step, 0)
    for copy in copies:
        copy.wait()


def mixer_backward(parts, d_res, scale_rows, xn, weights, saved, heads):
    length, width = xn.shape
    share = weights[0].shape[0]
    blocks = length // BLOCK
    size = share // heads
    shape = jax.ShapeDtypeStruct
    out = pl.pallas_call(
        functools.partial(mixer_backward_kernel, heads),
        out_shape=(
            shape((length, width), BF16),
            shape((8, width), F32),
            shape((share, length), BF16),
            shape((share, length), BF16),
            shape((share, length), BF16),
            shape((2 * NS, length), BF16),
            shape((HEAD_ROWS, length), BF16),
            shape((share, LANES), F32),
            shape((2 * NS, LANES), F32),
            shape((HEAD_ROWS, LANES), F32),
        )
        + tuple(shape(part.shape, part.dtype) for part in parts),
        in_specs=[VMEM] * 17 + [ANY] * len(parts),
        out_specs=(VMEM,) * 10 + (ANY,) * len(parts),
        scratch_shapes=[
            pltpu.VMEM((HEAD_ROWS, length), F32),
            pltpu.VMEM((HEAD_ROWS, length), F32),
            pltpu.VMEM((length, HEAD_ROWS), F32),
            pltpu.VMEM((blocks, BLOCK, BLOCK), F32),
            pltpu.VMEM((blocks, BLOCK, BLOCK), F32),
            pltpu.VMEM((share, length), F32),
            pltpu.VMEM((2 * NS, length), F32),
            pltpu.VMEM((HEAD_ROWS, length), F32),
            pltpu.VMEM((HEAD_ROWS, length), F32),
            pltpu.VMEM((size, length + LANES), F32),
            pltpu.VMEM((1, length), F32),
            pltpu.SemaphoreType.DMA((2, len(parts))),
        ],
        compiler_params=pltpu.CompilerParams(
            vmem_limit_bytes=VMEM_LIMIT, collective_id=3, has_side_effects=True
        ),
        cost_estimate=KERNEL_COST,
    )(d_res, scale_rows, xn, *weights, *saved, *parts)
    return out[:10], out[10:]


def call(kernel, out_shape, scratch, in_specs, args):
    return pl.pallas_call(
        kernel,
        out_shape=out_shape,
        in_specs=in_specs,
        out_specs=jax.tree.map(lambda _: VMEM, out_shape),
        scratch_shapes=scratch,
        compiler_params=pltpu.CompilerParams(vmem_limit_bytes=VMEM_LIMIT),
        cost_estimate=KERNEL_COST,
    )(*args)


def place_rows(slot_t, gates_t, placed):
    length, units = slot_t.shape

    def choose(block, carry):
        at = block_cols(block)
        slots = slot_t[at, :]
        for tile in range(units * CAP // LANES):
            low, high = tile * LANES // CAP, (tile * LANES + LANES - 1) // CAP
            lane = lax.broadcasted_iota(jnp.int32, (BLOCK, LANES), 1) + tile * LANES
            total = jnp.zeros((BLOCK, LANES), F32)
            for unit in range(low, high + 1):
                value = 1.0 if gates_t is None else gates_t[at, unit : unit + 1]
                total = jnp.where(lane == slots[:, unit : unit + 1] + unit * CAP, value, total)
            placed[at, tile * LANES : (tile + 1) * LANES] = total.astype(BF16)
        return carry

    lax.fori_loop(0, length // BLOCK, choose, 0)


def combine_kernel(members, slot_t, gates_t, extra_left, extra_right, *refs):
    rows, (out, chosen_s, rows_s, sems) = refs[:members], refs[members:]
    length, units = slot_t.shape
    part = units // members * CAP
    copies = []
    for member in range(members):
        copies.append(
            pltpu.make_async_copy(
                rows[member], rows_s.at[pl.ds(member * part, part)], sems.at[member]
            )
        )
        copies[-1].start()

    place_rows(slot_t, gates_t, chosen_s)
    for copy in copies:
        copy.wait()

    def columns(at, carry):
        cols = block_cols(at)
        total = dot_plain(chosen_s[...], rows_s[:, cols])
        total = total + dot_plain(extra_left[...], extra_right[:, cols])
        out[:, cols] = total.astype(BF16)
        return carry

    lax.fori_loop(0, out.shape[1] // BLOCK, columns, 0)


def combine_rows(slot_t, gates_t, rows, extra_left, extra_right):
    length, units = slot_t.shape
    members = len(rows)
    width = rows[0].shape[1]
    return call(
        functools.partial(combine_kernel, members),
        jax.ShapeDtypeStruct((length, width), BF16),
        [
            pltpu.VMEM((length, units * CAP), BF16),
            pltpu.VMEM((units * CAP, width), BF16),
            pltpu.SemaphoreType.DMA((members,)),
        ],
        [VMEM] * 4 + [ANY] * members,
        (slot_t, gates_t, extra_left, extra_right, *rows),
    )


def exchange_kernel(members, slot, gates, slot_t, second, cot, gate_sh, up_sh, down_sh, *refs):
    refs = list(refs)
    shards = [refs[at * members : (at + 1) * members] for at in range(3)]
    part, out_rows, hidden_sh, d_gate_sh, d_up_sh, token_out, cot_out, hidden_s, d_pre_s = refs[
        3 * members : 3 * members + 9
    ]
    (
        token_s,
        cot_s,
        token_send,
        cot_send,
        back_s,
        weights,
        chosen_s,
        gate_s,
        places_s,
        row_sems,
        weight_sems,
        out_sems,
    ) = refs[3 * members + 9 :]
    units, length = slot.shape
    width = second.shape[1]
    experts = units // members
    rows = experts * CAP
    hidden_width = weights.shape[3]
    depth = width // members
    chunk = min(BLOCK, hidden_width)
    me = lax.axis_index("row")
    partners = row_partners(members)
    weight_copies = []
    for member in range(members):
        place = pl.ds(pl.multiple_of((me ^ member) * depth, depth), depth)
        for which in range(3):
            weight_copies.append(
                pltpu.make_async_copy(
                    shards[which][member],
                    weights.at[which, :, place],
                    weight_sems.at[which, member],
                )
            )
            weight_copies[-1].start()
    greet(partners)

    def choose(unit, carry):
        at = pl.ds(pl.multiple_of(unit * CAP, CAP), CAP)
        place = lax.broadcasted_iota(jnp.int32, (CAP, length), 0)
        hit = place == slot[pl.ds(unit, 1), :]
        chosen_s[at, :] = jnp.where(hit, 1.0, 0.0).astype(BF16)
        gate_s[at, :] = row_sum(jnp.where(hit, gates[pl.ds(unit, 1), :], 0.0))
        return carry

    lax.fori_loop(0, units, choose, 0)

    def pick(source, weighted, kept, outgoing, first_sem):
        def columns(at, carry):
            cols = block_cols(at)
            picked = dot_plain(chosen_s[...], source[:, cols])
            if weighted:
                picked = picked * gate_s[...]
            picked = picked.astype(BF16)
            for expert in range(experts):
                kept[expert, :CAP, cols] = picked[expert * CAP : (expert + 1) * CAP]
            outgoing[:, cols] = picked[rows:]
            return carry

        lax.fori_loop(0, width // BLOCK, columns, 0)
        copies = []
        for k, other in enumerate(partners):
            for expert in range(experts):
                copies.append(
                    send(
                        outgoing.at[pl.ds(k * rows + expert * CAP, CAP)],
                        kept.at[expert, pl.ds((k + 1) * CAP, CAP)],
                        row_sems.at[first_sem, k, expert],
                        row_sems.at[first_sem + 1, k, expert],
                        other,
                    )
                )
        return copies

    copies = pick(cot, True, cot_s, cot_send, 0)
    copies += pick(second, False, token_s, token_send, 2)

    def shared_step(at, carry):
        at = block_cols(at)
        gate_pre = dot_last(second[at, :], gate_sh[...])
        up_pre = dot_last(second[at, :], up_sh[...])
        d_hidden = dot_last(cot[at, :], down_sh[...])
        logistic = jax.nn.sigmoid(gate_pre)
        active = gate_pre * logistic
        hidden_sh[at, :] = (active * up_pre).astype(BF16)
        slope = logistic * (1.0 + gate_pre * (1.0 - logistic))
        d_gate_sh[at, :] = (d_hidden * up_pre * slope).astype(BF16)
        d_up_sh[at, :] = (d_hidden * active).astype(BF16)
        return carry

    lax.fori_loop(0, length // BLOCK, shared_step, 0)
    for copy in weight_copies:
        copy.wait()
    for copy in copies:
        copy.wait()
    saves = [
        pltpu.make_async_copy(token_s, token_out, out_sems.at[0]),
        pltpu.make_async_copy(cot_s, cot_out, out_sems.at[1]),
    ]
    for copy in saves:
        copy.start()

    copies = []
    for expert in range(experts):

        def hidden_step(at, carry):
            cols = pl.ds(pl.multiple_of(at * chunk, chunk), chunk)
            up_cols = pl.ds(pl.multiple_of(hidden_width + at * chunk, chunk), chunk)
            gate_pre = dot_plain(token_s[expert], weights[0, expert, :, cols])
            up_pre = dot_plain(token_s[expert], weights[1, expert, :, cols])
            d_hidden = dot_plain(cot_s[expert], weights[2, expert, :, cols])
            logistic = jax.nn.sigmoid(gate_pre)
            active = gate_pre * logistic
            hidden_s[expert, :, cols] = (active * up_pre).astype(BF16)
            slope = logistic * (1.0 + gate_pre * (1.0 - logistic))
            d_pre_s[expert, :, cols] = (d_hidden * up_pre * slope).astype(BF16)
            d_pre_s[expert, :, up_cols] = (d_hidden * active).astype(BF16)
            return carry

        lax.fori_loop(0, hidden_width // chunk, hidden_step, 0)

        def back_step(at, carry):
            cols = block_cols(at)
            back = dot_last(d_pre_s[expert, :, :hidden_width], weights[0, expert, cols, :])
            back = back + dot_last(d_pre_s[expert, :, hidden_width:], weights[1, expert, cols, :])
            back = back.astype(BF16)
            back_s[expert * CAP : (expert + 1) * CAP, cols] = back[:CAP]
            for k in range(members - 1):
                token_send[k * rows + expert * CAP : k * rows + (expert + 1) * CAP, cols] = back[
                    (k + 1) * CAP : (k + 2) * CAP
                ]
            return carry

        lax.fori_loop(0, width // BLOCK, back_step, 0)
        for k, other in enumerate(partners):
            copies.append(
                send(
                    token_send.at[pl.ds(k * rows + expert * CAP, CAP)],
                    back_s.at[pl.ds((k + 1) * rows + expert * CAP, CAP)],
                    row_sems.at[4, k, expert],
                    row_sems.at[5, k, expert],
                    other,
                )
            )

    for expert in range(experts):

        def ahead_step(at, carry):
            cols = block_cols(at)
            ahead = dot_last(hidden_s[expert], weights[2, expert, cols, :]).astype(BF16)
            for member in range(members):
                out_rows[member, expert * CAP : (expert + 1) * CAP, cols] = ahead[
                    member * CAP : (member + 1) * CAP
                ]
            return carry

        lax.fori_loop(0, width // BLOCK, ahead_step, 0)

    place_rows(slot_t, None, places_s)
    for copy in copies:
        copy.wait()

    def columns(at, carry):
        cols = block_cols(at)
        total = dot_plain(places_s[...], back_s[:, cols])
        total = total + dot_plain(d_gate_sh[...], gate_sh[:, cols])
        total = total + dot_plain(d_up_sh[...], up_sh[:, cols])
        part[:, cols] = total.astype(BF16)
        return carry

    lax.fori_loop(0, width // BLOCK, columns, 0)
    for copy in saves:
        copy.wait()


def exchange_rows(slot, gates, slot_t, second, cot, shared_w, gate_parts, up_parts, down_parts):
    members = len(gate_parts)
    units, length = slot.shape
    width = second.shape[1]
    experts = units // members
    rows = experts * CAP
    hidden_width = gate_parts[0].shape[2]
    shared_width = shared_w[0].shape[0]
    shape = jax.ShapeDtypeStruct
    stacked = (experts, members * CAP, width)
    shared = shape((length, shared_width), BF16)
    return pl.pallas_call(
        functools.partial(exchange_kernel, members),
        out_shape=(
            shape((length, width), BF16),
            shape((members, rows, width), BF16),
            shared,
            shared,
            shared,
            shape(stacked, BF16),
            shape(stacked, BF16),
            shape((experts, members * CAP, hidden_width), BF16),
            shape((experts, members * CAP, 2 * hidden_width), BF16),
        ),
        in_specs=[VMEM] * 8 + [ANY] * (3 * members),
        out_specs=(VMEM,) * 5 + (ANY,) * 2 + (VMEM,) * 2,
        scratch_shapes=[
            pltpu.VMEM(stacked, BF16),
            pltpu.VMEM(stacked, BF16),
            pltpu.VMEM(((members - 1) * rows, width), BF16),
            pltpu.VMEM(((members - 1) * rows, width), BF16),
            pltpu.VMEM((members * rows, width), BF16),
            pltpu.VMEM((3, experts, width, hidden_width), BF16),
            pltpu.VMEM((units * CAP, length), BF16),
            pltpu.VMEM((units * CAP, 1), F32),
            pltpu.VMEM((length, units * CAP), BF16),
            pltpu.SemaphoreType.DMA((6, members - 1, experts)),
            pltpu.SemaphoreType.DMA((3, members)),
            pltpu.SemaphoreType.DMA((2,)),
        ],
        compiler_params=pltpu.CompilerParams(
            vmem_limit_bytes=VMEM_LIMIT, collective_id=4, has_side_effects=True
        ),
        cost_estimate=KERNEL_COST,
    )(slot, gates, slot_t, second, cot, *shared_w, *gate_parts, *up_parts, *down_parts)


def gather_kernel(
    rows_n, cols_n, pack, io, taps, pack_all, io_all, taps_all, row_sems, io_sems, tap_sems, own_sems
):
    me, at = lax.axis_index("row"), lax.axis_index("col")
    io_rows = io.shape[0]
    place = pl.ds(pl.multiple_of(at * io_rows, io_rows), io_rows)
    row_peers = [{"row": me ^ k} for k in range(1, rows_n)]
    col_peers = [{"col": at ^ k} for k in range(1, cols_n)]
    barrier = pltpu.get_barrier_semaphore()
    for other in row_peers + col_peers:
        pl.semaphore_signal(barrier, inc=1, device_id=other, device_id_type=MESH)
    pl.semaphore_wait(barrier, rows_n + cols_n - 2)

    def send(source, target, sems, k, other):
        copy = pltpu.make_async_remote_copy(
            src_ref=source,
            dst_ref=target,
            send_sem=sems.at[0, k],
            recv_sem=sems.at[1, k],
            device_id=other,
            device_id_type=MESH,
        )
        copy.start()
        return copy

    own = [
        pltpu.make_async_copy(pack, pack_all.at[me], own_sems.at[0]),
        pltpu.make_async_copy(io, io_all.at[me, place], own_sems.at[1]),
        pltpu.make_async_copy(taps, taps_all.at[place], own_sems.at[2]),
    ]
    for copy in own:
        copy.start()
    io_copies = [
        send(io, io_all.at[me, place], io_sems, k, other) for k, other in enumerate(col_peers)
    ]
    copies = [
        send(taps, taps_all.at[place], tap_sems, k, other) for k, other in enumerate(col_peers)
    ]
    copies += [
        send(pack, pack_all.at[me], row_sems, k, other) for k, other in enumerate(row_peers)
    ]
    own[1].wait()
    for copy in io_copies:
        copy.wait()
    copies += [
        send(io_all.at[me], io_all.at[me], row_sems, rows_n - 1 + k, other)
        for k, other in enumerate(row_peers)
    ]
    own[0].wait()
    own[2].wait()
    for copy in copies:
        copy.wait()


def gather_weights(pack, io, taps, rows_n, cols_n):
    shape = jax.ShapeDtypeStruct
    return pl.pallas_call(
        functools.partial(gather_kernel, rows_n, cols_n),
        out_shape=(
            shape((rows_n,) + pack.shape, BF16),
            shape((rows_n, cols_n * io.shape[0], io.shape[1]), BF16),
            shape((cols_n * io.shape[0], taps.shape[1]), BF16),
        ),
        in_specs=[ANY] * 3,
        out_specs=(ANY,) * 3,
        scratch_shapes=[
            pltpu.SemaphoreType.DMA((2, 2 * (rows_n - 1))),
            pltpu.SemaphoreType.DMA((2, cols_n - 1)),
            pltpu.SemaphoreType.DMA((2, cols_n - 1)),
            pltpu.SemaphoreType.DMA((3,)),
        ],
        compiler_params=pltpu.CompilerParams(collective_id=1, has_side_effects=True),
        cost_estimate=pl.CostEstimate(flops=1, bytes_accessed=1, transcendentals=0),
    )(pack, io, taps)


def row_norm(values, scale_gain):
    return values * lax.rsqrt(jnp.mean(values * values, axis=1, keepdims=True) + EPS) * scale_gain


def norm_adjoint(values, scale_gain, cotangent):
    inverse = lax.rsqrt(jnp.mean(values * values, axis=1, keepdims=True) + EPS)
    unit = values * inverse
    scaled = cotangent * scale_gain
    back = inverse * (scaled - unit * jnp.mean(scaled * unit, axis=1, keepdims=True))
    return back, jnp.sum(cotangent * unit, axis=0)


def local(
    layer_input,
    out_grad,
    seq_lengths,
    routes,
    route_gates,
    first_gain,
    gate_branch_proj,
    conv_in_proj,
    state_io_proj,
    step_proj,
    conv_kernel,
    conv_offset,
    state_conv_kernel,
    state_conv_offset,
    decay_log,
    step_offset,
    skip_scale,
    mixer_gain,
    out_proj,
    second_gain,
    expert_gate,
    expert_up,
    expert_down,
    shared_gate,
    shared_up,
    shared_down,
):
    rows_n = lax.axis_size("row")
    cols_n = lax.axis_size("col")
    row_index = lax.axis_index("row")
    col_index = lax.axis_index("col")
    micro_count, own_count, width = layer_input.shape
    length = own_count * cols_n
    local_experts, depth, hidden_width = expert_gate.shape
    share = conv_kernel.shape[1]
    heads = decay_log.shape[0]
    size = share // heads
    inner = share * cols_n
    io_width = state_conv_kernel.shape[1]
    shared_width = shared_gate.shape[1]
    per_device = max(1, local_experts // rows_n)
    split = max(1, rows_n // local_experts)
    part_width = hidden_width // split

    def swap(values, k):
        if k == 0:
            return values
        return lax.ppermute(values, "row", [(i, i ^ k) for i in range(rows_n)])

    def peer(k):
        return row_index ^ k

    def unit_of(member):
        return (member * per_device) // split, (member % split) * part_width

    def gather_width(pack):
        full = jnp.zeros((pack.shape[0], width), pack.dtype)
        for k in range(rows_n):
            full = lax.dynamic_update_slice(full, swap(pack, k), (0, peer(k) * depth))
        return full

    def add_shares(full):
        total = None
        for k in range(rows_n):
            part = lax.dynamic_slice(full, (0, peer(k) * depth), (full.shape[0], depth))
            part = swap(part, k).astype(F32)
            total = part if total is None else total + part
        return total

    def after(value, *others):
        return lax.optimization_barrier((value, *others))[0]

    micro = range(micro_count)
    own_rows = [layer_input[m].astype(F32) for m in micro]
    normed = [
        lax.all_gather(row_norm(own_rows[m], first_gain).astype(BF16), "col", axis=0, tiled=True)
        for m in micro
    ]

    own_taps = jnp.concatenate([state_conv_kernel, state_conv_offset[None, :]], axis=0).T
    tap_parts = []
    for _ in range(3):
        tap_parts.append(own_taps.astype(BF16))
        own_taps = own_taps - tap_parts[-1].astype(F32)
    tap_parts = jnp.pad(jnp.concatenate(tap_parts, axis=1), ((0, 0), (0, LANES - 15)))
    step_rows_t = jnp.pad(step_proj.T, ((0, HEAD_ROWS - heads), (0, 0)))
    in_all, io_all, taps_all = gather_weights(
        jnp.concatenate([gate_branch_proj.T, conv_in_proj.T, out_proj, step_rows_t], axis=0),
        state_io_proj.T,
        tap_parts,
        rows_n,
        cols_n,
    )

    def join(parts, first, count):
        return jnp.concatenate(
            [parts[member, first : first + count] for member in range(rows_n)], axis=1
        )

    wb, wc, wo = [join(in_all, at * share, share) for at in range(3)]
    ws = join(in_all, 3 * share, HEAD_ROWS)
    wio = join(io_all, 0, 2 * NS)
    taps_all = taps_all.astype(F32)
    io_taps = jnp.pad(taps_all[:, :5] + taps_all[:, 5:10] + taps_all[:, 10:15], ((0, 0), (0, 3)))
    chan = jnp.concatenate(
        [
            conv_kernel.T,
            conv_offset[:, None],
            mixer_gain[:, None],
            jnp.repeat(skip_scale, size)[:, None],
            jnp.zeros((share, 1), F32),
        ],
        axis=1,
    )
    head_params = jnp.pad(
        jnp.stack([step_offset, jnp.exp(decay_log)], axis=1), ((0, HEAD_ROWS - heads), (0, 6))
    )
    weights = (wb, wc, wio, ws, wo, chan, io_taps, head_params)

    sizes = (per_device, depth, part_width)

    def unit_parts(weight, transposed, moved=False):
        parts = []
        for k in range(rows_n):
            first, hidden_at = unit_of(peer(k))
            if transposed:
                part = lax.dynamic_slice(
                    weight, (first, hidden_at, 0), (per_device, part_width, depth)
                )
                part = jnp.swapaxes(part, 1, 2)
            else:
                part = lax.dynamic_slice(weight, (first, 0, hidden_at), sizes)
            parts.append(swap(after(part, in_all), k) if moved else part)
        return parts

    gates = unit_parts(expert_gate, False)
    ups = unit_parts(expert_up, False)
    downs = unit_parts(expert_down, True, moved=True)

    place_j = lax.broadcasted_iota(jnp.int32, (length, length), 0)
    place_i = lax.broadcasted_iota(jnp.int32, (length, length), 1)
    upper = (place_j <= place_i).astype(BF16)
    expert_ids = col_index * local_experts + jnp.arange(local_experts, dtype=jnp.int32)

    def slots_of(m):
        hit = routes[m].T[None] == expert_ids[:, None, None]
        mask = jnp.any(hit, axis=1)
        gates = jnp.sum(jnp.where(hit, route_gates[m].T[None], 0.0), axis=1)
        rank = dot_plain(mask.astype(BF16), upper).astype(jnp.int32) - 1
        slot = jnp.where(mask, rank, -(2**20))
        firsts = [unit_of(peer(k))[0] for k in range(rows_n)]
        take = lambda rows: jnp.concatenate(
            [lax.dynamic_slice(rows, (first, 0), (per_device, length)) for first in firsts], axis=0
        )
        return take(slot), take(gates)

    def swap_all(parts):
        return [swap(part, k) for k, part in enumerate(parts)]

    own_cots = []
    for m in micro:
        positions = col_index * own_count + jnp.arange(own_count)
        valid = (positions < seq_lengths[m, 0])[:, None]
        own_cots.append(jnp.where(valid, out_grad[m], jnp.zeros_like(out_grad[m])))
    slot_rows = [slots_of(m) for m in micro]
    slot_cols = [(slot.T, gates.T) for slot, gates in slot_rows]

    last = [None]

    def step(function, *args):
        if last[0] is not None:
            args, _ = lax.optimization_barrier((args, last[0]))
        out = function(*args)
        last[0] = jax.tree.leaves(out)[0]
        return out

    state = [{} for _ in micro]

    def mix(m, parts):
        s = state[m]
        (s["y_part"], s["squares"], *s["saved"]), received = step(
            lambda xn, *parts: mixer_forward(parts, xn, *weights, heads), normed[m], *parts[1:]
        )
        return [parts[0], *received]

    def sum_y(m, *others):
        s = state[m]
        s["y"] = lax.psum_scatter(
            after(s["y_part"], *others), "col", scatter_dimension=0, tiled=True
        )

    def scale_of(m):
        s = state[m]
        total = step(lambda squares: lax.psum(jnp.sum(squares, axis=0), "col"), s["squares"])
        s["rms"] = lax.rsqrt(total / inner + EPS)

    def second_norm(m):
        s = state[m]

        def run(y_own, rms):
            y_own = y_own.astype(F32)
            own_rms = lax.dynamic_slice(rms, (col_index * own_count,), (own_count,))
            residual = own_rows[m] + own_rms[:, None] * y_own
            return row_norm(residual, second_gain).astype(BF16), residual, y_own

        second, s["residual"], s["y_own"] = step(run, s["y"], s["rms"])
        s["second"] = lax.all_gather(second, "col", axis=0, tiled=True)
        if m:
            s["cot"] = gather_cot(m, second)

    def gather_cot(m, *others):
        return lax.all_gather(after(own_cots[m], *others), "col", axis=0, tiled=True)

    def exchange(m):
        s = state[m]
        slot, gates_of = slot_rows[m]
        (
            part,
            out_rows,
            s["shared_hidden"],
            s["d_shared_gate"],
            s["d_shared_up"],
            *s["expert_saved"],
        ) = step(
            lambda second, cot, gate_parts, up_parts, down_parts: exchange_rows(
                slot, gates_of, slot_cols[m][0], second, cot, shared_w, gate_parts, up_parts,
                down_parts,
            ),
            s["second"],
            s["cot"],
            gates,
            ups,
            downs,
        )
        s["second_share"] = lax.psum_scatter(part, "col", scatter_dimension=0, tiled=True)
        s["out_rows"] = swap_all([out_rows[k] for k in range(rows_n)])

    def ahead_rows(m):
        s = state[m]
        slot_t, gates_t = slot_cols[m]
        part = step(
            lambda rows, left: combine_rows(slot_t, gates_t, rows, left, shared_out),
            s["out_rows"],
            s["shared_hidden"],
        )
        s["branch_share"] = lax.psum_scatter(part, "col", scatter_dimension=0, tiled=True)

    def second_back(m):
        s = state[m]

        def run(share_in):
            back, gain_grad = norm_adjoint(s["residual"], second_gain, share_in.astype(F32))
            residual_grad = own_cots[m].astype(F32) + back
            low = residual_grad.astype(BF16)
            cross = jnp.sum(low.astype(F32) * s["y_own"], axis=1, keepdims=True)
            parts = [low]
            for _ in range(3):
                parts.append(cross.astype(BF16))
                cross = cross - parts[-1].astype(F32)
            parts.append(jnp.zeros((own_count, LANES - 3), BF16))
            return jnp.concatenate(parts, axis=1), residual_grad, gain_grad

        low, s["residual_grad"], s["second_gain_grad"] = step(run, s["second_share"])
        s["d_res"] = lax.all_gather(low, "col", axis=0, tiled=True)

    def mix_back(m, parts):
        s = state[m]
        scale_rows = jnp.pad(
            jnp.stack([s["rms"], jnp.full((length,), 1.0 / inner, F32)]), ((0, 6), (0, 0))
        )
        (first_part, *s["back"]), received = step(
            lambda d_res, scales, *parts: mixer_backward(
                parts, d_res, scales, normed[m], weights, s["saved"], heads
            ),
            s["d_res"],
            scale_rows,
            *parts[1:],
        )
        s["first_share"] = lax.psum_scatter(first_part, "col", scatter_dimension=0, tiled=True)
        return [parts[0], *received]

    def total_of(parts):
        return jax.tree.map(lambda *terms: functools.reduce(jnp.add, terms), *parts)

    def expert_grads(*saved):
        def over_rows(left, right):
            return jnp.einsum("ecd,ech->edh", left, right, preferred_element_type=F32)

        totals = total_of(
            [
                (over_rows(tokens, d_pre), over_rows(cot, hidden))
                for tokens, cot, hidden, d_pre in saved
            ]
        )
        both, down = totals[0].astype(BF16), totals[1].astype(BF16)
        return [
            [
                lax.dynamic_slice(full, (0, peer(k) * depth, at), (per_device, depth, part_width))
                for k in range(rows_n)
            ]
            for full, at in ((both, 0), (both, part_width), (down, 0))
        ]

    def finish_output(m):
        s = state[m]
        s["output"] = step(
            lambda share_in: (s["residual"] + share_in.astype(F32)).astype(BF16), s["branch_share"]
        )

    def finish_input(m):
        s = state[m]

        def run(share_in):
            back, _ = norm_adjoint(own_rows[m], first_gain, share_in.astype(F32))
            return s["residual_grad"] + back

        s["input_grad"] = step(run, s["first_share"])

    def dense_grads(m):
        s = state[m]
        _, mixed, d_branch, d_conv, d_io, d_step, *_ = s["back"]

        def run(xn, d_res, mixed, d_branch, d_conv, d_io, d_step):
            return (
                dot_plain(d_io, xn),
                dot_plain(d_branch, xn),
                dot_plain(d_conv, xn),
                dot_plain(mixed, d_res)[:, :width],
                dot_plain(d_step, xn),
            )

        s["dense"] = step(run, normed[m], s["d_res"], mixed, d_branch, d_conv, d_io, d_step)

    def shared_grads(m):
        s = state[m]

        def run(second, cot, hidden, d_gate, d_up):
            return dot_first(d_gate, second), dot_first(d_up, second), dot_first(hidden, cot)

        s["shared_grads"] = step(
            run, s["second"], s["cot"], s["shared_hidden"], s["d_shared_gate"], s["d_shared_up"]
        )

    def place_expert_grads(gate_parts, up_parts, down_parts):
        expert_gate_grad = jnp.zeros(expert_gate.shape, F32)
        expert_up_grad = jnp.zeros(expert_up.shape, F32)
        expert_down_grad = jnp.zeros(expert_down.shape, F32)
        for k in range(rows_n):
            first, hidden_at = unit_of(peer(k))
            place = (first, 0, hidden_at)
            expert_gate_grad = lax.dynamic_update_slice(
                expert_gate_grad, gate_parts[k].astype(F32), place
            )
            expert_up_grad = lax.dynamic_update_slice(
                expert_up_grad, up_parts[k].astype(F32), place
            )
            expert_down_grad = lax.dynamic_update_slice(
                expert_down_grad,
                jnp.swapaxes(down_parts[k].astype(F32), 1, 2),
                (first, hidden_at, 0),
            )
        return expert_gate_grad, expert_up_grad, expert_down_grad

    def arrive(parts):
        return step(lambda *values: values, *parts)

    first, second = 0, micro_count - 1
    state[first]["cot"] = gather_cot(first, normed[second])
    gates = mix(first, gates)
    (state[first]["cot"],) = arrive([state[first]["cot"]])
    sum_y(first)
    ups = mix(second, ups)
    scale_of(first)
    second_norm(first)
    sum_y(second)
    downs = arrive(downs)
    shared_full = step(
        lambda *parts: gather_width(jnp.concatenate(parts, axis=0)),
        shared_gate.T,
        shared_up.T,
        shared_down,
    )
    shared_w = (
        shared_full[:shared_width],
        shared_full[shared_width : 2 * shared_width],
        shared_full[2 * shared_width :],
    )
    shared_out = shared_w[2]
    scale_of(second)
    second_norm(second)
    exchange(first)
    exchange(second)
    second_back(first)
    gate_grads, up_grads, down_grads = step(expert_grads, *[s["expert_saved"] for s in state])
    second_back(second)
    ahead_rows(first)
    gate_grads = mix_back(first, gate_grads)
    ahead_rows(second)
    down_grads = swap_all(down_grads)
    shared_grads(first)
    shared_grads(second)
    dense_grads(first)
    finish_output(first)
    up_grads = mix_back(second, up_grads)
    dense_grads(second)
    finish_input(first)
    expert_gate_grad, expert_up_grad, expert_down_grad = step(
        place_expert_grads, gate_grads, up_grads, down_grads
    )
    shared = step(
        lambda *parts: add_shares(jnp.concatenate(parts, axis=0).astype(BF16)),
        *total_of([s["shared_grads"] for s in state])
    )
    shared_in_grad, down_grad = shared[: 2 * shared_width], shared[2 * shared_width :]
    finish_output(second)
    io_sum, *dense = total_of([s["dense"] for s in state])
    io_sum = lax.psum_scatter(io_sum.astype(BF16), "col", scatter_dimension=0, tiled=True)
    dense = add_shares(jnp.concatenate(dense, axis=0).astype(BF16))
    branch_grad, conv_grad = dense[:share], dense[share : 2 * share]
    out_grad_sum, step_grad = dense[2 * share : 3 * share], dense[3 * share :]
    all_sums, row_sums = [], []
    for s in state:
        gain_part, *_, chan_grad, io_grad, head_grad = s["back"]
        all_sums.append(
            (
                jnp.sum(gain_part, axis=0) / first_gain,
                s["second_gain_grad"],
                io_grad[:, :5].reshape(-1),
            )
        )
        row_sums.append(
            (
                chan_grad[:, :6].reshape(-1),
                jnp.sum(chan_grad[:, 6].reshape(heads, size), axis=1),
                head_grad[:heads, 0],
                head_grad[:heads, 1],
            )
        )
    all_total = total_of(all_sums)
    row_total = total_of(row_sums)
    small = jnp.concatenate(all_total + row_total)
    sums = functools.reduce(jnp.add, [swap(small, k) for k in range(rows_n)])
    all_count = sum(part.shape[0] for part in all_total)
    all_values = lax.psum(sums[:all_count], "col")
    io_proj_grad = add_shares(io_sum)
    finish_input(second)
    first_gain_grad = all_values[:width]
    second_gain_grad = all_values[width : 2 * width]
    io_values = lax.dynamic_slice(
        all_values[2 * width :].reshape(2 * NS, 5), (col_index * io_width, 0), (io_width, 5)
    )
    chan_values = sums[all_count : all_count + 6 * share].reshape(share, 6)
    head_values = sums[all_count + 6 * share :]
    return (
        jnp.stack([s["output"] for s in state]),
        jnp.stack([s["input_grad"] for s in state]),
        first_gain_grad,
        branch_grad.T,
        conv_grad.T,
        io_proj_grad.T,
        step_grad[:heads].T,
        chan_values[:, :4].T,
        chan_values[:, 4],
        io_values[:, :4].T,
        io_values[:, 4],
        head_values[heads : 2 * heads],
        head_values[2 * heads :],
        head_values[:heads],
        chan_values[:, 5],
        out_grad_sum,
        second_gain_grad,
        expert_gate_grad,
        expert_up_grad,
        expert_down_grad,
        shared_in_grad[:shared_width].T,
        shared_in_grad[shared_width:].T,
        down_grad,
    )


def solution(mesh):
    both = P(None, ("row", "col"), None)
    placed = (
        both,
        both,
        P(None, "row"),
        P(None, "row", None),
        P(None, "row", None),
        P(),
        P("row", "col"),
        P("row", "col"),
        P("row", "col"),
        P("row", "col"),
        P(None, "col"),
        P("col"),
        P(None, "col"),
        P("col"),
        P("col"),
        P("col"),
        P("col"),
        P("col"),
        P("col", "row"),
        P(),
        P("col", "row", None),
        P("col", "row", None),
        P("col", None, "row"),
        P("row", "col"),
        P("row", "col"),
        P("col", "row"),
    )
    return jax.shard_map(
        local,
        mesh=mesh,
        in_specs=placed,
        out_specs=(both, both, P()) + placed[6:19] + (P(),) + placed[20:],
        check_vma=False,
    )
```

```python
import functools

import jax
import jax.numpy as jnp
from jax import lax
from jax.experimental import pallas as pl
from jax.experimental.pallas import tpu as pltpu
from jax.sharding import PartitionSpec as P

NS = 128
BLOCK = 256
CAP = 144
EPS = 1e-05
HEAD_ROWS = 16
LANES = 128
F32 = jnp.float32
BF16 = jnp.bfloat16
VMEM = pl.BlockSpec(memory_space=pltpu.VMEM)
VMEM_LIMIT = 56 * 1024 * 1024
GROUP = 3
KERNEL_COST = pl.CostEstimate(flops=3 * 10**10, bytes_accessed=2**20, transcendentals=0)
ANY = pl.BlockSpec(memory_space=pl.ANY)
MESH = pl.DeviceIdType.MESH


def contract(left_op, right_op, left_dim, right_dim, precision=None):
    return lax.dot_general(
        left_op,
        right_op,
        (((left_dim,), (right_dim,)), ((), ())),
        preferred_element_type=F32,
        precision=precision,
    )


def dot_plain(left_op, right_op):
    return contract(left_op, right_op, 1, 0)


def dot_first(left_op, right_op):
    return contract(left_op, right_op, 0, 0)


def dot_last(left_op, right_op):
    return contract(left_op, right_op, 1, 1)


def silu_slope(values):
    logistic = jax.nn.sigmoid(values)
    return logistic * (1.0 + values * (1.0 - logistic))


def softplus(values):
    return jnp.maximum(values, 0.0) + jnp.log1p(jnp.exp(-jnp.abs(values)))


def shifts_back(current, before):
    joined = jnp.concatenate([before, current], axis=1)
    return [pltpu.roll(joined, step, 1)[:, LANES:] for step in (1, 2, 3)]


def load_block(ref, rows, block):
    cols = pl.ds(pl.multiple_of(block * BLOCK, BLOCK), BLOCK)
    current = ref[rows, cols]
    ahead = pl.multiple_of(jnp.maximum(block * BLOCK - LANES, 0), LANES)
    before = jnp.where(block > 0, ref[rows, pl.ds(ahead, LANES)], 0.0)
    return current, shifts_back(current, before)


def convolved(current, back, taps):
    return (
        taps[:, 4:5]
        + taps[:, 3:4] * current
        + taps[:, 2:3] * back[0]
        + taps[:, 1:2] * back[1]
        + taps[:, 0:1] * back[2]
    )


def conv_adjoint(adjoint, after, taps):
    joined = jnp.concatenate([adjoint, after], axis=1)
    width = joined.shape[1]
    total = taps[:, 3:4] * adjoint
    for step in (1, 2, 3):
        ahead = pltpu.roll(joined, width - step, 1)[:, :BLOCK]
        total = total + taps[:, 3 - step : 4 - step] * ahead
    return total


def lane_tile(columns):
    rows = columns[0].shape[0]
    lane = lax.broadcasted_iota(jnp.int32, (rows, LANES), 1)
    tile = jnp.zeros((rows, LANES), F32)
    for place, column in enumerate(columns):
        tile = jnp.where(lane == place, column, tile)
    return tile


def row_sum(values):
    return jnp.sum(values, axis=1, keepdims=True)


def decay_block(cum_row, cum_cols, head):
    lane = lax.broadcasted_iota(jnp.int32, cum_cols.shape, 1)
    cum_col = row_sum(jnp.where(lane == head, cum_cols, 0.0))
    place_j = lax.broadcasted_iota(jnp.int32, (BLOCK, BLOCK), 0)
    place_i = lax.broadcasted_iota(jnp.int32, (BLOCK, BLOCK), 1)
    return jnp.exp(jnp.where(place_j <= place_i, cum_row - cum_col, -1e30))


def step_rows(step_pre, head_params, step_s, cum_s, cum_t_s, blocks):
    step = softplus(step_pre + head_params[:, 0:1])
    step_s[...] = step
    log_decay = -(step * head_params[:, 1:2])
    place_j = lax.broadcasted_iota(jnp.int32, (BLOCK, BLOCK), 0)
    place_i = lax.broadcasted_iota(jnp.int32, (BLOCK, BLOCK), 1)
    upper = jnp.where(place_j <= place_i, 1.0, 0.0)
    for block in range(blocks):
        cols = slice(block * BLOCK, (block + 1) * BLOCK)
        cum = contract(log_decay[:, cols], upper, 1, 0, lax.Precision.HIGHEST)
        cum_s[:, cols] = cum
        cum_t_s[cols, :] = jnp.transpose(cum)


def score_blocks(io, scores_s, blocks):
    for block in range(blocks):
        cols = slice(block * BLOCK, (block + 1) * BLOCK)
        scores_s[block] = dot_first(io[:NS, cols], io[NS:, cols])


def block_cols(block):
    return pl.ds(pl.multiple_of(block * BLOCK, BLOCK), BLOCK)


def head_group(heads):
    return GROUP if heads % GROUP == 0 else 1


def greet(peers):
    barrier = pltpu.get_barrier_semaphore()
    for other in peers:
        pl.semaphore_signal(barrier, inc=1, device_id=other, device_id_type=MESH)
    pl.semaphore_wait(barrier, len(peers))


def row_partners(members):
    me = lax.axis_index("row")
    return [{"row": me ^ k} for k in range(1, members)]


def make_send(source, target, send_sem, recv_sem, other):
    return pltpu.make_async_remote_copy(
        src_ref=source,
        dst_ref=target,
        send_sem=send_sem,
        recv_sem=recv_sem,
        device_id=other,
        device_id_type=MESH,
    )


def send(*args):
    copy = make_send(*args)
    copy.start()
    return copy


def unit_of(member, per_device, split, part_width):
    if split == 1:
        return member * per_device, 0
    return (member * per_device) // split, pl.multiple_of((member % split) * part_width, LANES)


def unit_part(weight, member, per_device, split):
    part_width = weight.shape[2] // split
    first, hidden_at = unit_of(member, per_device, split, part_width)
    return weight.at[pl.ds(first, per_device), :, pl.ds(hidden_at, part_width)]


def send_stack(parts, stacked, sems):
    if not parts:
        return []
    me = lax.axis_index("row")
    copies = [pltpu.make_async_copy(parts[0], stacked.at[me], sems.at[0, 0])]
    copies[0].start()
    for k, other in enumerate(row_partners(len(parts)), 1):
        copies.append(send(parts[k], stacked.at[me], sems.at[0, k], sems.at[1, k], other))
    return copies


def mixer_forward_kernel(
    heads,
    cols_n,
    per_device,
    split,
    xn,
    wb,
    wc,
    wio,
    ws,
    wo,
    chan,
    io_taps,
    head_params,
    *refs,
):
    weight, *refs = refs
    count = len(refs) - 18
    y, squares, branch, conv, io_pre, io, step_pre, starts = refs[:8]
    received = refs[8 : 8 + count]
    step_s, cum_s, cum_t_s, scores_s, z_s, sems = refs[8 + count : 14 + count]
    squares_s, own_s, got_s, square_sems = refs[14 + count :]
    at = lax.axis_index("col")
    col_peers = [{"col": at ^ k} for k in range(1, cols_n)]
    row_peers = row_partners(count + 1)
    greet(row_peers + col_peers)
    copies = [
        send(
            unit_part(weight, lax.axis_index("row") ^ (k + 1), per_device, split),
            received[k],
            sems.at[0, k],
            sems.at[1, k],
            other,
        )
        for k, other in enumerate(row_peers)
    ]
    length = xn.shape[0]
    blocks = length // BLOCK
    size = wb.shape[0] // heads
    step_pre[...] = dot_last(ws[...], xn[...])
    step_rows(step_pre[...], head_params[...], step_s, cum_s, cum_t_s, blocks)

    def project(block, carry):
        cols = block_cols(block)
        rows = xn[cols, :]
        io_pre[:, cols] = dot_last(wio[...], rows)
        branch[:, cols] = dot_last(wb[...], rows)
        conv[:, cols] = dot_last(wc[...], rows)
        return carry

    lax.fori_loop(0, blocks, project, 0)

    def io_step(at, carry):
        rows = pl.ds(pl.multiple_of((at // blocks) * 64, 64), 64)
        block = at % blocks
        current, back = load_block(io_pre, rows, block)
        io[rows, block_cols(block)] = jax.nn.silu(
            convolved(current, back, io_taps[rows, :])
        ).astype(BF16)
        return carry

    lax.fori_loop(0, blocks * (2 * NS // 64), io_step, 0)
    score_blocks(io, scores_s, blocks)
    squares_s[...] = jnp.zeros_like(squares_s)

    group = head_group(heads)

    def head_step(first, carry):
        def block_steps(block, states):
            return tuple(
                block_step(first * group + at, block, state) for at, state in enumerate(states)
            )

        def block_step(head, block, state):
            rows = pl.ds(pl.multiple_of(head * size, size), size)
            params = chan[rows, :]
            cols = block_cols(block)
            current, back = load_block(conv, rows, block)
            x = jax.nn.silu(convolved(current, back, params))
            step_row = step_s[pl.ds(head, 1), cols]
            cum_row = cum_s[pl.ds(head, 1), cols]
            last = cum_row[:, BLOCK - 1 : BLOCK]
            mixing = (scores_s[block] * decay_block(cum_row, cum_t_s[cols, :], head)).astype(BF16)
            weighted = x * step_row
            starts[pl.ds(pl.multiple_of((head * blocks + block) * size, size), size), :] = state
            scanned = dot_plain(weighted.astype(BF16), mixing)
            scanned = scanned + dot_plain(state.astype(BF16), io[NS:, cols]) * jnp.exp(cum_row)
            scanned = scanned + params[:, 6:7] * x
            gated = scanned * jax.nn.silu(branch[rows, cols])
            squares_s[:, cols] += jnp.sum((gated * gated).reshape(size // 8, 8, BLOCK), axis=0)
            z_s[rows, cols] = (gated * params[:, 5:6]).astype(BF16)
            to_end = (weighted * jnp.exp(last - cum_row)).astype(BF16)
            return state * jnp.exp(last) + dot_last(to_end, io[:NS, cols])

        lax.fori_loop(0, blocks, block_steps, (jnp.zeros((size, NS), F32),) * group)
        return carry

    lax.fori_loop(0, heads // group, head_step, 0)
    own_s[...] = jnp.sum(squares_s[...], axis=0, keepdims=True)
    square_copies = [
        send(own_s, got_s.at[k], square_sems.at[0, k], square_sems.at[1, k], other)
        for k, other in enumerate(col_peers)
    ]

    def out_step(block, carry):
        cols = block_cols(block)
        y[cols, :] = dot_first(z_s[:, cols], wo[...]).astype(BF16)
        return carry

    lax.fori_loop(0, blocks, out_step, 0)
    for copy in square_copies:
        copy.wait()
    total = own_s[...]
    for k in range(cols_n - 1):
        total = total + got_s[k]
    squares[...] = total
    for copy in copies:
        copy.wait()


def mixer_forward(rows_n, cols_n, unit, weight, xn, wb, wc, wio, ws, wo, chan, io_taps, head_params, heads):
    length, width = xn.shape
    share = wb.shape[0]
    blocks = length // BLOCK
    size = share // heads
    shape = jax.ShapeDtypeStruct
    out = pl.pallas_call(
        functools.partial(mixer_forward_kernel, heads, cols_n, *unit),
        out_shape=(
            shape((length, width), BF16),
            shape((1, length), F32),
            shape((share, length), F32),
            shape((share, length), F32),
            shape((2 * NS, length), F32),
            shape((2 * NS, length), BF16),
            shape((HEAD_ROWS, length), F32),
            shape((heads * blocks * size, NS), F32),
        )
        + (shape((unit[0], weight.shape[1], weight.shape[2] // unit[1]), BF16),) * (rows_n - 1),
        in_specs=[VMEM] * 9 + [ANY],
        out_specs=(VMEM,) * 8 + (ANY,) * (rows_n - 1),
        scratch_shapes=[
            pltpu.VMEM((HEAD_ROWS, length), F32),
            pltpu.VMEM((HEAD_ROWS, length), F32),
            pltpu.VMEM((length, HEAD_ROWS), F32),
            pltpu.VMEM((blocks, BLOCK, BLOCK), F32),
            pltpu.VMEM((share, length), BF16),
            pltpu.SemaphoreType.DMA((2, rows_n - 1)),
            pltpu.VMEM((8, length), F32),
            pltpu.VMEM((1, length), F32),
            pltpu.VMEM((cols_n - 1, 1, length), F32),
            pltpu.SemaphoreType.DMA((2, cols_n - 1)),
        ],
        compiler_params=pltpu.CompilerParams(
            vmem_limit_bytes=VMEM_LIMIT, collective_id=2, has_side_effects=True
        ),
        cost_estimate=KERNEL_COST,
    )(xn, wb, wc, wio, ws, wo, chan, io_taps, head_params, weight)
    return out[:8], out[8:]


def mixer_backward_kernel(
    heads,
    members,
    moved_n,
    d_res,
    scale_rows,
    xn,
    wb,
    wc,
    wio,
    ws,
    wo,
    chan,
    io_taps,
    head_params,
    branch,
    conv,
    io_pre,
    io,
    step_pre,
    starts,
    *refs,
):
    refs = list(refs)
    parts, refs = refs[:members], refs[members:]
    moved, refs = refs[:moved_n], refs[moved_n:]
    first_part, gain_part, mixed, d_branch, d_conv, d_io, d_step = refs[:7]
    chan_grad_t, io_grad_t, head_grad = refs[7:10]
    stacked, arrived, refs = refs[10], refs[11 : 11 + moved_n], refs[11 + moved_n :]
    step_s, cum_s, cum_t_s, scores_s, d_scores_s, d_mixed_s, d_io_s = refs[:7]
    d_cum_s, d_size_s, adjoint_s, cube_s, sems, chan_grad, io_grad = refs[7:14]
    partners = row_partners(members)
    greet(partners)
    copies = [
        send(moved[k], arrived[k], refs[14].at[0, k], refs[14].at[1, k], partners[k])
        for k in range(moved_n)
    ]
    copies += send_stack(parts, stacked, sems)
    length, width = xn.shape
    blocks = length // BLOCK
    size = wb.shape[0] // heads
    step_rows(step_pre[...], head_params[...], step_s, cum_s, cum_t_s, blocks)
    score_blocks(io, scores_s, blocks)
    d_scores_s[...] = jnp.zeros_like(d_scores_s)
    d_io_s[...] = jnp.zeros_like(d_io_s)
    d_cum_s[...] = jnp.zeros_like(d_cum_s)
    d_size_s[...] = jnp.zeros_like(d_size_s)
    chan_grad[...] = jnp.zeros_like(chan_grad)
    io_grad[...] = jnp.zeros_like(io_grad)
    adjoint_s[:, :, length:] = jnp.zeros(adjoint_s.shape[:2] + (LANES,), F32)

    def project(block, carry):
        cols = block_cols(block)
        d_mixed_s[:, cols] = dot_last(wo[...], d_res[cols, :width])
        cross = jnp.transpose(d_res[cols, width:].astype(F32))
        cross = cross[0:1] + cross[1:2] + cross[2:3]
        rms = scale_rows[0:1, cols]
        cube_s[:, cols] = rms * rms * rms * cross * scale_rows[1:2, cols]
        return carry

    lax.fori_loop(0, blocks, project, 0)

    group = head_group(heads)

    def head_step(first, carry):
        def block_steps(reverse, d_states):
            return tuple(
                block_step(first * group + at, at, reverse, d_state)
                for at, d_state in enumerate(d_states)
            )

        def block_step(head, lane_set, reverse, d_state):
            rows = pl.ds(pl.multiple_of(head * size, size), size)
            params = chan[rows, :]
            block = blocks - 1 - reverse
            cols = block_cols(block)
            state = starts[pl.ds(pl.multiple_of((head * blocks + block) * size, size), size), :]
            state_low = state.astype(BF16)
            d_state_low = d_state.astype(BF16)
            write_rows = io[:NS, cols]
            read_rows = io[NS:, cols]
            step_row = step_s[pl.ds(head, 1), cols]
            cum_row = cum_s[pl.ds(head, 1), cols]
            last = cum_row[:, BLOCK - 1 : BLOCK]
            decays = decay_block(cum_row, cum_t_s[cols, :], head)
            mixing = (scores_s[block] * decays).astype(BF16)
            current, back = load_block(conv, rows, block)
            conv_act = convolved(current, back, params)
            logistic = jax.nn.sigmoid(conv_act)
            x = conv_act * logistic
            slope = logistic * (1.0 + conv_act * (1.0 - logistic))
            weighted = x * step_row
            weighted_low = weighted.astype(BF16)
            grown = jnp.exp(cum_row)
            within = dot_plain(weighted_low, mixing)
            carried = dot_plain(state_low, read_rows) * grown
            scanned = within + carried + params[:, 6:7] * x

            inverse_rms = scale_rows[0:1, cols]
            gate_in = branch[rows, cols]
            gate_logistic = jax.nn.sigmoid(gate_in)
            gate_out = gate_in * gate_logistic
            gated = scanned * gate_out
            d_mixed = d_mixed_s[rows, cols]
            gain = params[:, 5:6]
            mixed[rows, cols] = (gated * inverse_rms * gain).astype(BF16)
            d_gated = inverse_rms * (d_mixed * gain) - gated * cube_s[:, cols]
            d_gain = row_sum(d_mixed * gated * inverse_rms)
            d_scanned = d_gated * gate_out
            d_branch[rows, cols] = (
                d_gated * scanned * (gate_logistic * (1.0 + gate_in * (1.0 - gate_logistic)))
            ).astype(BF16)
            d_low = d_scanned.astype(BF16)
            d_skip = row_sum(d_scanned * x)

            d_within = dot_last(d_low, mixing)
            shrunk = jnp.exp(last - cum_row)
            d_fed = dot_plain(d_state_low, write_rows) * shrunk
            d_weighted = d_within + d_fed
            d_scores_s[block] += dot_first(weighted_low, d_low) * decays
            d_grown = (d_scanned * grown).astype(BF16)
            fed = (weighted * shrunk).astype(BF16)
            d_io_s[NS:, cols] += dot_first(state_low, d_grown)
            d_io_s[:NS, cols] += dot_first(d_state_low, fed)
            d_before = d_state * jnp.exp(last) + dot_last(d_grown, read_rows)

            fed_terms = weighted * d_fed
            d_cum = jnp.sum(
                d_low.astype(F32) * within
                - weighted_low.astype(F32) * d_within
                + d_scanned * carried
                - fed_terms,
                axis=0,
                keepdims=True,
            )
            at_end = jnp.sum(row_sum(fed_terms), axis=0, keepdims=True) + jnp.exp(last) * jnp.sum(
                row_sum(d_state * state), axis=0, keepdims=True
            )
            lane = lax.broadcasted_iota(jnp.int32, (1, BLOCK), 1)
            d_cum_s[pl.ds(head, 1), cols] = d_cum + jnp.where(lane == BLOCK - 1, at_end, 0.0)
            d_size_s[pl.ds(head, 1), cols] = jnp.sum(d_weighted * x, axis=0, keepdims=True)

            d_act = (d_weighted * step_row + params[:, 6:7] * d_scanned) * slope
            adjoint_s[lane_set, :, cols] = d_act
            after = adjoint_s[lane_set, :, pl.ds(pl.multiple_of((block + 1) * BLOCK, BLOCK), LANES)]
            d_conv[rows, cols] = conv_adjoint(d_act, after, params).astype(BF16)
            chan_grad[rows, :] += lane_tile(
                [
                    row_sum(d_act * back[2]),
                    row_sum(d_act * back[1]),
                    row_sum(d_act * back[0]),
                    row_sum(d_act * current),
                    row_sum(d_act),
                    d_gain,
                    d_skip,
                ]
            )
            return d_before

        lax.fori_loop(0, blocks, block_steps, (jnp.zeros((size, NS), F32),) * group)
        return carry

    lax.fori_loop(0, heads // group, head_step, 0)

    def scores_step(block, carry):
        cols = block_cols(block)
        d_scores = d_scores_s[block].astype(BF16)
        d_io_s[NS:, cols] += dot_plain(io[:NS, cols], d_scores)
        d_io_s[:NS, cols] += dot_last(io[NS:, cols], d_scores)
        return carry

    lax.fori_loop(0, blocks, scores_step, 0)

    def io_step(at, carry):
        rows = pl.ds(pl.multiple_of((at // blocks) * 64, 64), 64)
        block = blocks - 1 - at % blocks
        cols = block_cols(block)
        taps = io_taps[rows, :]
        current, back = load_block(io_pre, rows, block)
        d_act = d_io_s[rows, cols] * silu_slope(convolved(current, back, taps))
        adjoint_s[0, :64, cols] = d_act
        after = adjoint_s[0, :64, pl.ds(pl.multiple_of((block + 1) * BLOCK, BLOCK), LANES)]
        d_io[rows, cols] = conv_adjoint(d_act, after, taps).astype(BF16)
        io_grad[rows, :] += lane_tile(
            [
                row_sum(d_act * back[2]),
                row_sum(d_act * back[1]),
                row_sum(d_act * back[0]),
                row_sum(d_act * current),
                row_sum(d_act),
            ]
        )
        return carry

    lax.fori_loop(0, blocks * (2 * NS // 64), io_step, 0)

    place_j = lax.broadcasted_iota(jnp.int32, (BLOCK, BLOCK), 0)
    place_i = lax.broadcasted_iota(jnp.int32, (BLOCK, BLOCK), 1)
    lower = jnp.where(place_j >= place_i, 1.0, 0.0)
    rate = head_params[:, 1:2]
    decay_grad = jnp.zeros((HEAD_ROWS, 1), F32)
    offset_grad = jnp.zeros((HEAD_ROWS, 1), F32)
    for block in range(blocks):
        cols = slice(block * BLOCK, (block + 1) * BLOCK)
        d_log = contract(d_cum_s[:, cols], lower, 1, 0, lax.Precision.HIGHEST)
        decay_grad = decay_grad - row_sum(step_s[:, cols] * rate * d_log)
        d_size = d_size_s[:, cols] - rate * d_log
        d_pre = d_size * jax.nn.sigmoid(step_pre[:, cols] + head_params[:, 0:1])
        offset_grad = offset_grad + row_sum(d_pre)
        d_step[:, cols] = d_pre.astype(BF16)
    skip = jnp.sum(chan_grad[:, 6:7].reshape(heads, size, 1), axis=1)
    skip = jnp.concatenate([skip, jnp.zeros((HEAD_ROWS - heads, 1), F32)], axis=0)
    head_grad[...] = lane_tile([decay_grad, offset_grad, skip])
    gain_part[...] = jnp.zeros_like(gain_part)

    def first_step(block, carry):
        cols = block_cols(block)
        part = (
            dot_first(d_branch[:, cols], wb[...])
            + dot_first(d_conv[:, cols], wc[...])
            + dot_first(d_io[:, cols], wio[...])
            + dot_first(d_step[:, cols], ws[...])
        )
        first_part[cols, :] = part.astype(BF16)
        product = part * xn[cols, :].astype(F32)
        gain_part[...] += jnp.sum(product.reshape(BLOCK // 8, 8, -1), axis=0)
        return carry

    lax.fori_loop(0, blocks, first_step, 0)
    chan_grad_t[...] = jnp.transpose(chan_grad[...])[:8]
    io_grad_t[...] = jnp.transpose(io_grad[...])[:8]
    for copy in copies:
        copy.wait()


def mixer_backward(parts, moved, d_res, scale_rows, xn, weights, saved, heads):
    length, width = xn.shape
    share = weights[0].shape[0]
    blocks = length // BLOCK
    size = share // heads
    shape = jax.ShapeDtypeStruct
    out = pl.pallas_call(
        functools.partial(mixer_backward_kernel, heads, len(parts), len(moved)),
        out_shape=(
            shape((length, width), BF16),
            shape((8, width), F32),
            shape((share, length), BF16),
            shape((share, length), BF16),
            shape((share, length), BF16),
            shape((2 * NS, length), BF16),
            shape((HEAD_ROWS, length), BF16),
            shape((8, share), F32),
            shape((8, 2 * NS), F32),
            shape((HEAD_ROWS, LANES), F32),
        )
        + (shape((len(parts),) + parts[0].shape, BF16),)
        + tuple(shape(rows.shape, BF16) for rows in moved),
        in_specs=[VMEM] * 17 + [ANY] * (len(parts) + len(moved)),
        out_specs=(VMEM,) * 10 + (ANY,) * (1 + len(moved)),
        scratch_shapes=[
            pltpu.VMEM((HEAD_ROWS, length), F32),
            pltpu.VMEM((HEAD_ROWS, length), F32),
            pltpu.VMEM((length, HEAD_ROWS), F32),
            pltpu.VMEM((blocks, BLOCK, BLOCK), F32),
            pltpu.VMEM((blocks, BLOCK, BLOCK), F32),
            pltpu.VMEM((share, length), F32),
            pltpu.VMEM((2 * NS, length), F32),
            pltpu.VMEM((HEAD_ROWS, length), F32),
            pltpu.VMEM((HEAD_ROWS, length), F32),
            pltpu.VMEM((head_group(heads), size, length + LANES), F32),
            pltpu.VMEM((1, length), F32),
            pltpu.SemaphoreType.DMA((2, len(parts))),
            pltpu.VMEM((share, LANES), F32),
            pltpu.VMEM((2 * NS, LANES), F32),
        ]
        + [pltpu.SemaphoreType.DMA((2, len(moved)))] * bool(moved),
        compiler_params=pltpu.CompilerParams(
            vmem_limit_bytes=VMEM_LIMIT,
            collective_id=3 if moved else 8,
            has_side_effects=True,
        ),
        cost_estimate=KERNEL_COST,
    )(d_res, scale_rows, xn, *weights, *saved, *parts, *moved)
    return out[:10], out[10], out[11:]


def place_rows(slot_t, gates_t, placed):
    length, units = slot_t.shape

    def choose(block, carry):
        at = block_cols(block)
        slots = slot_t[at, :]
        for tile in range(units * CAP // LANES):
            low, high = tile * LANES // CAP, (tile * LANES + LANES - 1) // CAP
            lane = lax.broadcasted_iota(jnp.int32, (BLOCK, LANES), 1) + tile * LANES
            total = jnp.zeros((BLOCK, LANES), F32)
            for unit in range(low, high + 1):
                value = 1.0 if gates_t is None else gates_t[at, unit : unit + 1]
                total = jnp.where(lane == slots[:, unit : unit + 1] + unit * CAP, value, total)
            placed[at, tile * LANES : (tile + 1) * LANES] = total.astype(BF16)
        return carry

    lax.fori_loop(0, length // BLOCK, choose, 0)


def combine_kernel(members, with_parts, slot_t, gates_t, extra_left, extra_right, *refs):
    refs = list(refs)
    rows, refs = refs[:members], refs[members:]
    if with_parts:
        parts, out, stacked, chosen_s, rows_s, sems, part_sems = refs[:members], *refs[members:]
        greet(row_partners(members))
        copies = send_stack(parts, stacked, part_sems)
    else:
        out, chosen_s, rows_s, sems = refs
        copies = []
    part = rows_s.shape[0] // members
    loads = []
    for member in range(members):
        loads.append(
            pltpu.make_async_copy(
                rows[member], rows_s.at[pl.ds(member * part, part)], sems.at[member]
            )
        )
        loads[-1].start()
    place_rows(slot_t, gates_t, chosen_s)
    for copy in loads:
        copy.wait()

    def columns(at, carry):
        cols = block_cols(at)
        total = dot_plain(chosen_s[...], rows_s[:, cols])
        total = total + dot_plain(extra_left[...], extra_right[:, cols])
        out[:, cols] = total.astype(BF16)
        return carry

    lax.fori_loop(0, out.shape[1] // BLOCK, columns, 0)
    for copy in copies:
        copy.wait()


def combine_rows(slot_t, gates_t, rows, extra_left, extra_right, parts):
    length, units = slot_t.shape
    members = len(rows)
    width = rows[0].shape[1]
    shape = jax.ShapeDtypeStruct
    out = [shape((length, width), BF16)]
    scratch = [
        pltpu.VMEM((length, units * CAP), BF16),
        pltpu.VMEM((units * CAP, width), BF16),
        pltpu.SemaphoreType.DMA((members,)),
    ]
    params = {}
    if parts:
        out.append(shape((members,) + parts[0].shape, BF16))
        scratch.append(pltpu.SemaphoreType.DMA((2, members)))
        params = {"collective_id": 9, "has_side_effects": True}
    return pl.pallas_call(
        functools.partial(combine_kernel, members, bool(parts)),
        out_shape=tuple(out),
        in_specs=[VMEM] * 4 + [ANY] * (members + len(parts)),
        out_specs=(VMEM,) + (ANY,) * (len(out) - 1),
        scratch_shapes=scratch,
        compiler_params=pltpu.CompilerParams(vmem_limit_bytes=VMEM_LIMIT, **params),
        cost_estimate=KERNEL_COST,
    )(slot_t, gates_t, extra_left, extra_right, *rows, *parts)


def spread_start(
    members, weighted, slot, gates, source, received, outgoing, chosen_s, gate_s, row_sems, own_sems
):
    units, length = slot.shape
    width = source.shape[1]
    experts = units // members
    rows = experts * CAP
    partners = row_partners(members)

    def choose(unit, carry):
        at = pl.ds(pl.multiple_of(unit * CAP, CAP), CAP)
        place = lax.broadcasted_iota(jnp.int32, (CAP, length), 0)
        hit = place == slot[pl.ds(unit, 1), :]
        chosen_s[at, :] = jnp.where(hit, 1.0, 0.0).astype(BF16)
        if weighted:
            gate_s[at, :] = row_sum(jnp.where(hit, gates[pl.ds(unit, 1), :], 0.0))
        return carry

    lax.fori_loop(0, units, choose, 0)

    def pairs(part):
        out = []
        for expert in range(experts):
            for k, other in enumerate(partners):
                out.append(
                    make_send(
                        outgoing.at[pl.ds((k + 1) * rows + expert * CAP, CAP), part],
                        received.at[expert, pl.ds((k + 1) * CAP, CAP), part],
                        row_sems.at[0, k, expert],
                        row_sems.at[1, k, expert],
                        other,
                    )
                )
            out.append(
                pltpu.make_async_copy(
                    outgoing.at[pl.ds(expert * CAP, CAP), part],
                    received.at[expert, pl.ds(0, CAP), part],
                    own_sems.at[expert],
                )
            )
        return out

    def columns(at, carry):
        cols = block_cols(at)
        picked = dot_plain(chosen_s[...], source[:, cols])
        if weighted:
            picked = picked * gate_s[...]
        outgoing[:, cols] = picked.astype(BF16)
        for copy in pairs(cols):
            copy.start()
        return carry

    lax.fori_loop(0, width // BLOCK, columns, 0)
    return pairs(pl.ds(0, width))


def spread_kernel(members, weighted, before_n, slot, gates, source, *refs):
    if weighted:
        received, refs = refs[0], refs[1:]
    else:
        cot, gate_sh, up_sh, down_sh = refs[:4]
        before, refs = refs[4 : 4 + before_n], refs[4 + before_n :]
        received, hidden_sh, d_gate_sh, d_up_sh = refs[:4]
        grads, refs = refs[4:7], refs[7:]
    outgoing, chosen_s, gate_s, row_sems, own_sems = refs
    length, width = source.shape
    partners = row_partners(members)
    greet(partners)
    copies = spread_start(
        members, weighted, slot, gates, source, received, outgoing, chosen_s, gate_s, row_sems, own_sems
    )

    if not weighted:

        def shared_step(at, carry):
            at = block_cols(at)
            gate_pre = dot_last(source[at, :], gate_sh[...])
            up_pre = dot_last(source[at, :], up_sh[...])
            d_hidden = dot_last(cot[at, :], down_sh[...])
            logistic = jax.nn.sigmoid(gate_pre)
            active = gate_pre * logistic
            hidden_sh[at, :] = (active * up_pre).astype(BF16)
            slope = logistic * (1.0 + gate_pre * (1.0 - logistic))
            d_gate_sh[at, :] = (d_hidden * up_pre * slope).astype(BF16)
            d_up_sh[at, :] = (d_hidden * active).astype(BF16)
            return carry

        lax.fori_loop(0, length // BLOCK, shared_step, 0)

        def grad_step(at, carry):
            cols = block_cols(at)
            for at, (rows, right) in enumerate(
                ((source, d_gate_sh), (source, d_up_sh), (cot, hidden_sh))
            ):
                value = dot_first(rows[:, cols], right[...])
                if before:
                    value = value + before[at][cols, :]
                grads[at][cols, :] = value.astype(grads[at].dtype)
            return carry

        lax.fori_loop(0, width // BLOCK, grad_step, 0)
    for copy in copies:
        copy.wait()


def spread_scratch(members, units, length, width):
    experts = units // members
    return [
        pltpu.VMEM((units * CAP, width), BF16),
        pltpu.VMEM((units * CAP, length), BF16),
        pltpu.VMEM((units * CAP, 1), F32),
        pltpu.SemaphoreType.DMA((2, members - 1, experts)),
        pltpu.SemaphoreType.DMA((experts,)),
    ]


def spread_rows(members, slot, gates, source, cot=None, shared_w=(), before=(), grad_type=F32):
    units, length = slot.shape
    width = source.shape[1]
    experts = units // members
    weighted = cot is None
    shape = jax.ShapeDtypeStruct
    out = [shape((experts, members * CAP, width), BF16)]
    out += [shape((length, weight.shape[0]), BF16) for weight in shared_w]
    out += [shape(weight.shape[::-1], grad_type) for weight in shared_w]
    extra = () if weighted else (cot, *shared_w, *before)
    return pl.pallas_call(
        functools.partial(spread_kernel, members, weighted, len(before)),
        out_shape=tuple(out),
        in_specs=[VMEM] * (3 + len(extra)),
        out_specs=(ANY,) + (VMEM,) * (2 * len(shared_w)),
        scratch_shapes=spread_scratch(members, units, length, width),
        compiler_params=pltpu.CompilerParams(
            vmem_limit_bytes=VMEM_LIMIT,
            collective_id=4 if weighted else 11 if before else 5,
            has_side_effects=True,
        ),
        cost_estimate=KERNEL_COST,
    )(slot, gates, source, *extra)


def expert_kernel(
    members, split, following, slot_t, token_s, cot_s, d_gate_sh, d_up_sh, gate_sh, up_sh, *refs
):
    refs = list(refs)
    if following:
        slot, gates, source = refs[:3]
        received, picked_s, chosen_s, gate_s, spread_sems, own_sems = refs[-6:]
        refs = refs[3:-6]
    else:
        grads, grad_outs, grad_got, grad_sems = refs[:3], refs[-7:-4], refs[-4:-1], refs[-1]
        refs = refs[3:-7]
    shards = [refs[at * members : (at + 1) * members] for at in range(3)]
    part, out_rows, hidden_s, d_pre_s, outgoing, back_s, weights, places_s, row_sems, weight_sems = (
        refs[3 * members :]
    )
    experts, _, width = token_s.shape
    rows = experts * CAP
    hidden_width = weights.shape[3]
    depth = width // members
    chunk = min(BLOCK, hidden_width)
    me = lax.axis_index("row")
    partners = row_partners(members)
    weight_copies = []
    for which in range(3):
        for member in range(members):
            place = pl.ds(pl.multiple_of((me ^ member) * depth, depth), depth)
            shard = shards[which][member]
            if member == 0 and which < 2:
                shard = unit_part(shard, me, experts, split)
            weight_copies.append(
                pltpu.make_async_copy(
                    shard,
                    weights.at[which, :, place],
                    weight_sems.at[which, member],
                )
            )
            weight_copies[-1].start()
    greet(partners)
    spread = []
    if following:
        spread = spread_start(
            members,
            True,
            slot,
            gates,
            source,
            received,
            picked_s,
            chosen_s,
            gate_s,
            spread_sems,
            own_sems,
        )
    grad_copies = []
    if not following:
        for which in range(3):
            for k, other in enumerate(partners):
                place = pl.ds(pl.multiple_of((me ^ (k + 1)) * depth, depth), depth)
                grad_copies.append(
                    send(
                        grads[which].at[place],
                        grad_got[which].at[k],
                        grad_sems.at[0, which, k],
                        grad_sems.at[1, which, k],
                        other,
                    )
                )
    for copy in weight_copies:
        copy.wait()
    copies = []
    for expert in range(experts):

        def hidden_step(at, carry):
            cols = pl.ds(pl.multiple_of(at * chunk, chunk), chunk)
            up_cols = pl.ds(pl.multiple_of(hidden_width + at * chunk, chunk), chunk)
            gate_pre = dot_plain(token_s[expert], weights[0, expert, :, cols])
            up_pre = dot_plain(token_s[expert], weights[1, expert, :, cols])
            d_hidden = dot_plain(cot_s[expert], weights[2, expert, :, cols])
            logistic = jax.nn.sigmoid(gate_pre)
            active = gate_pre * logistic
            hidden_s[expert, :, cols] = (active * up_pre).astype(BF16)
            slope = logistic * (1.0 + gate_pre * (1.0 - logistic))
            d_pre_s[expert, :, cols] = (d_hidden * up_pre * slope).astype(BF16)
            d_pre_s[expert, :, up_cols] = (d_hidden * active).astype(BF16)
            return carry

        lax.fori_loop(0, hidden_width // chunk, hidden_step, 0)

        def back_step(at, carry):
            cols = block_cols(at)
            back = dot_last(d_pre_s[expert, :, :hidden_width], weights[0, expert, cols, :])
            back = back + dot_last(d_pre_s[expert, :, hidden_width:], weights[1, expert, cols, :])
            back = back.astype(BF16)
            back_s[expert * CAP : (expert + 1) * CAP, cols] = back[:CAP]
            for k in range(members - 1):
                outgoing[k * rows + expert * CAP : k * rows + (expert + 1) * CAP, cols] = back[
                    (k + 1) * CAP : (k + 2) * CAP
                ]
            for copy in returns(cols):
                copy.start()
            return carry

        def returns(cols, expert=expert):
            return [
                make_send(
                    outgoing.at[pl.ds(k * rows + expert * CAP, CAP), cols],
                    back_s.at[pl.ds((k + 1) * rows + expert * CAP, CAP), cols],
                    row_sems.at[0, k, expert],
                    row_sems.at[1, k, expert],
                    other,
                )
                for k, other in enumerate(partners)
            ]

        lax.fori_loop(0, width // BLOCK, back_step, 0)
        copies += returns(pl.ds(0, width))

    for expert in range(experts):

        def ahead_step(at, carry):
            cols = block_cols(at)
            ahead = dot_last(hidden_s[expert], weights[2, expert, cols, :]).astype(BF16)
            for member in range(members):
                out_rows[member][expert * CAP : (expert + 1) * CAP, cols] = ahead[
                    member * CAP : (member + 1) * CAP
                ]
            return carry

        lax.fori_loop(0, width // BLOCK, ahead_step, 0)

    place_rows(slot_t, None, places_s)
    for copy in copies:
        copy.wait()

    def columns(at, carry):
        cols = block_cols(at)
        total = dot_plain(places_s[...], back_s[:, cols])
        total = total + dot_plain(d_gate_sh[...], gate_sh[:, cols])
        total = total + dot_plain(d_up_sh[...], up_sh[:, cols])
        part[:, cols] = total.astype(BF16)
        return carry

    lax.fori_loop(0, width // BLOCK, columns, 0)
    for copy in spread + grad_copies:
        copy.wait()
    if not following:
        own = pl.ds(pl.multiple_of(me * depth, depth), depth)
        for which in range(3):
            value = grads[which][own, :].astype(F32)
            for k in range(members - 1):
                value = value + grad_got[which][k].astype(F32)
            grad_outs[which][...] = value


def expert_rows(
    following, grads, slot_t, tokens, cots, d_gate_sh, d_up_sh, shared_w, gate_parts, up_parts, down_parts
):
    members = len(gate_parts)
    length, units = slot_t.shape
    experts, stacked, width = tokens.shape
    rows = experts * CAP
    hidden_width = gate_parts[1].shape[2]
    split = gate_parts[0].shape[2] // hidden_width
    shape = jax.ShapeDtypeStruct
    extra = 3
    firsts = 7 + extra + 3 * members
    outs_n = 3 + members + (1 if following else 3)
    depth = width // members

    def kernel(*refs):
        ins, outs, scratch = refs[:firsts], refs[firsts : firsts + outs_n], refs[firsts + outs_n :]
        more = outs[3 + members :]
        outs, tail, scratch = outs[: 3 + members], (*more, *scratch[6:]), scratch[:6]
        expert_kernel(
            members, split, bool(following), *ins, outs[0], outs[1 : 1 + members], *outs[1 + members :],
            *scratch, *tail,
        )

    out_shape = [shape((length, width), BF16)] + [shape((rows, width), BF16)] * members
    out_shape += [
        shape((experts, stacked, hidden_width), BF16),
        shape((experts, stacked, 2 * hidden_width), BF16),
    ]
    out_specs = [VMEM] * (3 + members)
    scratch = [
        pltpu.VMEM(((members - 1) * rows, width), BF16),
        pltpu.VMEM((members * rows, width), BF16),
        pltpu.VMEM((3, experts, width, hidden_width), BF16),
        pltpu.VMEM((length, units * CAP), BF16),
        pltpu.SemaphoreType.DMA((2, members - 1, experts)),
        pltpu.SemaphoreType.DMA((3, members)),
    ]
    if following:
        out_shape.append(shape((experts, stacked, width), BF16))
        out_specs.append(ANY)
        scratch += spread_scratch(members, units, length, width)
    else:
        for grad in grads:
            out_shape.append(shape((depth, grad.shape[1]), F32))
            out_specs.append(VMEM)
            scratch.append(pltpu.VMEM((members - 1, depth, grad.shape[1]), BF16))
        scratch.append(pltpu.SemaphoreType.DMA((2, 3, members - 1)))
    out = pl.pallas_call(
        kernel,
        out_shape=tuple(out_shape),
        in_specs=[VMEM] * (7 + extra) + [ANY] * (3 * members),
        out_specs=tuple(out_specs),
        scratch_shapes=scratch,
        compiler_params=pltpu.CompilerParams(
            vmem_limit_bytes=VMEM_LIMIT,
            collective_id=6 if following else 10,
            has_side_effects=True,
        ),
        cost_estimate=KERNEL_COST,
    )(
        slot_t,
        tokens,
        cots,
        d_gate_sh,
        d_up_sh,
        *shared_w[:2],
        *(following or grads),
        *gate_parts,
        *up_parts,
        *down_parts,
    )
    return out[0], out[1 : 1 + members], out[1 + members : 3 + members], out[3 + members :]


def tail_kernel(rows_n, cols_n, micro_n, first_gain, *refs):
    refs = list(refs)
    sets = [refs[at * 12 : (at + 1) * 12] for at in range(micro_n)]
    refs = refs[micro_n * 12 :]
    outs, small_outs, refs = refs[:5], refs[5:9], refs[9:]
    totals, got, refs = refs[:4], refs[4:9], refs[9:]
    io_s, io_got, io_t_s, small_s, small_got, few_got, row_sems, col_sems = (
        refs[0], refs[1], refs[2], refs[3:7], refs[7:11], refs[11:13], refs[13], refs[14]
    )
    me, at = lax.axis_index("row"), lax.axis_index("col")
    width = sets[0][0].shape[1]
    depth = width // rows_n
    io_rows = io_got.shape[1]
    row_peers = row_partners(rows_n)
    col_peers = [{"col": at ^ k} for k in range(1, cols_n)]
    greet(row_peers + col_peers)
    row_copies, small_copies = [], []

    def to_row(which, k, source, target, other):
        return send(source, target, row_sems.at[0, which, k], row_sems.at[1, which, k], other)

    def to_col(which, k, source, target, other):
        return send(source, target, col_sems.at[0, which, k], col_sems.at[1, which, k], other)

    def total_of(place):
        return functools.reduce(jnp.add, [one[place][...] for one in sets])

    gain = jnp.sum(total_of(7), axis=0, keepdims=True) / first_gain[...]
    small_s[0][...] = jnp.concatenate([gain, total_of(8)], axis=0)
    for which, place in ((1, 10), (2, 9), (3, 11)):
        small_s[which][...] = total_of(place)
    for which in range(4):
        for k, other in enumerate(row_peers):
            small_copies.append(
                to_row(which, k, small_s[which], small_got[which].at[k], other)
            )

    def io_step(block, carry):
        cols = block_cols(block)
        io_s[:, cols] = functools.reduce(
            jnp.add, [dot_plain(one[6][...], one[0][:, cols]) for one in sets]
        ).astype(BF16)
        return carry

    lax.fori_loop(0, width // BLOCK, io_step, 0)
    io_copies = []
    for k, other in enumerate(col_peers):
        place = pl.ds(pl.multiple_of((at ^ (k + 1)) * io_rows, io_rows), io_rows)
        io_copies.append(to_col(0, k, io_s.at[place], io_got.at[k], other))
    def grads_at(cols):
        rows_t = [jnp.transpose(one[0][:, cols]) for one in sets]
        d_res_t = [jnp.transpose(one[1][:, cols]) for one in sets]
        for which, left in enumerate((2, 3, 4, 5)):
            right_t = d_res_t if left == 4 else rows_t
            totals[which][cols, :] = functools.reduce(
                jnp.add, [dot_last(right, one[left][...]) for right, one in zip(right_t, sets)]
            ).astype(BF16)

    def send_grads(k):
        place = pl.ds(pl.multiple_of((me ^ k) * depth, depth), depth)
        for which in range(4):
            row_copies.append(
                to_row(
                    4 + which, k - 1, totals[which].at[place], got[which].at[k - 1], row_peers[k - 1]
                )
            )

    if depth % LANES == 0:
        for k in [*range(1, rows_n), 0]:
            grads_at(pl.ds(pl.multiple_of((me ^ k) * depth, depth), depth))
            if k:
                send_grads(k)
    else:

        def grad_step(block, carry):
            grads_at(block_cols(block))
            return carry

        lax.fori_loop(0, width // BLOCK, grad_step, 0)
        for k in range(1, rows_n):
            send_grads(k)
    for copy in small_copies:
        copy.wait()
    for which in range(4):
        value = small_s[which][...]
        for k in range(rows_n - 1):
            value = value + small_got[which][k]
        small_s[which][...] = value
    few_copies = [
        to_col(1 + which, k, small_s[which], few_got[which].at[k], other)
        for which in range(2)
        for k, other in enumerate(col_peers)
    ]
    for copy in io_copies:
        copy.wait()
    io_total = io_s[pl.ds(pl.multiple_of(at * io_rows, io_rows), io_rows), :].astype(F32)
    for k in range(cols_n - 1):
        io_total = io_total + io_got[k].astype(F32)
    io_t_s[...] = jnp.transpose(io_total).astype(BF16)
    for k, other in enumerate(row_peers):
        place = pl.ds(pl.multiple_of((me ^ (k + 1)) * depth, depth), depth)
        row_copies.append(to_row(8, k, io_t_s.at[place], got[4].at[k], other))
    for copy in few_copies:
        copy.wait()
    for which in range(4):
        value = small_s[which][...]
        if which < 2:
            for k in range(cols_n - 1):
                value = value + few_got[which][k]
        small_outs[which][...] = value
    own = pl.ds(pl.multiple_of(me * depth, depth), depth)
    for copy in row_copies:
        copy.wait()
    for which, total in enumerate([*totals, io_t_s]):
        value = total[own, :].astype(F32)
        for k in range(rows_n - 1):
            value = value + got[which][k].astype(F32)
        outs[which][...] = value


def tail_sums(rows_n, cols_n, first_gain, sets):
    width = sets[0][0].shape[1]
    depth = width // rows_n
    io_full = sets[0][6].shape[0]
    io_rows = io_full // cols_n
    shares = [left.shape[0] for left in sets[0][2:6]]
    shape = jax.ShapeDtypeStruct
    vmem = lambda *dims: pltpu.VMEM(dims, BF16)
    small = [(2, width), sets[0][10].shape, sets[0][9].shape, sets[0][11].shape]
    small_f32 = lambda lead, dims: pltpu.VMEM(lead + dims, F32)
    return pl.pallas_call(
        functools.partial(tail_kernel, rows_n, cols_n, len(sets)),
        out_shape=tuple(shape((depth, share), F32) for share in shares + [io_rows])
        + tuple(shape(dims, F32) for dims in small),
        in_specs=[VMEM] * (1 + 12 * len(sets)),
        out_specs=(VMEM,) * 9,
        scratch_shapes=[vmem(width, share) for share in shares]
        + [vmem(rows_n - 1, depth, share) for share in shares + [io_rows]]
        + [vmem(io_full, width), vmem(cols_n - 1, io_rows, width), vmem(width, io_rows)]
        + [small_f32((), dims) for dims in small]
        + [small_f32((rows_n - 1,), dims) for dims in small]
        + [small_f32((cols_n - 1,), dims) for dims in small[:2]]
        + [
            pltpu.SemaphoreType.DMA((2, 9, rows_n - 1)),
            pltpu.SemaphoreType.DMA((2, 3, cols_n - 1)),
        ],
        compiler_params=pltpu.CompilerParams(
            vmem_limit_bytes=VMEM_LIMIT, collective_id=7, has_side_effects=True
        ),
        cost_estimate=KERNEL_COST,
    )(first_gain, *[ref for one in sets for ref in one])


def gather_kernel(
    rows_n,
    cols_n,
    pack,
    io,
    taps,
    first,
    pack_all,
    io_all,
    taps_all,
    first_all,
    row_sems,
    io_sems,
    tap_sems,
    own_sems,
    first_sems,
):
    me, at = lax.axis_index("row"), lax.axis_index("col")
    io_rows = io.shape[0]
    place = pl.ds(pl.multiple_of(at * io_rows, io_rows), io_rows)
    row_peers = [{"row": me ^ k} for k in range(1, rows_n)]
    col_peers = [{"col": at ^ k} for k in range(1, cols_n)]
    barrier = pltpu.get_barrier_semaphore()
    for other in row_peers + col_peers:
        pl.semaphore_signal(barrier, inc=1, device_id=other, device_id_type=MESH)
    pl.semaphore_wait(barrier, rows_n + cols_n - 2)

    def send_one(source, target, sems, k, other):
        return send(source, target, sems.at[0, k], sems.at[1, k], other)

    own = [
        pltpu.make_async_copy(pack, pack_all.at[me], own_sems.at[0]),
        pltpu.make_async_copy(io, io_all.at[me, place], own_sems.at[1]),
        pltpu.make_async_copy(taps, taps_all.at[place], own_sems.at[2]),
        pltpu.make_async_copy(first, first_all.at[at], own_sems.at[3]),
    ]
    for copy in own:
        copy.start()

    def send_first(which, k, source, owner, other):
        return make_send(
            source,
            first_all.at[owner],
            first_sems.at[0, which, k],
            first_sems.at[1, which, k],
            other,
        )

    far = [
        send_first(0, k, first, at, {"col": at ^ (2 * k)}) for k in range(1, cols_n // 2)
    ]
    near = [send_first(1, 0, first, at, {"col": at ^ 1})]
    for copy in far + near:
        copy.start()
    io_copies = [
        send_one(io, io_all.at[me, place], io_sems, k, other) for k, other in enumerate(col_peers)
    ]
    copies = [
        send_one(taps, taps_all.at[place], tap_sems, k, other)
        for k, other in enumerate(col_peers)
    ]
    copies += [
        send_one(pack, pack_all.at[me], row_sems, k, other) for k, other in enumerate(row_peers)
    ]
    own[1].wait()
    for copy in io_copies:
        copy.wait()
    copies += [
        send_one(io_all.at[me], io_all.at[me], row_sems, rows_n - 1 + k, other)
        for k, other in enumerate(row_peers)
    ]
    for k, copy in enumerate(far, 1):
        copy.wait()
        owner = at ^ (2 * k)
        near.append(send_first(1, k, first_all.at[owner], owner, {"col": at ^ 1}))
        near[-1].start()
    own[0].wait()
    own[2].wait()
    own[3].wait()
    for copy in near + copies:
        copy.wait()


def gather_weights(pack, io, taps, first, rows_n, cols_n):
    shape = jax.ShapeDtypeStruct
    return pl.pallas_call(
        functools.partial(gather_kernel, rows_n, cols_n),
        out_shape=(
            shape((rows_n,) + pack.shape, BF16),
            shape((rows_n, cols_n * io.shape[0], io.shape[1]), BF16),
            shape((cols_n * io.shape[0], taps.shape[1]), BF16),
            shape((cols_n,) + first.shape, BF16),
        ),
        in_specs=[ANY] * 4,
        out_specs=(ANY,) * 4,
        scratch_shapes=[
            pltpu.SemaphoreType.DMA((2, 2 * (rows_n - 1))),
            pltpu.SemaphoreType.DMA((2, cols_n - 1)),
            pltpu.SemaphoreType.DMA((2, cols_n - 1)),
            pltpu.SemaphoreType.DMA((4,)),
            pltpu.SemaphoreType.DMA((2, 2, cols_n // 2)),
        ],
        compiler_params=pltpu.CompilerParams(collective_id=1, has_side_effects=True),
        cost_estimate=pl.CostEstimate(flops=1, bytes_accessed=1, transcendentals=0),
    )(pack, io, taps, first)


def row_norm(values, scale_gain):
    return values * lax.rsqrt(jnp.mean(values * values, axis=1, keepdims=True) + EPS) * scale_gain


def norm_adjoint(values, scale_gain, cotangent):
    inverse = lax.rsqrt(jnp.mean(values * values, axis=1, keepdims=True) + EPS)
    unit = values * inverse
    scaled = cotangent * scale_gain
    back = inverse * (scaled - unit * jnp.mean(scaled * unit, axis=1, keepdims=True))
    return back, jnp.sum(cotangent * unit, axis=0, keepdims=True)


def local(
    layer_input,
    out_grad,
    seq_lengths,
    routes,
    route_gates,
    first_gain,
    gate_branch_proj,
    conv_in_proj,
    state_io_proj,
    step_proj,
    conv_kernel,
    conv_offset,
    state_conv_kernel,
    state_conv_offset,
    decay_log,
    step_offset,
    skip_scale,
    mixer_gain,
    out_proj,
    second_gain,
    expert_gate,
    expert_up,
    expert_down,
    shared_gate,
    shared_up,
    shared_down,
):
    rows_n = lax.axis_size("row")
    cols_n = lax.axis_size("col")
    row_index = lax.axis_index("row")
    col_index = lax.axis_index("col")
    micro_count, own_count, width = layer_input.shape
    length = own_count * cols_n
    local_experts, depth, hidden_width = expert_gate.shape
    share = conv_kernel.shape[1]
    heads = decay_log.shape[0]
    size = share // heads
    inner = share * cols_n
    io_width = state_conv_kernel.shape[1]
    shared_width = shared_gate.shape[1]
    per_device = max(1, local_experts // rows_n)
    split = max(1, rows_n // local_experts)
    part_width = hidden_width // split

    def swap(values, k):
        if k == 0:
            return values
        return lax.ppermute(values, "row", [(i, i ^ k) for i in range(rows_n)])

    def peer(k):
        return row_index ^ k

    def unit_at(member):
        return (member * per_device) // split, (member % split) * part_width

    def gather_width(pack):
        full = jnp.zeros((pack.shape[0], width), pack.dtype)
        for k in range(rows_n):
            full = lax.dynamic_update_slice(full, swap(pack, k), (0, peer(k) * depth))
        return full

    def after(value, *others):
        return lax.optimization_barrier((value, *others))[0]

    micro = range(micro_count)
    own_rows = [layer_input[m].astype(F32) for m in micro]
    first_rows = [row_norm(own_rows[m], first_gain).astype(BF16) for m in micro]

    own_taps = jnp.concatenate([state_conv_kernel, state_conv_offset[None, :]], axis=0).T
    tap_parts = []
    for _ in range(3):
        tap_parts.append(own_taps.astype(BF16))
        own_taps = own_taps - tap_parts[-1].astype(F32)
    tap_parts = jnp.pad(jnp.concatenate(tap_parts, axis=1), ((0, 0), (0, LANES - 15)))
    step_rows_t = jnp.pad(step_proj.T, ((0, HEAD_ROWS - heads), (0, 0)))
    in_all, io_all, taps_all, first_all = gather_weights(
        jnp.concatenate([gate_branch_proj.T, conv_in_proj.T, out_proj, step_rows_t], axis=0),
        state_io_proj.T,
        tap_parts,
        first_rows[0],
        rows_n,
        cols_n,
    )

    normed = [first_all.reshape(length, width)] + [
        lax.all_gather(after(rows, in_all), "col", axis=0, tiled=True) for rows in first_rows[1:]
    ]

    def join(parts, first, count):
        return jnp.concatenate(
            [parts[member, first : first + count] for member in range(rows_n)], axis=1
        )

    wb, wc, wo = [join(in_all, at * share, share) for at in range(3)]
    ws = join(in_all, 3 * share, HEAD_ROWS)
    wio = join(io_all, 0, 2 * NS)
    taps_all = taps_all.astype(F32)
    io_taps = jnp.pad(taps_all[:, :5] + taps_all[:, 5:10] + taps_all[:, 10:15], ((0, 0), (0, 3)))
    chan = jnp.concatenate(
        [
            conv_kernel.T,
            conv_offset[:, None],
            mixer_gain[:, None],
            jnp.repeat(skip_scale, size)[:, None],
            jnp.zeros((share, 1), F32),
        ],
        axis=1,
    )
    head_params = jnp.pad(
        jnp.stack([step_offset, jnp.exp(decay_log)], axis=1), ((0, HEAD_ROWS - heads), (0, 6))
    )
    weights = (wb, wc, wio, ws, wo, chan, io_taps, head_params)

    downs = []
    for k in range(rows_n):
        first, hidden_at = unit_at(peer(k))
        part = lax.dynamic_slice(
            expert_down, (first, hidden_at, 0), (per_device, part_width, depth)
        )
        downs.append(swap(after(jnp.swapaxes(part, 1, 2), in_all), k))

    place_j = lax.broadcasted_iota(jnp.int32, (length, length), 0)
    place_i = lax.broadcasted_iota(jnp.int32, (length, length), 1)
    upper = (place_j <= place_i).astype(BF16)
    expert_ids = col_index * local_experts + jnp.arange(local_experts, dtype=jnp.int32)

    def slots_of(m):
        hit = routes[m].T[None] == expert_ids[:, None, None]
        mask = jnp.any(hit, axis=1)
        gates = jnp.sum(jnp.where(hit, route_gates[m].T[None], 0.0), axis=1)
        rank = dot_plain(mask.astype(BF16), upper).astype(jnp.int32) - 1
        slot = jnp.where(mask, rank, -(2**20))
        firsts = [unit_at(peer(k))[0] for k in range(rows_n)]
        take = lambda rows: jnp.concatenate(
            [lax.dynamic_slice(rows, (first, 0), (per_device, length)) for first in firsts], axis=0
        )
        return take(slot), take(gates)

    def swap_all(parts):
        return [swap(part, k) for k, part in enumerate(parts)]

    own_cots = []
    for m in micro:
        positions = col_index * own_count + jnp.arange(own_count)
        valid = (positions < seq_lengths[m, 0])[:, None]
        own_cots.append(jnp.where(valid, out_grad[m], jnp.zeros_like(out_grad[m])))
    slot_rows = [slots_of(m) for m in micro]
    slot_cols = [(slot.T, gates.T) for slot, gates in slot_rows]

    last = [None]

    def step(function, *args):
        if last[0] is not None:
            args, _ = lax.optimization_barrier((args, last[0]))
        out = function(*args)
        last[0] = jax.tree.leaves(out)[0]
        return out

    state = [{} for _ in micro]

    def mix(m, weight):
        s = state[m]
        (s["y_part"], s["squares"], *s["saved"]), received = step(
            lambda xn: mixer_forward(
                rows_n, cols_n, (per_device, split), weight, xn, *weights, heads
            ),
            normed[m],
        )
        return [weight, *received]

    def sum_y(m, *others):
        s = state[m]
        s["y"] = lax.psum_scatter(
            after(s["y_part"], *others), "col", scatter_dimension=0, tiled=True
        )

    def scale_of(m):
        s = state[m]
        s["rms"] = lax.rsqrt(s["squares"][0] / inner + EPS)

    def second_norm(m):
        s = state[m]

        def run(y_own, rms):
            y_own = y_own.astype(F32)
            own_rms = lax.dynamic_slice(rms, (col_index * own_count,), (own_count,))
            residual = own_rows[m] + own_rms[:, None] * y_own
            return row_norm(residual, second_gain).astype(BF16), residual, y_own

        second, s["residual"], s["y_own"] = step(run, s["y"], s["rms"])
        s["second"] = lax.all_gather(second, "col", axis=0, tiled=True)
        s["second_own"] = second

    def gather_cot(m, *others):
        return lax.all_gather(after(own_cots[m], *others), "col", axis=0, tiled=True)

    def spread_cot(m):
        s = state[m]
        slot, gates_of = slot_rows[m]
        (s["cot_rows"],) = step(
            lambda cot: spread_rows(rows_n, slot, gates_of, cot), s["cot"]
        )

    def spread_tokens(m):
        s = state[m]
        slot, gates_of = slot_rows[m]
        (
            s["token_rows"],
            s["shared_hidden"],
            s["d_shared_gate"],
            s["d_shared_up"],
            *s["shared_grads"],
        ) = step(
            lambda second, cot, before: spread_rows(
                rows_n,
                slot,
                gates_of,
                second,
                cot,
                shared_w,
                before,
                BF16 if m == micro_count - 1 else F32,
            ),
            s["second"],
            s["cot"],
            state[m - 1]["shared_grads"] if m else (),
        )

    def experts(m):
        s = state[m]
        later = state[m + 1] if m + 1 < micro_count else None
        part, out_rows, saved, spread = step(
            lambda cot, grads, *args: expert_rows(
                () if later is None else (*slot_rows[m + 1], cot), grads, slot_cols[m][0], *args
            ),
            s["cot"] if later is None else later["cot"],
            s["shared_grads"],
            s["token_rows"],
            s["cot_rows"],
            s["d_shared_gate"],
            s["d_shared_up"],
            shared_w,
            gates,
            ups,
            downs,
        )
        s["expert_saved"] = [s["token_rows"], s["cot_rows"], *saved]
        if later is None:
            s["shared_totals"] = spread
        else:
            (later["cot_rows"],) = spread
        s["second_share"] = lax.psum_scatter(part, "col", scatter_dimension=0, tiled=True)
        s["out_rows"] = list(out_rows) if later is None else swap_all(out_rows)

    def ahead_rows(m, parts=()):
        s = state[m]
        slot_t, gates_t = slot_cols[m]
        part, *stacked = step(
            lambda rows, left, parts: combine_rows(
                slot_t, gates_t, rows, left, shared_out, parts
            ),
            s["out_rows"],
            s["shared_hidden"],
            parts,
        )
        s["branch_share"] = lax.psum_scatter(part, "col", scatter_dimension=0, tiled=True)
        return stacked

    def second_back(m):
        s = state[m]

        def run(share_in):
            back, gain_grad = norm_adjoint(s["residual"], second_gain, share_in.astype(F32))
            residual_grad = own_cots[m].astype(F32) + back
            low = residual_grad.astype(BF16)
            cross = jnp.sum(low.astype(F32) * s["y_own"], axis=1, keepdims=True)
            parts = [low]
            for _ in range(3):
                parts.append(cross.astype(BF16))
                cross = cross - parts[-1].astype(F32)
            parts.append(jnp.zeros((own_count, LANES - 3), BF16))
            return jnp.concatenate(parts, axis=1), residual_grad, gain_grad

        low, s["residual_grad"], s["second_gain_grad"] = step(run, s["second_share"])
        s["low"] = low
        s["d_res"] = lax.all_gather(low, "col", axis=0, tiled=True)

    def mix_back(m, parts, moved=()):
        s = state[m]
        scale_rows = jnp.pad(
            jnp.stack([s["rms"], jnp.full((length,), 1.0 / inner, F32)]), ((0, 6), (0, 0))
        )
        (first_part, *s["back"]), stacked, arrived = step(
            lambda d_res, scales, parts, moved: mixer_backward(
                parts, moved, d_res, scales, normed[m], weights, s["saved"], heads
            ),
            s["d_res"],
            scale_rows,
            parts,
            moved,
        )
        s["first_part"] = first_part
        return stacked, arrived

    def total_of(parts):
        return jax.tree.map(lambda *terms: functools.reduce(jnp.add, terms), *parts)

    def expert_grads(*saved):
        def over_rows(left, right):
            return jnp.einsum("ecd,ech->edh", left, right, preferred_element_type=F32)

        totals = total_of(
            [
                (over_rows(tokens, d_pre), over_rows(cot, hidden))
                for tokens, cot, hidden, d_pre in saved
            ]
        )
        both, down = totals[0].astype(BF16), totals[1].astype(BF16)
        return [
            [
                lax.dynamic_slice(full, (0, peer(k) * depth, at), (per_device, depth, part_width))
                for k in range(rows_n)
            ]
            for full, at in ((both, 0), (both, part_width), (down, 0))
        ]

    def sum_first(m, *others):
        s = state[m]
        s["first_share"] = lax.psum_scatter(
            after(s["first_part"], *others), "col", scatter_dimension=0, tiled=True
        )

    def finish_output(m):
        s = state[m]
        s["output"] = step(
            lambda share_in: (s["residual"] + share_in.astype(F32)).astype(BF16), s["branch_share"]
        )

    def finish_input(m):
        s = state[m]

        def run(share_in):
            back, _ = norm_adjoint(own_rows[m], first_gain, share_in.astype(F32))
            return s["residual_grad"] + back

        s["input_grad"] = step(run, s["first_share"])

    def whole_experts(stacked):
        stacked = stacked.reshape(local_experts, split, depth, part_width)
        return jnp.swapaxes(stacked, 1, 2).reshape(local_experts, depth, hidden_width)

    def arrive(parts):
        return step(lambda *values: values, *parts)

    first, second = 0, micro_count - 1
    state[first]["cot"] = gather_cot(first, in_all)
    gates = mix(first, expert_gate)
    (normed[second],) = arrive([normed[second]])
    sum_y(first)
    scale_of(first)
    state[second]["cot"] = gather_cot(second, state[first]["squares"])
    ups = mix(second, expert_up)
    downs = arrive(downs)
    (state[first]["cot"],) = arrive([state[first]["cot"]])
    scale_of(second)
    second_norm(first)
    sum_y(second, state[first]["second_own"])
    spread_cot(first)
    shared_full = step(
        lambda *parts: gather_width(jnp.concatenate(parts, axis=0)),
        shared_gate.T,
        shared_up.T,
        shared_down,
    )
    shared_w = (
        shared_full[:shared_width],
        shared_full[shared_width : 2 * shared_width],
        shared_full[2 * shared_width :],
    )
    shared_out = shared_w[2]
    spread_tokens(first)
    second_norm(second)
    experts(first)
    spread_tokens(second)
    second_back(first)
    experts(second)
    (state[first]["d_res"],) = arrive([state[first]["d_res"]])
    shared_totals = state[second]["shared_totals"]
    gate_grads, up_grads, down_grads = step(expert_grads, *[s["expert_saved"] for s in state])
    state[first]["out_rows"] = arrive(state[first]["out_rows"])
    second_back(second)
    ahead_rows(first)
    rows = state[second]["out_rows"]
    gate_grads, arrived = mix_back(first, gate_grads, rows[1:])
    state[second]["out_rows"] = [rows[0], *arrived]
    (state[second]["d_res"],) = arrive([state[second]["d_res"]])
    sum_first(first, state[second]["low"])
    (down_grads,) = ahead_rows(second, down_grads)
    finish_output(first)
    up_grads, _ = mix_back(second, up_grads)
    sum_first(second)
    finish_input(first)
    finish_output(second)
    sets = []
    for m in micro:
        s = state[m]
        gain_part, mixed, d_branch, d_conv, d_io, d_step, chan_grad, io_grad, head_grad = s["back"]
        sets.append(
            [
                normed[m],
                s["d_res"],
                d_branch,
                d_conv,
                mixed,
                d_step,
                d_io,
                gain_part,
                s["second_gain_grad"],
                chan_grad,
                io_grad,
                head_grad,
            ]
        )
    branch_grad, conv_grad, out_grad_sum, step_grad, io_proj_grad, gains, io_sums, chans, by_head = (
        step(lambda sets: tail_sums(rows_n, cols_n, first_gain[None, :], sets), sets)
    )
    finish_input(second)
    io_values = lax.dynamic_slice(io_sums, (0, col_index * io_width), (5, io_width))
    return (
        jnp.stack([s["output"] for s in state]),
        jnp.stack([s["input_grad"] for s in state]),
        gains[0],
        branch_grad,
        conv_grad,
        io_proj_grad,
        step_grad[:, :heads],
        chans[:4],
        chans[4],
        io_values[:4],
        io_values[4],
        by_head[:heads, 0],
        by_head[:heads, 1],
        by_head[:heads, 2],
        chans[5],
        out_grad_sum.T,
        gains[1],
        whole_experts(gate_grads).astype(F32),
        whole_experts(up_grads).astype(F32),
        jnp.swapaxes(whole_experts(down_grads).astype(F32), 1, 2),
        shared_totals[0],
        shared_totals[1],
        shared_totals[2].T,
    )


def solution(mesh):
    both = P(None, ("row", "col"), None)
    placed = (
        both,
        both,
        P(None, "row"),
        P(None, "row", None),
        P(None, "row", None),
        P(),
        P("row", "col"),
        P("row", "col"),
        P("row", "col"),
        P("row", "col"),
        P(None, "col"),
        P("col"),
        P(None, "col"),
        P("col"),
        P("col"),
        P("col"),
        P("col"),
        P("col"),
        P("col", "row"),
        P(),
        P("col", "row", None),
        P("col", "row", None),
        P("col", None, "row"),
        P("row", "col"),
        P("row", "col"),
        P("col", "row"),
    )
    return jax.shard_map(
        local,
        mesh=mesh,
        in_specs=placed,
        out_specs=(both, both, P()) + placed[6:19] + (P(),) + placed[20:],
        check_vma=False,
    )
```

```python
import functools

import jax
import jax.numpy as jnp
from jax import lax
from jax.experimental import pallas as pl
from jax.experimental.pallas import tpu as pltpu
from jax.sharding import PartitionSpec as P

NS = 128
BLOCK = 256
CAP = 144
EPS = 1e-05
HEAD_ROWS = 16
LANES = 128
F32 = jnp.float32
BF16 = jnp.bfloat16
VMEM = pl.BlockSpec(memory_space=pltpu.VMEM)
VMEM_LIMIT = 56 * 1024 * 1024
GROUP = 3
KERNEL_COST = pl.CostEstimate(flops=3 * 10**10, bytes_accessed=2**20, transcendentals=0)
ANY = pl.BlockSpec(memory_space=pl.ANY)
MESH = pl.DeviceIdType.MESH


def contract(left_op, right_op, left_dim, right_dim, precision=None):
    return lax.dot_general(
        left_op,
        right_op,
        (((left_dim,), (right_dim,)), ((), ())),
        preferred_element_type=F32,
        precision=precision,
    )


def dot_plain(left_op, right_op):
    return contract(left_op, right_op, 1, 0)


def dot_first(left_op, right_op):
    return contract(left_op, right_op, 0, 0)


def dot_last(left_op, right_op):
    return contract(left_op, right_op, 1, 1)


def silu_slope(values):
    logistic = jax.nn.sigmoid(values)
    return logistic * (1.0 + values * (1.0 - logistic))


def softplus(values):
    return jnp.maximum(values, 0.0) + jnp.log1p(jnp.exp(-jnp.abs(values)))


def shifts_back(current, before):
    joined = jnp.concatenate([before, current], axis=1)
    return [pltpu.roll(joined, step, 1)[:, LANES:] for step in (1, 2, 3)]


def load_block(ref, rows, block):
    cols = pl.ds(pl.multiple_of(block * BLOCK, BLOCK), BLOCK)
    current = ref[rows, cols]
    ahead = pl.multiple_of(jnp.maximum(block * BLOCK - LANES, 0), LANES)
    before = jnp.where(block > 0, ref[rows, pl.ds(ahead, LANES)], 0.0)
    return current, shifts_back(current, before)


def convolved(current, back, taps):
    return (
        taps[:, 4:5]
        + taps[:, 3:4] * current
        + taps[:, 2:3] * back[0]
        + taps[:, 1:2] * back[1]
        + taps[:, 0:1] * back[2]
    )


def conv_adjoint(adjoint, after, taps):
    joined = jnp.concatenate([adjoint, after], axis=1)
    width = joined.shape[1]
    total = taps[:, 3:4] * adjoint
    for step in (1, 2, 3):
        ahead = pltpu.roll(joined, width - step, 1)[:, :BLOCK]
        total = total + taps[:, 3 - step : 4 - step] * ahead
    return total


def lane_tile(columns):
    rows = columns[0].shape[0]
    lane = lax.broadcasted_iota(jnp.int32, (rows, LANES), 1)
    tile = jnp.zeros((rows, LANES), F32)
    for place, column in enumerate(columns):
        tile = jnp.where(lane == place, column, tile)
    return tile


def row_sum(values):
    return jnp.sum(values, axis=1, keepdims=True)


def decay_block(cum_row, cum_cols, head):
    lane = lax.broadcasted_iota(jnp.int32, cum_cols.shape, 1)
    cum_col = row_sum(jnp.where(lane == head, cum_cols, 0.0))
    place_j = lax.broadcasted_iota(jnp.int32, (BLOCK, BLOCK), 0)
    place_i = lax.broadcasted_iota(jnp.int32, (BLOCK, BLOCK), 1)
    return jnp.exp(jnp.where(place_j <= place_i, cum_row - cum_col, -1e30))


def step_rows(step_pre, head_params, step_s, cum_s, cum_t_s, blocks):
    step = softplus(step_pre + head_params[:, 0:1])
    step_s[...] = step
    log_decay = -(step * head_params[:, 1:2])
    place_j = lax.broadcasted_iota(jnp.int32, (BLOCK, BLOCK), 0)
    place_i = lax.broadcasted_iota(jnp.int32, (BLOCK, BLOCK), 1)
    upper = jnp.where(place_j <= place_i, 1.0, 0.0)
    for block in range(blocks):
        cols = slice(block * BLOCK, (block + 1) * BLOCK)
        cum = contract(log_decay[:, cols], upper, 1, 0, lax.Precision.HIGHEST)
        cum_s[:, cols] = cum
        cum_t_s[cols, :] = jnp.transpose(cum)


def score_blocks(io, scores_s, blocks):
    for block in range(blocks):
        cols = slice(block * BLOCK, (block + 1) * BLOCK)
        scores_s[block] = dot_first(io[:NS, cols], io[NS:, cols])


def block_cols(block):
    return pl.ds(pl.multiple_of(block * BLOCK, BLOCK), BLOCK)


def head_group(heads):
    return GROUP if heads % GROUP == 0 else 1


def greet(peers):
    barrier = pltpu.get_barrier_semaphore()
    for other in peers:
        pl.semaphore_signal(barrier, inc=1, device_id=other, device_id_type=MESH)
    pl.semaphore_wait(barrier, len(peers))


def row_partners(members):
    me = lax.axis_index("row")
    return [{"row": me ^ k} for k in range(1, members)]


def make_send(source, target, send_sem, recv_sem, other):
    return pltpu.make_async_remote_copy(
        src_ref=source,
        dst_ref=target,
        send_sem=send_sem,
        recv_sem=recv_sem,
        device_id=other,
        device_id_type=MESH,
    )


def send(*args):
    copy = make_send(*args)
    copy.start()
    return copy


def unit_of(member, per_device, split, part_width):
    if split == 1:
        return member * per_device, 0
    return (member * per_device) // split, pl.multiple_of((member % split) * part_width, LANES)


def unit_part(weight, member, per_device, split):
    part_width = weight.shape[2] // split
    first, hidden_at = unit_of(member, per_device, split, part_width)
    return weight.at[pl.ds(first, per_device), :, pl.ds(hidden_at, part_width)]


def send_stack(parts, stacked, sems):
    if not parts:
        return []
    me = lax.axis_index("row")
    copies = [pltpu.make_async_copy(parts[0], stacked.at[me], sems.at[0, 0])]
    copies[0].start()
    for k, other in enumerate(row_partners(len(parts)), 1):
        copies.append(send(parts[k], stacked.at[me], sems.at[0, k], sems.at[1, k], other))
    return copies


def mixer_forward_kernel(
    heads,
    cols_n,
    per_device,
    split,
    xn,
    wb,
    wc,
    wio,
    ws,
    wo,
    chan,
    io_taps,
    head_params,
    *refs,
):
    weight, *refs = refs
    count = len(refs) - 18
    y, squares, branch, conv, io_pre, io, step_pre, starts = refs[:8]
    received = refs[8 : 8 + count]
    step_s, cum_s, cum_t_s, scores_s, z_s, sems = refs[8 + count : 14 + count]
    squares_s, own_s, got_s, square_sems = refs[14 + count :]
    at = lax.axis_index("col")
    col_peers = [{"col": at ^ k} for k in range(1, cols_n)]
    row_peers = row_partners(count + 1)
    greet(row_peers + col_peers)
    copies = [
        send(
            unit_part(weight, lax.axis_index("row") ^ (k + 1), per_device, split),
            received[k],
            sems.at[0, k],
            sems.at[1, k],
            other,
        )
        for k, other in enumerate(row_peers)
    ]
    length = xn.shape[0]
    blocks = length // BLOCK
    size = wb.shape[0] // heads
    step_pre[...] = dot_last(ws[...], xn[...])
    step_rows(step_pre[...], head_params[...], step_s, cum_s, cum_t_s, blocks)

    def project(block, carry):
        cols = block_cols(block)
        rows = xn[cols, :]
        io_pre[:, cols] = dot_last(wio[...], rows)
        branch[:, cols] = dot_last(wb[...], rows)
        conv[:, cols] = dot_last(wc[...], rows)
        return carry

    lax.fori_loop(0, blocks, project, 0)

    def io_step(at, carry):
        rows = pl.ds(pl.multiple_of((at // blocks) * 64, 64), 64)
        block = at % blocks
        current, back = load_block(io_pre, rows, block)
        io[rows, block_cols(block)] = jax.nn.silu(
            convolved(current, back, io_taps[rows, :])
        ).astype(BF16)
        return carry

    lax.fori_loop(0, blocks * (2 * NS // 64), io_step, 0)
    score_blocks(io, scores_s, blocks)
    squares_s[...] = jnp.zeros_like(squares_s)

    group = head_group(heads)

    def head_step(first, carry):
        def block_steps(block, states):
            return tuple(
                block_step(first * group + at, block, state) for at, state in enumerate(states)
            )

        def block_step(head, block, state):
            rows = pl.ds(pl.multiple_of(head * size, size), size)
            params = chan[rows, :]
            cols = block_cols(block)
            current, back = load_block(conv, rows, block)
            x = jax.nn.silu(convolved(current, back, params))
            step_row = step_s[pl.ds(head, 1), cols]
            cum_row = cum_s[pl.ds(head, 1), cols]
            last = cum_row[:, BLOCK - 1 : BLOCK]
            mixing = (scores_s[block] * decay_block(cum_row, cum_t_s[cols, :], head)).astype(BF16)
            weighted = x * step_row
            starts[pl.ds(pl.multiple_of((head * blocks + block) * size, size), size), :] = state
            scanned = dot_plain(weighted.astype(BF16), mixing)
            scanned = scanned + dot_plain(state.astype(BF16), io[NS:, cols]) * jnp.exp(cum_row)
            scanned = scanned + params[:, 6:7] * x
            gated = scanned * jax.nn.silu(branch[rows, cols])
            squares_s[:, cols] += jnp.sum((gated * gated).reshape(size // 8, 8, BLOCK), axis=0)
            z_s[rows, cols] = (gated * params[:, 5:6]).astype(BF16)
            to_end = (weighted * jnp.exp(last - cum_row)).astype(BF16)
            return state * jnp.exp(last) + dot_last(to_end, io[:NS, cols])

        lax.fori_loop(0, blocks, block_steps, (jnp.zeros((size, NS), F32),) * group)
        return carry

    lax.fori_loop(0, heads // group, head_step, 0)
    own_s[...] = jnp.sum(squares_s[...], axis=0, keepdims=True)
    square_copies = [
        send(own_s, got_s.at[k], square_sems.at[0, k], square_sems.at[1, k], other)
        for k, other in enumerate(col_peers)
    ]

    def out_step(block, carry):
        cols = block_cols(block)
        y[cols, :] = dot_first(z_s[:, cols], wo[...]).astype(BF16)
        return carry

    lax.fori_loop(0, blocks, out_step, 0)
    for copy in square_copies:
        copy.wait()
    total = own_s[...]
    for k in range(cols_n - 1):
        total = total + got_s[k]
    squares[...] = total
    for copy in copies:
        copy.wait()


def mixer_forward(rows_n, cols_n, unit, weight, xn, wb, wc, wio, ws, wo, chan, io_taps, head_params, heads):
    length, width = xn.shape
    share = wb.shape[0]
    blocks = length // BLOCK
    size = share // heads
    shape = jax.ShapeDtypeStruct
    out = pl.pallas_call(
        functools.partial(mixer_forward_kernel, heads, cols_n, *unit),
        out_shape=(
            shape((length, width), BF16),
            shape((1, length), F32),
            shape((share, length), F32),
            shape((share, length), F32),
            shape((2 * NS, length), F32),
            shape((2 * NS, length), BF16),
            shape((HEAD_ROWS, length), F32),
            shape((heads * blocks * size, NS), F32),
        )
        + (shape((unit[0], weight.shape[1], weight.shape[2] // unit[1]), BF16),) * (rows_n - 1),
        in_specs=[VMEM] * 9 + [ANY],
        out_specs=(VMEM,) * 8 + (ANY,) * (rows_n - 1),
        scratch_shapes=[
            pltpu.VMEM((HEAD_ROWS, length), F32),
            pltpu.VMEM((HEAD_ROWS, length), F32),
            pltpu.VMEM((length, HEAD_ROWS), F32),
            pltpu.VMEM((blocks, BLOCK, BLOCK), F32),
            pltpu.VMEM((share, length), BF16),
            pltpu.SemaphoreType.DMA((2, rows_n - 1)),
            pltpu.VMEM((8, length), F32),
            pltpu.VMEM((1, length), F32),
            pltpu.VMEM((cols_n - 1, 1, length), F32),
            pltpu.SemaphoreType.DMA((2, cols_n - 1)),
        ],
        compiler_params=pltpu.CompilerParams(
            vmem_limit_bytes=VMEM_LIMIT, collective_id=2, has_side_effects=True
        ),
        cost_estimate=KERNEL_COST,
    )(xn, wb, wc, wio, ws, wo, chan, io_taps, head_params, weight)
    return out[:8], out[8:]


def mixer_backward_kernel(
    heads,
    members,
    moved_n,
    d_res,
    scale_rows,
    xn,
    wb,
    wc,
    wio,
    ws,
    wo,
    chan,
    io_taps,
    head_params,
    branch,
    conv,
    io_pre,
    io,
    step_pre,
    starts,
    *refs,
):
    refs = list(refs)
    parts, refs = refs[:members], refs[members:]
    moved, refs = refs[:moved_n], refs[moved_n:]
    first_part, gain_part, mixed, d_branch, d_conv, d_io, d_step = refs[:7]
    chan_grad_t, io_grad_t, head_grad = refs[7:10]
    stacked, arrived, refs = refs[10], refs[11 : 11 + moved_n], refs[11 + moved_n :]
    step_s, cum_s, cum_t_s, scores_s, d_scores_s, d_mixed_s, d_io_s = refs[:7]
    d_cum_s, d_size_s, adjoint_s, cube_s, sems, chan_grad, io_grad = refs[7:14]
    partners = row_partners(members)
    greet(partners)
    copies = [
        send(moved[k], arrived[k], refs[14].at[0, k], refs[14].at[1, k], partners[k])
        for k in range(moved_n)
    ]
    copies += send_stack(parts, stacked, sems)
    length, width = xn.shape
    blocks = length // BLOCK
    size = wb.shape[0] // heads
    step_rows(step_pre[...], head_params[...], step_s, cum_s, cum_t_s, blocks)
    score_blocks(io, scores_s, blocks)
    d_scores_s[...] = jnp.zeros_like(d_scores_s)
    d_io_s[...] = jnp.zeros_like(d_io_s)
    d_cum_s[...] = jnp.zeros_like(d_cum_s)
    d_size_s[...] = jnp.zeros_like(d_size_s)
    chan_grad[...] = jnp.zeros_like(chan_grad)
    io_grad[...] = jnp.zeros_like(io_grad)
    adjoint_s[:, :, length:] = jnp.zeros(adjoint_s.shape[:2] + (LANES,), F32)

    def project(block, carry):
        cols = block_cols(block)
        d_mixed_s[:, cols] = dot_last(wo[...], d_res[cols, :width])
        cross = jnp.transpose(d_res[cols, width:].astype(F32))
        cross = cross[0:1] + cross[1:2] + cross[2:3]
        rms = scale_rows[0:1, cols]
        cube_s[:, cols] = rms * rms * rms * cross * scale_rows[1:2, cols]
        return carry

    lax.fori_loop(0, blocks, project, 0)

    group = head_group(heads)

    def head_step(first, carry):
        def block_steps(reverse, d_states):
            return tuple(
                block_step(first * group + at, at, reverse, d_state)
                for at, d_state in enumerate(d_states)
            )

        def block_step(head, lane_set, reverse, d_state):
            rows = pl.ds(pl.multiple_of(head * size, size), size)
            params = chan[rows, :]
            block = blocks - 1 - reverse
            cols = block_cols(block)
            state = starts[pl.ds(pl.multiple_of((head * blocks + block) * size, size), size), :]
            state_low = state.astype(BF16)
            d_state_low = d_state.astype(BF16)
            write_rows = io[:NS, cols]
            read_rows = io[NS:, cols]
            step_row = step_s[pl.ds(head, 1), cols]
            cum_row = cum_s[pl.ds(head, 1), cols]
            last = cum_row[:, BLOCK - 1 : BLOCK]
            decays = decay_block(cum_row, cum_t_s[cols, :], head)
            mixing = (scores_s[block] * decays).astype(BF16)
            current, back = load_block(conv, rows, block)
            conv_act = convolved(current, back, params)
            logistic = jax.nn.sigmoid(conv_act)
            x = conv_act * logistic
            slope = logistic * (1.0 + conv_act * (1.0 - logistic))
            weighted = x * step_row
            weighted_low = weighted.astype(BF16)
            grown = jnp.exp(cum_row)
            within = dot_plain(weighted_low, mixing)
            carried = dot_plain(state_low, read_rows) * grown
            scanned = within + carried + params[:, 6:7] * x

            inverse_rms = scale_rows[0:1, cols]
            gate_in = branch[rows, cols]
            gate_logistic = jax.nn.sigmoid(gate_in)
            gate_out = gate_in * gate_logistic
            gated = scanned * gate_out
            d_mixed = d_mixed_s[rows, cols]
            gain = params[:, 5:6]
            mixed[rows, cols] = (gated * inverse_rms * gain).astype(BF16)
            d_gated = inverse_rms * (d_mixed * gain) - gated * cube_s[:, cols]
            d_gain = row_sum(d_mixed * gated * inverse_rms)
            d_scanned = d_gated * gate_out
            d_branch[rows, cols] = (
                d_gated * scanned * (gate_logistic * (1.0 + gate_in * (1.0 - gate_logistic)))
            ).astype(BF16)
            d_low = d_scanned.astype(BF16)
            d_skip = row_sum(d_scanned * x)

            d_within = dot_last(d_low, mixing)
            shrunk = jnp.exp(last - cum_row)
            d_fed = dot_plain(d_state_low, write_rows) * shrunk
            d_weighted = d_within + d_fed
            d_scores_s[block] += dot_first(weighted_low, d_low) * decays
            d_grown = (d_scanned * grown).astype(BF16)
            fed = (weighted * shrunk).astype(BF16)
            d_io_s[NS:, cols] += dot_first(state_low, d_grown)
            d_io_s[:NS, cols] += dot_first(d_state_low, fed)
            d_before = d_state * jnp.exp(last) + dot_last(d_grown, read_rows)

            fed_terms = weighted * d_fed
            d_cum = jnp.sum(
                d_low.astype(F32) * within
                - weighted_low.astype(F32) * d_within
                + d_scanned * carried
                - fed_terms,
                axis=0,
                keepdims=True,
            )
            at_end = jnp.sum(row_sum(fed_terms), axis=0, keepdims=True) + jnp.exp(last) * jnp.sum(
                row_sum(d_state * state), axis=0, keepdims=True
            )
            lane = lax.broadcasted_iota(jnp.int32, (1, BLOCK), 1)
            d_cum_s[pl.ds(head, 1), cols] = d_cum + jnp.where(lane == BLOCK - 1, at_end, 0.0)
            d_size_s[pl.ds(head, 1), cols] = jnp.sum(d_weighted * x, axis=0, keepdims=True)

            d_act = (d_weighted * step_row + params[:, 6:7] * d_scanned) * slope
            adjoint_s[lane_set, :, cols] = d_act
            after = adjoint_s[lane_set, :, pl.ds(pl.multiple_of((block + 1) * BLOCK, BLOCK), LANES)]
            d_conv[rows, cols] = conv_adjoint(d_act, after, params).astype(BF16)
            chan_grad[rows, :] += lane_tile(
                [
                    row_sum(d_act * back[2]),
                    row_sum(d_act * back[1]),
                    row_sum(d_act * back[0]),
                    row_sum(d_act * current),
                    row_sum(d_act),
                    d_gain,
                    d_skip,
                ]
            )
            return d_before

        lax.fori_loop(0, blocks, block_steps, (jnp.zeros((size, NS), F32),) * group)
        return carry

    lax.fori_loop(0, heads // group, head_step, 0)

    def scores_step(block, carry):
        cols = block_cols(block)
        d_scores = d_scores_s[block].astype(BF16)
        d_io_s[NS:, cols] += dot_plain(io[:NS, cols], d_scores)
        d_io_s[:NS, cols] += dot_last(io[NS:, cols], d_scores)
        return carry

    lax.fori_loop(0, blocks, scores_step, 0)

    def io_step(at, carry):
        rows = pl.ds(pl.multiple_of((at // blocks) * 64, 64), 64)
        block = blocks - 1 - at % blocks
        cols = block_cols(block)
        taps = io_taps[rows, :]
        current, back = load_block(io_pre, rows, block)
        d_act = d_io_s[rows, cols] * silu_slope(convolved(current, back, taps))
        adjoint_s[0, :64, cols] = d_act
        after = adjoint_s[0, :64, pl.ds(pl.multiple_of((block + 1) * BLOCK, BLOCK), LANES)]
        d_io[rows, cols] = conv_adjoint(d_act, after, taps).astype(BF16)
        io_grad[rows, :] += lane_tile(
            [
                row_sum(d_act * back[2]),
                row_sum(d_act * back[1]),
                row_sum(d_act * back[0]),
                row_sum(d_act * current),
                row_sum(d_act),
            ]
        )
        return carry

    lax.fori_loop(0, blocks * (2 * NS // 64), io_step, 0)

    place_j = lax.broadcasted_iota(jnp.int32, (BLOCK, BLOCK), 0)
    place_i = lax.broadcasted_iota(jnp.int32, (BLOCK, BLOCK), 1)
    lower = jnp.where(place_j >= place_i, 1.0, 0.0)
    rate = head_params[:, 1:2]
    decay_grad = jnp.zeros((HEAD_ROWS, 1), F32)
    offset_grad = jnp.zeros((HEAD_ROWS, 1), F32)
    for block in range(blocks):
        cols = slice(block * BLOCK, (block + 1) * BLOCK)
        d_log = contract(d_cum_s[:, cols], lower, 1, 0, lax.Precision.HIGHEST)
        decay_grad = decay_grad - row_sum(step_s[:, cols] * rate * d_log)
        d_size = d_size_s[:, cols] - rate * d_log
        d_pre = d_size * jax.nn.sigmoid(step_pre[:, cols] + head_params[:, 0:1])
        offset_grad = offset_grad + row_sum(d_pre)
        d_step[:, cols] = d_pre.astype(BF16)
    skip = jnp.sum(chan_grad[:, 6:7].reshape(heads, size, 1), axis=1)
    skip = jnp.concatenate([skip, jnp.zeros((HEAD_ROWS - heads, 1), F32)], axis=0)
    head_grad[...] = lane_tile([decay_grad, offset_grad, skip])
    gain_part[...] = jnp.zeros_like(gain_part)

    def first_step(block, carry):
        cols = block_cols(block)
        part = (
            dot_first(d_branch[:, cols], wb[...])
            + dot_first(d_conv[:, cols], wc[...])
            + dot_first(d_io[:, cols], wio[...])
            + dot_first(d_step[:, cols], ws[...])
        )
        first_part[cols, :] = part.astype(BF16)
        product = part * xn[cols, :].astype(F32)
        gain_part[...] += jnp.sum(product.reshape(BLOCK // 8, 8, -1), axis=0)
        return carry

    lax.fori_loop(0, blocks, first_step, 0)
    chan_grad_t[...] = jnp.transpose(chan_grad[...])[:8]
    io_grad_t[...] = jnp.transpose(io_grad[...])[:8]
    for copy in copies:
        copy.wait()


def mixer_backward(parts, moved, d_res, scale_rows, xn, weights, saved, heads):
    length, width = xn.shape
    share = weights[0].shape[0]
    blocks = length // BLOCK
    size = share // heads
    shape = jax.ShapeDtypeStruct
    out = pl.pallas_call(
        functools.partial(mixer_backward_kernel, heads, len(parts), len(moved)),
        out_shape=(
            shape((length, width), BF16),
            shape((8, width), F32),
            shape((share, length), BF16),
            shape((share, length), BF16),
            shape((share, length), BF16),
            shape((2 * NS, length), BF16),
            shape((HEAD_ROWS, length), BF16),
            shape((8, share), F32),
            shape((8, 2 * NS), F32),
            shape((HEAD_ROWS, LANES), F32),
        )
        + (shape((len(parts),) + parts[0].shape, BF16),)
        + tuple(shape(rows.shape, BF16) for rows in moved),
        in_specs=[VMEM] * 17 + [ANY] * (len(parts) + len(moved)),
        out_specs=(VMEM,) * 10 + (ANY,) * (1 + len(moved)),
        scratch_shapes=[
            pltpu.VMEM((HEAD_ROWS, length), F32),
            pltpu.VMEM((HEAD_ROWS, length), F32),
            pltpu.VMEM((length, HEAD_ROWS), F32),
            pltpu.VMEM((blocks, BLOCK, BLOCK), F32),
            pltpu.VMEM((blocks, BLOCK, BLOCK), F32),
            pltpu.VMEM((share, length), F32),
            pltpu.VMEM((2 * NS, length), F32),
            pltpu.VMEM((HEAD_ROWS, length), F32),
            pltpu.VMEM((HEAD_ROWS, length), F32),
            pltpu.VMEM((head_group(heads), size, length + LANES), F32),
            pltpu.VMEM((1, length), F32),
            pltpu.SemaphoreType.DMA((2, len(parts))),
            pltpu.VMEM((share, LANES), F32),
            pltpu.VMEM((2 * NS, LANES), F32),
        ]
        + [pltpu.SemaphoreType.DMA((2, len(moved)))] * bool(moved),
        compiler_params=pltpu.CompilerParams(
            vmem_limit_bytes=VMEM_LIMIT,
            collective_id=3 if moved else 8,
            has_side_effects=True,
        ),
        cost_estimate=KERNEL_COST,
    )(d_res, scale_rows, xn, *weights, *saved, *parts, *moved)
    return out[:10], out[10], out[11:]


def place_rows(slot_t, gates_t, placed):
    length, units = slot_t.shape

    def choose(block, carry):
        at = block_cols(block)
        slots = slot_t[at, :]
        for tile in range(units * CAP // LANES):
            low, high = tile * LANES // CAP, (tile * LANES + LANES - 1) // CAP
            lane = lax.broadcasted_iota(jnp.int32, (BLOCK, LANES), 1) + tile * LANES
            total = jnp.zeros((BLOCK, LANES), F32)
            for unit in range(low, high + 1):
                value = 1.0 if gates_t is None else gates_t[at, unit : unit + 1]
                total = jnp.where(lane == slots[:, unit : unit + 1] + unit * CAP, value, total)
            placed[at, tile * LANES : (tile + 1) * LANES] = total.astype(BF16)
        return carry

    lax.fori_loop(0, length // BLOCK, choose, 0)


def combine_kernel(members, with_parts, slot_t, gates_t, extra_left, extra_right, *refs):
    refs = list(refs)
    rows, refs = refs[:members], refs[members:]
    if with_parts:
        parts, out, stacked, chosen_s, rows_s, sems, part_sems = refs[:members], *refs[members:]
        greet(row_partners(members))
        copies = send_stack(parts, stacked, part_sems)
    else:
        out, chosen_s, rows_s, sems = refs
        copies = []
    part = rows_s.shape[0] // members
    loads = []
    for member in range(members):
        loads.append(
            pltpu.make_async_copy(
                rows[member], rows_s.at[pl.ds(member * part, part)], sems.at[member]
            )
        )
        loads[-1].start()
    place_rows(slot_t, gates_t, chosen_s)
    for copy in loads:
        copy.wait()

    def columns(at, carry):
        cols = block_cols(at)
        total = dot_plain(chosen_s[...], rows_s[:, cols])
        total = total + dot_plain(extra_left[...], extra_right[:, cols])
        out[:, cols] = total.astype(BF16)
        return carry

    lax.fori_loop(0, out.shape[1] // BLOCK, columns, 0)
    for copy in copies:
        copy.wait()


def combine_rows(slot_t, gates_t, rows, extra_left, extra_right, parts):
    length, units = slot_t.shape
    members = len(rows)
    width = rows[0].shape[1]
    shape = jax.ShapeDtypeStruct
    out = [shape((length, width), BF16)]
    scratch = [
        pltpu.VMEM((length, units * CAP), BF16),
        pltpu.VMEM((units * CAP, width), BF16),
        pltpu.SemaphoreType.DMA((members,)),
    ]
    params = {}
    if parts:
        out.append(shape((members,) + parts[0].shape, BF16))
        scratch.append(pltpu.SemaphoreType.DMA((2, members)))
        params = {"collective_id": 9, "has_side_effects": True}
    return pl.pallas_call(
        functools.partial(combine_kernel, members, bool(parts)),
        out_shape=tuple(out),
        in_specs=[VMEM] * 4 + [ANY] * (members + len(parts)),
        out_specs=(VMEM,) + (ANY,) * (len(out) - 1),
        scratch_shapes=scratch,
        compiler_params=pltpu.CompilerParams(vmem_limit_bytes=VMEM_LIMIT, **params),
        cost_estimate=KERNEL_COST,
    )(slot_t, gates_t, extra_left, extra_right, *rows, *parts)


def spread_start(
    members, weighted, slot, gates, source, received, outgoing, chosen_s, gate_s, row_sems, own_sems
):
    units, length = slot.shape
    width = source.shape[1]
    experts = units // members
    rows = experts * CAP
    partners = row_partners(members)

    def choose(unit, carry):
        at = pl.ds(pl.multiple_of(unit * CAP, CAP), CAP)
        place = lax.broadcasted_iota(jnp.int32, (CAP, length), 0)
        hit = place == slot[pl.ds(unit, 1), :]
        chosen_s[at, :] = jnp.where(hit, 1.0, 0.0).astype(BF16)
        if weighted:
            gate_s[at, :] = row_sum(jnp.where(hit, gates[pl.ds(unit, 1), :], 0.0))
        return carry

    lax.fori_loop(0, units, choose, 0)

    def pairs(part):
        out = []
        for expert in range(experts):
            for k, other in enumerate(partners):
                out.append(
                    make_send(
                        outgoing.at[pl.ds((k + 1) * rows + expert * CAP, CAP), part],
                        received.at[expert, pl.ds((k + 1) * CAP, CAP), part],
                        row_sems.at[0, k, expert],
                        row_sems.at[1, k, expert],
                        other,
                    )
                )
            out.append(
                pltpu.make_async_copy(
                    outgoing.at[pl.ds(expert * CAP, CAP), part],
                    received.at[expert, pl.ds(0, CAP), part],
                    own_sems.at[expert],
                )
            )
        return out

    def columns(at, carry):
        cols = block_cols(at)
        picked = dot_plain(chosen_s[...], source[:, cols])
        if weighted:
            picked = picked * gate_s[...]
        outgoing[:, cols] = picked.astype(BF16)
        for copy in pairs(cols):
            copy.start()
        return carry

    lax.fori_loop(0, width // BLOCK, columns, 0)
    return pairs(pl.ds(0, width))


def spread_kernel(members, weighted, before_n, slot, gates, source, *refs):
    if weighted:
        received, refs = refs[0], refs[1:]
    else:
        cot, gate_sh, up_sh, down_sh = refs[:4]
        before, refs = refs[4 : 4 + before_n], refs[4 + before_n :]
        received, hidden_sh, d_gate_sh, d_up_sh = refs[:4]
        grads, refs = refs[4:7], refs[7:]
    outgoing, chosen_s, gate_s, row_sems, own_sems = refs
    length, width = source.shape
    partners = row_partners(members)
    greet(partners)
    copies = spread_start(
        members, weighted, slot, gates, source, received, outgoing, chosen_s, gate_s, row_sems, own_sems
    )

    if not weighted:

        def shared_step(at, carry):
            at = block_cols(at)
            gate_pre = dot_last(source[at, :], gate_sh[...])
            up_pre = dot_last(source[at, :], up_sh[...])
            d_hidden = dot_last(cot[at, :], down_sh[...])
            logistic = jax.nn.sigmoid(gate_pre)
            active = gate_pre * logistic
            hidden_sh[at, :] = (active * up_pre).astype(BF16)
            slope = logistic * (1.0 + gate_pre * (1.0 - logistic))
            d_gate_sh[at, :] = (d_hidden * up_pre * slope).astype(BF16)
            d_up_sh[at, :] = (d_hidden * active).astype(BF16)
            return carry

        lax.fori_loop(0, length // BLOCK, shared_step, 0)

        def grad_step(at, carry):
            cols = block_cols(at)
            for at, (rows, right) in enumerate(
                ((source, d_gate_sh), (source, d_up_sh), (cot, hidden_sh))
            ):
                value = dot_first(rows[:, cols], right[...])
                if before:
                    value = value + before[at][cols, :]
                grads[at][cols, :] = value.astype(grads[at].dtype)
            return carry

        lax.fori_loop(0, width // BLOCK, grad_step, 0)
    for copy in copies:
        copy.wait()


def spread_scratch(members, units, length, width):
    experts = units // members
    return [
        pltpu.VMEM((units * CAP, width), BF16),
        pltpu.VMEM((units * CAP, length), BF16),
        pltpu.VMEM((units * CAP, 1), F32),
        pltpu.SemaphoreType.DMA((2, members - 1, experts)),
        pltpu.SemaphoreType.DMA((experts,)),
    ]


def spread_rows(members, slot, gates, source, cot=None, shared_w=(), before=(), grad_type=F32):
    units, length = slot.shape
    width = source.shape[1]
    experts = units // members
    weighted = cot is None
    shape = jax.ShapeDtypeStruct
    out = [shape((experts, members * CAP, width), BF16)]
    out += [shape((length, weight.shape[0]), BF16) for weight in shared_w]
    out += [shape(weight.shape[::-1], grad_type) for weight in shared_w]
    extra = () if weighted else (cot, *shared_w, *before)
    return pl.pallas_call(
        functools.partial(spread_kernel, members, weighted, len(before)),
        out_shape=tuple(out),
        in_specs=[VMEM] * (3 + len(extra)),
        out_specs=(ANY,) + (VMEM,) * (2 * len(shared_w)),
        scratch_shapes=spread_scratch(members, units, length, width),
        compiler_params=pltpu.CompilerParams(
            vmem_limit_bytes=VMEM_LIMIT,
            collective_id=4 if weighted else 11 if before else 5,
            has_side_effects=True,
        ),
        cost_estimate=KERNEL_COST,
    )(slot, gates, source, *extra)


def expert_kernel(
    members, split, following, slot_t, token_s, cot_s, d_gate_sh, d_up_sh, gate_sh, up_sh, *refs
):
    refs = list(refs)
    if following:
        slot, gates, source = refs[:3]
        received, picked_s, chosen_s, gate_s, spread_sems, own_sems = refs[-6:]
        refs = refs[3:-6]
    else:
        grads, grad_outs, grad_got, grad_sems = refs[:3], refs[-7:-4], refs[-4:-1], refs[-1]
        refs = refs[3:-7]
    shards = [refs[at * members : (at + 1) * members] for at in range(3)]
    part, out_rows, hidden_s, d_pre_s, outgoing, back_s, weights, places_s, row_sems, weight_sems = (
        refs[3 * members :]
    )
    experts, _, width = token_s.shape
    rows = experts * CAP
    hidden_width = weights.shape[3]
    depth = width // members
    chunk = min(BLOCK, hidden_width)
    me = lax.axis_index("row")
    partners = row_partners(members)
    weight_copies = []
    for which in range(3):
        for member in range(members):
            place = pl.ds(pl.multiple_of((me ^ member) * depth, depth), depth)
            shard = shards[which][member]
            if member == 0 and which < 2:
                shard = unit_part(shard, me, experts, split)
            weight_copies.append(
                pltpu.make_async_copy(
                    shard,
                    weights.at[which, :, place],
                    weight_sems.at[which, member],
                )
            )
            weight_copies[-1].start()
    greet(partners)
    spread = []
    if following:
        spread = spread_start(
            members,
            True,
            slot,
            gates,
            source,
            received,
            picked_s,
            chosen_s,
            gate_s,
            spread_sems,
            own_sems,
        )
    grad_copies = []
    if not following:
        for which in range(3):
            for k, other in enumerate(partners):
                place = pl.ds(pl.multiple_of((me ^ (k + 1)) * depth, depth), depth)
                grad_copies.append(
                    send(
                        grads[which].at[place],
                        grad_got[which].at[k],
                        grad_sems.at[0, which, k],
                        grad_sems.at[1, which, k],
                        other,
                    )
                )
    for copy in weight_copies:
        copy.wait()
    copies = []
    for expert in range(experts):

        def hidden_step(at, carry):
            cols = pl.ds(pl.multiple_of(at * chunk, chunk), chunk)
            up_cols = pl.ds(pl.multiple_of(hidden_width + at * chunk, chunk), chunk)
            gate_pre = dot_plain(token_s[expert], weights[0, expert, :, cols])
            up_pre = dot_plain(token_s[expert], weights[1, expert, :, cols])
            d_hidden = dot_plain(cot_s[expert], weights[2, expert, :, cols])
            logistic = jax.nn.sigmoid(gate_pre)
            active = gate_pre * logistic
            hidden_s[expert, :, cols] = (active * up_pre).astype(BF16)
            slope = logistic * (1.0 + gate_pre * (1.0 - logistic))
            d_pre_s[expert, :, cols] = (d_hidden * up_pre * slope).astype(BF16)
            d_pre_s[expert, :, up_cols] = (d_hidden * active).astype(BF16)
            return carry

        lax.fori_loop(0, hidden_width // chunk, hidden_step, 0)

        def back_step(at, carry):
            cols = block_cols(at)
            back = dot_last(d_pre_s[expert, :, :hidden_width], weights[0, expert, cols, :])
            back = back + dot_last(d_pre_s[expert, :, hidden_width:], weights[1, expert, cols, :])
            back = back.astype(BF16)
            back_s[expert * CAP : (expert + 1) * CAP, cols] = back[:CAP]
            for k in range(members - 1):
                outgoing[k * rows + expert * CAP : k * rows + (expert + 1) * CAP, cols] = back[
                    (k + 1) * CAP : (k + 2) * CAP
                ]
            for copy in returns(cols):
                copy.start()
            return carry

        def returns(cols, expert=expert):
            return [
                make_send(
                    outgoing.at[pl.ds(k * rows + expert * CAP, CAP), cols],
                    back_s.at[pl.ds((k + 1) * rows + expert * CAP, CAP), cols],
                    row_sems.at[0, k, expert],
                    row_sems.at[1, k, expert],
                    other,
                )
                for k, other in enumerate(partners)
            ]

        lax.fori_loop(0, width // BLOCK, back_step, 0)
        copies += returns(pl.ds(0, width))

    for expert in range(experts):

        def ahead_step(at, carry):
            cols = block_cols(at)
            ahead = dot_last(hidden_s[expert], weights[2, expert, cols, :]).astype(BF16)
            for member in range(members):
                out_rows[member][expert * CAP : (expert + 1) * CAP, cols] = ahead[
                    member * CAP : (member + 1) * CAP
                ]
            return carry

        lax.fori_loop(0, width // BLOCK, ahead_step, 0)

    place_rows(slot_t, None, places_s)
    for copy in copies:
        copy.wait()

    def columns(at, carry):
        cols = block_cols(at)
        total = dot_plain(places_s[...], back_s[:, cols])
        total = total + dot_plain(d_gate_sh[...], gate_sh[:, cols])
        total = total + dot_plain(d_up_sh[...], up_sh[:, cols])
        part[:, cols] = total.astype(BF16)
        return carry

    lax.fori_loop(0, width // BLOCK, columns, 0)
    for copy in spread + grad_copies:
        copy.wait()
    if not following:
        own = pl.ds(pl.multiple_of(me * depth, depth), depth)
        for which in range(3):
            value = grads[which][own, :].astype(F32)
            for k in range(members - 1):
                value = value + grad_got[which][k].astype(F32)
            grad_outs[which][...] = value


def expert_rows(
    following, grads, slot_t, tokens, cots, d_gate_sh, d_up_sh, shared_w, gate_parts, up_parts, down_parts
):
    members = len(gate_parts)
    length, units = slot_t.shape
    experts, stacked, width = tokens.shape
    rows = experts * CAP
    hidden_width = gate_parts[1].shape[2]
    split = gate_parts[0].shape[2] // hidden_width
    shape = jax.ShapeDtypeStruct
    extra = 3
    firsts = 7 + extra + 3 * members
    outs_n = 3 + members + (1 if following else 3)
    depth = width // members

    def kernel(*refs):
        ins, outs, scratch = refs[:firsts], refs[firsts : firsts + outs_n], refs[firsts + outs_n :]
        more = outs[3 + members :]
        outs, tail, scratch = outs[: 3 + members], (*more, *scratch[6:]), scratch[:6]
        expert_kernel(
            members, split, bool(following), *ins, outs[0], outs[1 : 1 + members], *outs[1 + members :],
            *scratch, *tail,
        )

    out_shape = [shape((length, width), BF16)] + [shape((rows, width), BF16)] * members
    out_shape += [
        shape((experts, stacked, hidden_width), BF16),
        shape((experts, stacked, 2 * hidden_width), BF16),
    ]
    out_specs = [VMEM] * (3 + members)
    scratch = [
        pltpu.VMEM(((members - 1) * rows, width), BF16),
        pltpu.VMEM((members * rows, width), BF16),
        pltpu.VMEM((3, experts, width, hidden_width), BF16),
        pltpu.VMEM((length, units * CAP), BF16),
        pltpu.SemaphoreType.DMA((2, members - 1, experts)),
        pltpu.SemaphoreType.DMA((3, members)),
    ]
    if following:
        out_shape.append(shape((experts, stacked, width), BF16))
        out_specs.append(ANY)
        scratch += spread_scratch(members, units, length, width)
    else:
        for grad in grads:
            out_shape.append(shape((depth, grad.shape[1]), F32))
            out_specs.append(VMEM)
            scratch.append(pltpu.VMEM((members - 1, depth, grad.shape[1]), BF16))
        scratch.append(pltpu.SemaphoreType.DMA((2, 3, members - 1)))
    out = pl.pallas_call(
        kernel,
        out_shape=tuple(out_shape),
        in_specs=[VMEM] * (7 + extra) + [ANY] * (3 * members),
        out_specs=tuple(out_specs),
        scratch_shapes=scratch,
        compiler_params=pltpu.CompilerParams(
            vmem_limit_bytes=VMEM_LIMIT,
            collective_id=6 if following else 10,
            has_side_effects=True,
        ),
        cost_estimate=KERNEL_COST,
    )(
        slot_t,
        tokens,
        cots,
        d_gate_sh,
        d_up_sh,
        *shared_w[:2],
        *(following or grads),
        *gate_parts,
        *up_parts,
        *down_parts,
    )
    return out[0], out[1 : 1 + members], out[1 + members : 3 + members], out[3 + members :]


def tail_kernel(rows_n, cols_n, micro_n, first_gain, *refs):
    refs = list(refs)
    sets = [refs[at * 12 : (at + 1) * 12] for at in range(micro_n)]
    refs = refs[micro_n * 12 :]
    pieces, refs = refs[:rows_n], refs[rows_n:]
    outs, small_outs, refs = refs[:2], refs[2:6], refs[6:]
    totals, got, refs = refs[:5], refs[5:7], refs[7:]
    rows_t, refs = refs[:micro_n], refs[micro_n:]
    io_s, io_got, small_s, small_got, few_got, row_sems, col_sems = (
        refs[0], refs[1], refs[2:6], refs[6:10], refs[10:12], refs[12], refs[13]
    )
    me, at = lax.axis_index("row"), lax.axis_index("col")
    width = sets[0][0].shape[1]
    depth = width // rows_n
    io_rows = io_got.shape[1]
    row_peers = row_partners(rows_n)
    col_peers = [{"col": at ^ k} for k in range(1, cols_n)]
    greet(row_peers + col_peers)
    row_copies, small_copies = [], []

    def to_row(which, k, source, target, other):
        return send(source, target, row_sems.at[0, which, k], row_sems.at[1, which, k], other)

    def to_col(which, k, source, target, other):
        return send(source, target, col_sems.at[0, which, k], col_sems.at[1, which, k], other)

    def total_of(place):
        return functools.reduce(jnp.add, [one[place][...] for one in sets])

    gain = jnp.sum(total_of(7), axis=0, keepdims=True) / first_gain[...]
    small_s[0][...] = jnp.concatenate([gain, total_of(8)], axis=0)
    for which, place in ((1, 10), (2, 9), (3, 11)):
        small_s[which][...] = total_of(place)
    for which in range(4):
        for k, other in enumerate(row_peers):
            small_copies.append(
                to_row(which, k, small_s[which], small_got[which].at[k], other)
            )

    def total_at(which, cols, rights, left):
        totals[which][cols, :] = functools.reduce(
            jnp.add, [dot_last(right, one[left][...]) for right, one in zip(rights, sets)]
        ).astype(BF16)

    def early_step(block, carry):
        cols = block_cols(block)
        rights = [jnp.transpose(one[0][:, cols]) for one in sets]
        for kept, right in zip(rows_t, rights):
            kept[cols, :] = right
        total_at(3, cols, rights, 5)
        total_at(4, cols, rights, 6)
        return carry

    lax.fori_loop(0, width // BLOCK, early_step, 0)
    for k, other in enumerate(row_peers):
        place = pl.ds(pl.multiple_of((me ^ (k + 1)) * depth, depth), depth)
        for which in range(2):
            row_copies.append(
                to_row(4 + which, k, totals[3 + which].at[place], got[which].at[k], other)
            )

    def late_step(block, carry):
        cols = block_cols(block)
        rights = [kept[cols, :] for kept in rows_t]
        total_at(0, cols, rights, 2)
        total_at(1, cols, rights, 3)
        total_at(2, cols, [jnp.transpose(one[1][:, cols]) for one in sets], 4)
        return carry

    lax.fori_loop(0, width // BLOCK, late_step, 0)
    for k in range(rows_n):
        place = pl.ds(pl.multiple_of((me ^ k) * depth, depth), depth)
        for which in range(3):
            pieces[k][which] = totals[which][place, :]
    for copy in small_copies:
        copy.wait()
    for which in range(4):
        value = small_s[which][...]
        for k in range(rows_n - 1):
            value = value + small_got[which][k]
        small_s[which][...] = value
    few_copies = [
        to_col(1 + which, k, small_s[which], few_got[which].at[k], other)
        for which in range(2)
        for k, other in enumerate(col_peers)
    ]
    own = pl.ds(pl.multiple_of(me * depth, depth), depth)
    for copy in row_copies:
        copy.wait()
    sums = []
    for which in range(2):
        value = totals[3 + which][own, :].astype(F32)
        for k in range(rows_n - 1):
            value = value + got[which][k].astype(F32)
        sums.append(value)
    outs[0][...] = sums[0]
    io_s[...] = jnp.transpose(sums[1]).astype(BF16)
    io_copies = []
    for k, other in enumerate(col_peers):
        place = pl.ds(pl.multiple_of((at ^ (k + 1)) * io_rows, io_rows), io_rows)
        io_copies.append(to_col(0, k, io_s.at[place], io_got.at[k], other))
    for copy in few_copies:
        copy.wait()
    for which in range(4):
        value = small_s[which][...]
        if which < 2:
            for k in range(cols_n - 1):
                value = value + few_got[which][k]
        small_outs[which][...] = value
    for copy in io_copies:
        copy.wait()
    value = io_s[pl.ds(pl.multiple_of(at * io_rows, io_rows), io_rows), :].astype(F32)
    for k in range(cols_n - 1):
        value = value + io_got[k].astype(F32)
    outs[1][...] = jnp.transpose(value)


def tail_sums(rows_n, cols_n, first_gain, sets):
    width = sets[0][0].shape[1]
    depth = width // rows_n
    io_full = sets[0][6].shape[0]
    io_rows = io_full // cols_n
    shares = [left.shape[0] for left in sets[0][2:6]]
    shape = jax.ShapeDtypeStruct
    vmem = lambda *dims: pltpu.VMEM(dims, BF16)
    small = [(2, width), sets[0][10].shape, sets[0][9].shape, sets[0][11].shape]
    small_f32 = lambda lead, dims: pltpu.VMEM(lead + dims, F32)
    return pl.pallas_call(
        functools.partial(tail_kernel, rows_n, cols_n, len(sets)),
        out_shape=(shape((3, depth, shares[0]), BF16),) * rows_n
        + (shape((depth, shares[3]), F32), shape((depth, io_rows), F32))
        + tuple(shape(dims, F32) for dims in small),
        in_specs=[VMEM] * (1 + 12 * len(sets)),
        out_specs=(VMEM,) * (rows_n + 6),
        scratch_shapes=[vmem(width, share) for share in shares + [io_full]]
        + [vmem(rows_n - 1, depth, share) for share in (shares[3], io_full)]
        + [vmem(width, sets[0][0].shape[0])] * len(sets)
        + [vmem(io_full, depth), vmem(cols_n - 1, io_rows, depth)]
        + [small_f32((), dims) for dims in small]
        + [small_f32((rows_n - 1,), dims) for dims in small]
        + [small_f32((cols_n - 1,), dims) for dims in small[:2]]
        + [
            pltpu.SemaphoreType.DMA((2, 6, rows_n - 1)),
            pltpu.SemaphoreType.DMA((2, 3, cols_n - 1)),
        ],
        compiler_params=pltpu.CompilerParams(
            vmem_limit_bytes=VMEM_LIMIT, collective_id=7, has_side_effects=True
        ),
        cost_estimate=KERNEL_COST,
    )(first_gain, *[ref for one in sets for ref in one])


def gather_kernel(
    rows_n,
    cols_n,
    pack,
    io,
    taps,
    first,
    pack_all,
    io_all,
    taps_all,
    first_all,
    row_sems,
    io_sems,
    tap_sems,
    own_sems,
    first_sems,
):
    me, at = lax.axis_index("row"), lax.axis_index("col")
    io_rows = io.shape[0]
    place = pl.ds(pl.multiple_of(at * io_rows, io_rows), io_rows)
    row_peers = [{"row": me ^ k} for k in range(1, rows_n)]
    col_peers = [{"col": at ^ k} for k in range(1, cols_n)]
    barrier = pltpu.get_barrier_semaphore()
    for other in row_peers + col_peers:
        pl.semaphore_signal(barrier, inc=1, device_id=other, device_id_type=MESH)
    pl.semaphore_wait(barrier, rows_n + cols_n - 2)

    def send_one(source, target, sems, k, other):
        return send(source, target, sems.at[0, k], sems.at[1, k], other)

    own = [
        pltpu.make_async_copy(pack, pack_all.at[me], own_sems.at[0]),
        pltpu.make_async_copy(io, io_all.at[me, place], own_sems.at[1]),
        pltpu.make_async_copy(taps, taps_all.at[place], own_sems.at[2]),
        pltpu.make_async_copy(first, first_all.at[at], own_sems.at[3]),
    ]
    for copy in own:
        copy.start()

    def send_first(which, k, source, owner, other):
        return make_send(
            source,
            first_all.at[owner],
            first_sems.at[0, which, k],
            first_sems.at[1, which, k],
            other,
        )

    far = [
        send_first(0, k, first, at, {"col": at ^ (2 * k)}) for k in range(1, cols_n // 2)
    ]
    near = [send_first(1, 0, first, at, {"col": at ^ 1})]
    for copy in far + near:
        copy.start()
    io_copies = [
        send_one(io, io_all.at[me, place], io_sems, k, other) for k, other in enumerate(col_peers)
    ]
    copies = [
        send_one(taps, taps_all.at[place], tap_sems, k, other)
        for k, other in enumerate(col_peers)
    ]
    copies += [
        send_one(pack, pack_all.at[me], row_sems, k, other) for k, other in enumerate(row_peers)
    ]
    own[1].wait()
    for copy in io_copies:
        copy.wait()
    copies += [
        send_one(io_all.at[me], io_all.at[me], row_sems, rows_n - 1 + k, other)
        for k, other in enumerate(row_peers)
    ]
    for k, copy in enumerate(far, 1):
        copy.wait()
        owner = at ^ (2 * k)
        near.append(send_first(1, k, first_all.at[owner], owner, {"col": at ^ 1}))
        near[-1].start()
    own[0].wait()
    own[2].wait()
    own[3].wait()
    for copy in near + copies:
        copy.wait()


def gather_weights(pack, io, taps, first, rows_n, cols_n):
    shape = jax.ShapeDtypeStruct
    return pl.pallas_call(
        functools.partial(gather_kernel, rows_n, cols_n),
        out_shape=(
            shape((rows_n,) + pack.shape, BF16),
            shape((rows_n, cols_n * io.shape[0], io.shape[1]), BF16),
            shape((cols_n * io.shape[0], taps.shape[1]), BF16),
            shape((cols_n,) + first.shape, BF16),
        ),
        in_specs=[ANY] * 4,
        out_specs=(ANY,) * 4,
        scratch_shapes=[
            pltpu.SemaphoreType.DMA((2, 2 * (rows_n - 1))),
            pltpu.SemaphoreType.DMA((2, cols_n - 1)),
            pltpu.SemaphoreType.DMA((2, cols_n - 1)),
            pltpu.SemaphoreType.DMA((4,)),
            pltpu.SemaphoreType.DMA((2, 2, cols_n // 2)),
        ],
        compiler_params=pltpu.CompilerParams(collective_id=1, has_side_effects=True),
        cost_estimate=pl.CostEstimate(flops=1, bytes_accessed=1, transcendentals=0),
    )(pack, io, taps, first)


def row_norm(values, scale_gain):
    return values * lax.rsqrt(jnp.mean(values * values, axis=1, keepdims=True) + EPS) * scale_gain


def norm_adjoint(values, scale_gain, cotangent):
    inverse = lax.rsqrt(jnp.mean(values * values, axis=1, keepdims=True) + EPS)
    unit = values * inverse
    scaled = cotangent * scale_gain
    back = inverse * (scaled - unit * jnp.mean(scaled * unit, axis=1, keepdims=True))
    return back, jnp.sum(cotangent * unit, axis=0, keepdims=True)


def local(
    layer_input,
    out_grad,
    seq_lengths,
    routes,
    route_gates,
    first_gain,
    gate_branch_proj,
    conv_in_proj,
    state_io_proj,
    step_proj,
    conv_kernel,
    conv_offset,
    state_conv_kernel,
    state_conv_offset,
    decay_log,
    step_offset,
    skip_scale,
    mixer_gain,
    out_proj,
    second_gain,
    expert_gate,
    expert_up,
    expert_down,
    shared_gate,
    shared_up,
    shared_down,
):
    rows_n = lax.axis_size("row")
    cols_n = lax.axis_size("col")
    row_index = lax.axis_index("row")
    col_index = lax.axis_index("col")
    micro_count, own_count, width = layer_input.shape
    length = own_count * cols_n
    local_experts, depth, hidden_width = expert_gate.shape
    share = conv_kernel.shape[1]
    heads = decay_log.shape[0]
    size = share // heads
    inner = share * cols_n
    io_width = state_conv_kernel.shape[1]
    shared_width = shared_gate.shape[1]
    per_device = max(1, local_experts // rows_n)
    split = max(1, rows_n // local_experts)
    part_width = hidden_width // split

    def swap(values, k):
        if k == 0:
            return values
        return lax.ppermute(values, "row", [(i, i ^ k) for i in range(rows_n)])

    def peer(k):
        return row_index ^ k

    def unit_at(member):
        return (member * per_device) // split, (member % split) * part_width

    def gather_width(pack):
        full = jnp.zeros((pack.shape[0], width), pack.dtype)
        for k in range(rows_n):
            full = lax.dynamic_update_slice(full, swap(pack, k), (0, peer(k) * depth))
        return full

    def after(value, *others):
        return lax.optimization_barrier((value, *others))[0]

    micro = range(micro_count)
    own_rows = [layer_input[m].astype(F32) for m in micro]
    first_rows = [row_norm(own_rows[m], first_gain).astype(BF16) for m in micro]

    own_taps = jnp.concatenate([state_conv_kernel, state_conv_offset[None, :]], axis=0).T
    tap_parts = []
    for _ in range(3):
        tap_parts.append(own_taps.astype(BF16))
        own_taps = own_taps - tap_parts[-1].astype(F32)
    tap_parts = jnp.pad(jnp.concatenate(tap_parts, axis=1), ((0, 0), (0, LANES - 15)))
    step_rows_t = jnp.pad(step_proj.T, ((0, HEAD_ROWS - heads), (0, 0)))
    in_all, io_all, taps_all, first_all = gather_weights(
        jnp.concatenate([gate_branch_proj.T, conv_in_proj.T, out_proj, step_rows_t], axis=0),
        state_io_proj.T,
        tap_parts,
        first_rows[0],
        rows_n,
        cols_n,
    )

    normed = [first_all.reshape(length, width)] + [
        lax.all_gather(after(rows, in_all), "col", axis=0, tiled=True) for rows in first_rows[1:]
    ]

    def join(parts, first, count):
        return jnp.concatenate(
            [parts[member, first : first + count] for member in range(rows_n)], axis=1
        )

    wb, wc, wo = [join(in_all, at * share, share) for at in range(3)]
    ws = join(in_all, 3 * share, HEAD_ROWS)
    wio = join(io_all, 0, 2 * NS)
    taps_all = taps_all.astype(F32)
    io_taps = jnp.pad(taps_all[:, :5] + taps_all[:, 5:10] + taps_all[:, 10:15], ((0, 0), (0, 3)))
    chan = jnp.concatenate(
        [
            conv_kernel.T,
            conv_offset[:, None],
            mixer_gain[:, None],
            jnp.repeat(skip_scale, size)[:, None],
            jnp.zeros((share, 1), F32),
        ],
        axis=1,
    )
    head_params = jnp.pad(
        jnp.stack([step_offset, jnp.exp(decay_log)], axis=1), ((0, HEAD_ROWS - heads), (0, 6))
    )
    weights = (wb, wc, wio, ws, wo, chan, io_taps, head_params)

    downs = []
    for k in range(rows_n):
        first, hidden_at = unit_at(peer(k))
        part = lax.dynamic_slice(
            expert_down, (first, hidden_at, 0), (per_device, part_width, depth)
        )
        downs.append(swap(after(jnp.swapaxes(part, 1, 2), in_all), k))

    place_j = lax.broadcasted_iota(jnp.int32, (length, length), 0)
    place_i = lax.broadcasted_iota(jnp.int32, (length, length), 1)
    upper = (place_j <= place_i).astype(BF16)
    expert_ids = col_index * local_experts + jnp.arange(local_experts, dtype=jnp.int32)

    def slots_of(m):
        hit = routes[m].T[None] == expert_ids[:, None, None]
        mask = jnp.any(hit, axis=1)
        gates = jnp.sum(jnp.where(hit, route_gates[m].T[None], 0.0), axis=1)
        rank = dot_plain(mask.astype(BF16), upper).astype(jnp.int32) - 1
        slot = jnp.where(mask, rank, -(2**20))
        firsts = [unit_at(peer(k))[0] for k in range(rows_n)]
        take = lambda rows: jnp.concatenate(
            [lax.dynamic_slice(rows, (first, 0), (per_device, length)) for first in firsts], axis=0
        )
        return take(slot), take(gates)

    def swap_all(parts):
        return [swap(part, k) for k, part in enumerate(parts)]

    own_cots = []
    for m in micro:
        positions = col_index * own_count + jnp.arange(own_count)
        valid = (positions < seq_lengths[m, 0])[:, None]
        own_cots.append(jnp.where(valid, out_grad[m], jnp.zeros_like(out_grad[m])))
    slot_rows = [slots_of(m) for m in micro]
    slot_cols = [(slot.T, gates.T) for slot, gates in slot_rows]

    last = [None]

    def step(function, *args):
        if last[0] is not None:
            args, _ = lax.optimization_barrier((args, last[0]))
        out = function(*args)
        last[0] = jax.tree.leaves(out)[0]
        return out

    state = [{} for _ in micro]

    def mix(m, weight):
        s = state[m]
        (s["y_part"], s["squares"], *s["saved"]), received = step(
            lambda xn: mixer_forward(
                rows_n, cols_n, (per_device, split), weight, xn, *weights, heads
            ),
            normed[m],
        )
        return [weight, *received]

    def sum_y(m, *others):
        s = state[m]
        s["y"] = lax.psum_scatter(
            after(s["y_part"], *others), "col", scatter_dimension=0, tiled=True
        )

    def scale_of(m):
        s = state[m]
        s["rms"] = lax.rsqrt(s["squares"][0] / inner + EPS)

    def second_norm(m):
        s = state[m]

        def run(y_own, rms):
            y_own = y_own.astype(F32)
            own_rms = lax.dynamic_slice(rms, (col_index * own_count,), (own_count,))
            residual = own_rows[m] + own_rms[:, None] * y_own
            return row_norm(residual, second_gain).astype(BF16), residual, y_own

        second, s["residual"], s["y_own"] = step(run, s["y"], s["rms"])
        s["second"] = lax.all_gather(second, "col", axis=0, tiled=True)
        s["second_own"] = second

    def gather_cot(m, *others):
        return lax.all_gather(after(own_cots[m], *others), "col", axis=0, tiled=True)

    def spread_cot(m):
        s = state[m]
        slot, gates_of = slot_rows[m]
        (s["cot_rows"],) = step(
            lambda cot: spread_rows(rows_n, slot, gates_of, cot), s["cot"]
        )

    def spread_tokens(m):
        s = state[m]
        slot, gates_of = slot_rows[m]
        (
            s["token_rows"],
            s["shared_hidden"],
            s["d_shared_gate"],
            s["d_shared_up"],
            *s["shared_grads"],
        ) = step(
            lambda second, cot, before: spread_rows(
                rows_n,
                slot,
                gates_of,
                second,
                cot,
                shared_w,
                before,
                BF16 if m == micro_count - 1 else F32,
            ),
            s["second"],
            s["cot"],
            state[m - 1]["shared_grads"] if m else (),
        )

    def experts(m):
        s = state[m]
        later = state[m + 1] if m + 1 < micro_count else None
        part, out_rows, saved, spread = step(
            lambda cot, grads, *args: expert_rows(
                () if later is None else (*slot_rows[m + 1], cot), grads, slot_cols[m][0], *args
            ),
            s["cot"] if later is None else later["cot"],
            s["shared_grads"],
            s["token_rows"],
            s["cot_rows"],
            s["d_shared_gate"],
            s["d_shared_up"],
            shared_w,
            gates,
            ups,
            downs,
        )
        s["expert_saved"] = [s["token_rows"], s["cot_rows"], *saved]
        if later is None:
            s["shared_totals"] = spread
        else:
            (later["cot_rows"],) = spread
        s["second_share"] = lax.psum_scatter(part, "col", scatter_dimension=0, tiled=True)
        s["out_rows"] = list(out_rows) if later is None else swap_all(out_rows)

    def ahead_rows(m, parts=()):
        s = state[m]
        slot_t, gates_t = slot_cols[m]
        part, *stacked = step(
            lambda rows, left, parts: combine_rows(
                slot_t, gates_t, rows, left, shared_out, parts
            ),
            s["out_rows"],
            s["shared_hidden"],
            parts,
        )
        s["branch_share"] = lax.psum_scatter(part, "col", scatter_dimension=0, tiled=True)
        return stacked

    def second_back(m):
        s = state[m]

        def run(share_in):
            back, gain_grad = norm_adjoint(s["residual"], second_gain, share_in.astype(F32))
            residual_grad = own_cots[m].astype(F32) + back
            low = residual_grad.astype(BF16)
            cross = jnp.sum(low.astype(F32) * s["y_own"], axis=1, keepdims=True)
            parts = [low]
            for _ in range(3):
                parts.append(cross.astype(BF16))
                cross = cross - parts[-1].astype(F32)
            parts.append(jnp.zeros((own_count, LANES - 3), BF16))
            return jnp.concatenate(parts, axis=1), residual_grad, gain_grad

        low, s["residual_grad"], s["second_gain_grad"] = step(run, s["second_share"])
        s["low"] = low
        s["d_res"] = lax.all_gather(low, "col", axis=0, tiled=True)

    def mix_back(m, parts, moved=()):
        s = state[m]
        scale_rows = jnp.pad(
            jnp.stack([s["rms"], jnp.full((length,), 1.0 / inner, F32)]), ((0, 6), (0, 0))
        )
        (first_part, *s["back"]), stacked, arrived = step(
            lambda d_res, scales, parts, moved: mixer_backward(
                parts, moved, d_res, scales, normed[m], weights, s["saved"], heads
            ),
            s["d_res"],
            scale_rows,
            parts,
            moved,
        )
        s["first_part"] = first_part
        return stacked, arrived

    def total_of(parts):
        return jax.tree.map(lambda *terms: functools.reduce(jnp.add, terms), *parts)

    def expert_grads(*saved):
        def over_rows(left, right):
            return jnp.einsum("ecd,ech->edh", left, right, preferred_element_type=F32)

        totals = total_of(
            [
                (over_rows(tokens, d_pre), over_rows(cot, hidden))
                for tokens, cot, hidden, d_pre in saved
            ]
        )
        both, down = totals[0].astype(BF16), totals[1].astype(BF16)
        return [
            [
                lax.dynamic_slice(full, (0, peer(k) * depth, at), (per_device, depth, part_width))
                for k in range(rows_n)
            ]
            for full, at in ((both, 0), (both, part_width), (down, 0))
        ]

    def sum_first(m, *others):
        s = state[m]
        s["first_share"] = lax.psum_scatter(
            after(s["first_part"], *others), "col", scatter_dimension=0, tiled=True
        )

    def finish_output(m):
        s = state[m]
        s["output"] = step(
            lambda share_in: (s["residual"] + share_in.astype(F32)).astype(BF16), s["branch_share"]
        )

    def finish_input(m):
        s = state[m]

        def run(share_in):
            back, _ = norm_adjoint(own_rows[m], first_gain, share_in.astype(F32))
            return s["residual_grad"] + back

        s["input_grad"] = step(run, s["first_share"])

    def whole_experts(stacked):
        stacked = stacked.reshape(local_experts, split, depth, part_width)
        return jnp.swapaxes(stacked, 1, 2).reshape(local_experts, depth, hidden_width)

    def arrive(parts):
        return step(lambda *values: values, *parts)

    first, second = 0, micro_count - 1
    state[first]["cot"] = gather_cot(first, in_all)
    gates = mix(first, expert_gate)
    (normed[second],) = arrive([normed[second]])
    sum_y(first)
    scale_of(first)
    state[second]["cot"] = gather_cot(second, state[first]["squares"])
    ups = mix(second, expert_up)
    downs = arrive(downs)
    (state[first]["cot"],) = arrive([state[first]["cot"]])
    scale_of(second)
    second_norm(first)
    sum_y(second, state[first]["second_own"])
    spread_cot(first)
    shared_full = step(
        lambda *parts: gather_width(jnp.concatenate(parts, axis=0)),
        shared_gate.T,
        shared_up.T,
        shared_down,
    )
    shared_w = (
        shared_full[:shared_width],
        shared_full[shared_width : 2 * shared_width],
        shared_full[2 * shared_width :],
    )
    shared_out = shared_w[2]
    spread_tokens(first)
    second_norm(second)
    experts(first)
    spread_tokens(second)
    second_back(first)
    experts(second)
    (state[first]["d_res"],) = arrive([state[first]["d_res"]])
    shared_totals = state[second]["shared_totals"]
    gate_grads, up_grads, down_grads = step(expert_grads, *[s["expert_saved"] for s in state])
    state[first]["out_rows"] = arrive(state[first]["out_rows"])
    second_back(second)
    ahead_rows(first)
    rows = state[second]["out_rows"]
    gate_grads, arrived = mix_back(first, gate_grads, rows[1:])
    state[second]["out_rows"] = [rows[0], *arrived]
    (state[second]["d_res"],) = arrive([state[second]["d_res"]])
    sum_first(first, state[second]["low"])
    (down_grads,) = ahead_rows(second, down_grads)
    finish_output(first)
    up_grads, _ = mix_back(second, up_grads)
    sum_first(second)
    finish_input(first)
    finish_output(second)
    sets = []
    for m in micro:
        s = state[m]
        gain_part, mixed, d_branch, d_conv, d_io, d_step, chan_grad, io_grad, head_grad = s["back"]
        sets.append(
            [
                normed[m],
                s["d_res"],
                d_branch,
                d_conv,
                mixed,
                d_step,
                d_io,
                gain_part,
                s["second_gain_grad"],
                chan_grad,
                io_grad,
                head_grad,
            ]
        )
    *pieces, step_grad, io_proj_grad, gains, io_sums, chans, by_head = step(
        lambda sets: tail_sums(rows_n, cols_n, first_gain[None, :], sets), sets
    )
    pieces = swap_all(pieces)
    gate_grads, up_grads, down_grads = arrive([gate_grads, up_grads, down_grads])
    branch_grad, conv_grad, out_grad_sum = [
        functools.reduce(jnp.add, [piece[which].astype(F32) for piece in pieces])
        for which in range(3)
    ]
    finish_input(second)
    io_values = lax.dynamic_slice(io_sums, (0, col_index * io_width), (5, io_width))
    return (
        jnp.stack([s["output"] for s in state]),
        jnp.stack([s["input_grad"] for s in state]),
        gains[0],
        branch_grad,
        conv_grad,
        io_proj_grad,
        step_grad[:, :heads],
        chans[:4],
        chans[4],
        io_values[:4],
        io_values[4],
        by_head[:heads, 0],
        by_head[:heads, 1],
        by_head[:heads, 2],
        chans[5],
        out_grad_sum.T,
        gains[1],
        whole_experts(gate_grads).astype(F32),
        whole_experts(up_grads).astype(F32),
        jnp.swapaxes(whole_experts(down_grads).astype(F32), 1, 2),
        shared_totals[0],
        shared_totals[1],
        shared_totals[2].T,
    )


def solution(mesh):
    both = P(None, ("row", "col"), None)
    placed = (
        both,
        both,
        P(None, "row"),
        P(None, "row", None),
        P(None, "row", None),
        P(),
        P("row", "col"),
        P("row", "col"),
        P("row", "col"),
        P("row", "col"),
        P(None, "col"),
        P("col"),
        P(None, "col"),
        P("col"),
        P("col"),
        P("col"),
        P("col"),
        P("col"),
        P("col", "row"),
        P(),
        P("col", "row", None),
        P("col", "row", None),
        P("col", None, "row"),
        P("row", "col"),
        P("row", "col"),
        P("col", "row"),
    )
    return jax.shard_map(
        local,
        mesh=mesh,
        in_specs=placed,
        out_specs=(both, both, P()) + placed[6:19] + (P(),) + placed[20:],
        check_vma=False,
    )
```
